32 devices in a mesh: prow: 4 (over z), pcol: 8 (over y, x, core).
Axes of the slice: x: 2, y: 2, z: 4, core: 2. Of those that a mesh axis runs over, the one named last changes fastest.
Arguments:
- factors: bfloat16 [4, 4096, 512], P(None, ('prow', 'pcol')), may hold values from -0.25 to 0.25
- x_factor: bfloat16 [512, 512], replicated, may hold values from -0.25 to 0.25
- zinv_factor: bfloat16 [512, 512], replicated, may hold values from -0.25 to 0.25
- placement: int32 [4096], replicated, may hold values from 0 to 4095, as said below
Outputs:
- trailing: float32 [4096, 4096], P('prow', 'pcol')
- panels: float32 [4096, 1024], P('prow', 'pcol')
The draws below stay inside these ranges and needn't reach their ends.
Inputs may be any that keep to these rules, and one draw needn't show every extreme that they name: placement is a permutation of the Schur rows; device d (grid rows slowest) assembles the rows placement[d * 128] to placement[d * 128 + 127]; among one device's rows at most 64 share the same owner grid row (natural row i belongs to grid row (i div 64) mod 4), and some device has exactly 64 such rows.
All inputs are finite; a program needn't handle non-finite values.
Results may differ from the reference program's by a relative error of at most 0.003.
Values may be sent and summed in bfloat16 or wider, within the bound.
No kernel may reach another device: no remote copies, remote signals or barrier semaphores. Data moves between devices by JAX's collectives and lax.ppermute only.
A program may use at most 128 MiB of HBM per device.

```python
import jax
import jax.numpy as jnp
from jax import lax

NORD = 512
M = 4096
RANK = 4
NB = 64
K = 1024
ROWS_DEV = 128
N_PROW = 4
N_PCOL = 8


def draw_placement(key, part):
    devices_all = M // ROWS_DEV
    base = ROWS_DEV // N_PROW
    key_shift, key_rows, key_slots = jax.random.split(jax.random.fold_in(key, 7), 3)
    shifts = jax.random.randint(key_shift, (devices_all // 2, N_PROW // 2), -base, base + 1)
    shifts = shifts.at[0, 0].set(base)
    paired = jnp.stack([shifts, -shifts], axis=2).reshape(devices_all // 2, N_PROW)
    counts = base + jnp.stack([paired, -paired], axis=1).reshape(devices_all, N_PROW)
    offsets = jnp.cumsum(counts, axis=0) - counts
    ends = jnp.cumsum(counts, axis=1)
    begins = ends - counts
    slots = jnp.arange(ROWS_DEV)
    owner = jnp.sum((ends[:, None, :] <= slots[None, :, None]).astype(jnp.int32), axis=2)
    within = slots[None, :] - jnp.take_along_axis(begins, owner, axis=1)
    picked = jnp.take_along_axis(offsets, owner, axis=1) + within
    share = M // N_PROW
    orders = jax.vmap(lambda k: jax.random.permutation(k, share))(jax.random.split(key_rows, N_PROW))
    listed = orders[owner, picked]
    natural = listed // NB * NB * N_PROW + owner * NB + listed % NB
    shuffled = jax.vmap(lambda k, row: jax.random.permutation(k, row))(jax.random.split(key_slots, devices_all), natural)
    return shuffled.reshape(M).astype(jnp.int32)


def block_levels(stream_key, dims, cuts, low, high):
    factor_of, own = 1.0, jax.random.fold_in(stream_key, 6)
    for position, blocks in cuts:
        heights = jnp.exp(jax.random.uniform(jax.random.fold_in(own, position), (blocks,), jnp.float32, low / len(cuts), high / len(cuts)))
        factor_of = factor_of * jnp.repeat(heights, dims[position] // blocks).reshape([-1 if axis == position else 1 for axis in range(len(dims))])
    return factor_of


def gaussian(key, shape, deviation, bound, cuts=(), held_as=jnp.bfloat16):
    values = jax.random.normal(key, shape, jnp.float32) * deviation
    if len(cuts) > 0:
        values = block_levels(key, shape, cuts, -0.22, 0.18) * values
    return jnp.clip(values, min=-bound, max=bound).astype(held_as)


def setup_inputs(seed: int = 0) -> dict:
    key_of = jax.random.split(jax.random.key(seed), 5)
    factors = gaussian(key_of[0], (RANK, M, NORD), (NORD ** -0.5), 0.25, ((1, 32),))
    x_factor = gaussian(key_of[1], (NORD, NORD), NORD ** -0.5, 0.25)
    zinv_factor = gaussian(key_of[2], (NORD, NORD), NORD ** -0.5, 0.25)
    placement = draw_placement(jax.random.fold_in(key_of[4], 71), 0)
    return {"factors": factors, "x_factor": x_factor, "zinv_factor": zinv_factor, "placement": placement}


rank_signs = (1.0, 1.0, -1.0, -1.0)
block_rows = 256

def to_cyclic(matrix, which_axis, groups):
    length = matrix.shape[which_axis]
    moved = jnp.moveaxis(matrix, which_axis, 0)
    tail_shape = moved.shape[1:]
    moved = moved.reshape((length // (NB * groups), groups, NB) + tail_shape)
    moved = jnp.swapaxes(moved, 0, 1).reshape((length,) + tail_shape)
    return jnp.moveaxis(moved, 0, which_axis)

def reference(factors, x_factor, zinv_factor, placement):
    natural = jnp.zeros_like(factors).at[:, placement, :].set(factors)
    stacked = natural.reshape(RANK * M, NORD)
    proj_x = jnp.dot(stacked.astype(jnp.float32), x_factor.astype(jnp.float32), preferred_element_type=jnp.float32).astype(jnp.bfloat16)
    proj_z = jnp.dot(stacked.astype(jnp.float32), zinv_factor.astype(jnp.float32), preferred_element_type=jnp.float32).astype(jnp.bfloat16)
    cube_x = proj_x.reshape(RANK, M, NORD)
    cube_z = proj_z.reshape(RANK, M, NORD)
    weights = jnp.array(rank_signs, jnp.float32)

    def one_block(first):
        left_x = lax.dynamic_slice_in_dim(cube_x, first, block_rows, 1).reshape(RANK * block_rows, NORD)
        left_z = lax.dynamic_slice_in_dim(cube_z, first, block_rows, 1).reshape(RANK * block_rows, NORD)
        inner_x = jnp.dot(left_x.astype(jnp.float32), proj_x.T.astype(jnp.float32), preferred_element_type=jnp.float32)
        inner_z = jnp.dot(left_z.astype(jnp.float32), proj_z.T.astype(jnp.float32), preferred_element_type=jnp.float32)
        product = (inner_x * inner_z).reshape(RANK, block_rows, RANK, M)
        return jnp.einsum('r,riqj,q->ij', weights, product, weights)
    starts = (jnp.arange(M // block_rows) * block_rows).astype(jnp.int32)
    schur = lax.map(one_block, starts).reshape(M, M)
    leading = jnp.linalg.cholesky(schur[:K, :K])
    panel_rows = lax.linalg.triangular_solve(leading, schur[:, :K], left_side=False, lower=True, transpose_a=True)
    rest = schur - jnp.dot(panel_rows, panel_rows.T, precision=lax.Precision.HIGHEST)
    trailing = to_cyclic(to_cyclic(rest, 0, N_PROW), 1, N_PCOL)
    panels = to_cyclic(to_cyclic(panel_rows, 0, N_PROW), 1, N_PCOL)
    return (trailing, panels)
```

```python
import functools

import jax
import jax.numpy as jnp
from jax import lax
from jax.experimental import pallas as pl
from jax.experimental.pallas import tpu as pltpu
from jax.sharding import PartitionSpec as P

RANK = 4
NB = 64
K = 1024
SUB = 8
BLK = 128
MIB = 2**20

rank_signs = (1.0, 1.0, -1.0, -1.0)
NT = ((1,), (1,))
NN = ((1,), (0,))
VMEM = pl.BlockSpec(memory_space=pltpu.VMEM)
SMEM = pl.BlockSpec(memory_space=pltpu.SMEM)


def split(x):
    hi = x.astype(jnp.bfloat16)
    lo = (x - hi.astype(jnp.float32)).astype(jnp.bfloat16)
    return hi, lo


def dot_bf16(a, b, dims):
    return lax.dot_general(a, b, (dims, ((), ())), preferred_element_type=jnp.float32)


def dot3(a, b, dims):
    return dot_bf16(a[0], b[0], dims) + (dot_bf16(a[0], b[1], dims) + dot_bf16(a[1], b[0], dims))


def project_kernel(wanted_ref, placement_ref, factors_ref, x_ref, z_ref, yx_ref, yz_ref, *, chunk):
    slots = factors_ref.shape[0]
    width = x_ref.shape[0]
    rows = wanted_ref.shape[0]
    wanted = wanted_ref[...]
    total = jnp.zeros((rows, RANK * width), jnp.float32)
    for first in range(0, slots, chunk):
        here = placement_ref[:, first:first + chunk]
        pick = jnp.where(wanted == here, 1.0, 0.0).astype(jnp.bfloat16)
        total = total + dot_bf16(pick, factors_ref[first:first + chunk, :], NN)
    picked = total.astype(jnp.bfloat16)
    for r in range(RANK):
        mine = picked[:, r * width:(r + 1) * width]
        yx_ref[r] = dot_bf16(mine, x_ref[...], NN).astype(jnp.bfloat16)
        yz_ref[r] = dot_bf16(mine, z_ref[...], NN).astype(jnp.bfloat16)


def project(wanted, placement, factors, x_factor, z_factor):
    rows = wanted.shape[0]
    slots, wide = factors.shape
    width = x_factor.shape[0]
    tile = min(256, rows)
    whole = lambda *shape: pl.BlockSpec(shape, lambda i: (0,) * len(shape))
    out = pl.BlockSpec((RANK, tile, width), lambda i: (0, i, 0))
    return pl.pallas_call(
        functools.partial(project_kernel, chunk=512),
        grid=(rows // tile,),
        out_shape=(jax.ShapeDtypeStruct((RANK, rows, width), jnp.bfloat16),) * 2,
        in_specs=[pl.BlockSpec((tile, 1), lambda i: (i, 0)), whole(1, slots), whole(slots, wide), whole(width, width), whole(width, width)],
        out_specs=(out, out),
        compiler_params=pltpu.CompilerParams(vmem_limit_bytes=56 * MIB),
        cost_estimate=pl.CostEstimate(flops=2 * rows * wide * (slots + 2 * width), bytes_accessed=2 * slots * wide + 4 * rows * wide, transcendentals=0),
    )(wanted.reshape(rows, 1), placement.reshape(1, slots), factors, x_factor, z_factor)


def gram_kernel(lx_ref, lz_ref, rx_ref, rz_ref, out_ref):
    total = jnp.zeros(out_ref.shape, jnp.float32)
    for q in range(RANK):
        for r in range(RANK):
            gx = dot_bf16(lx_ref[r], rx_ref[q], NT)
            gz = dot_bf16(lz_ref[r], rz_ref[q], NT)
            if rank_signs[q] * rank_signs[r] > 0:
                total = total + gx * gz
            else:
                total = total - gx * gz
    out_ref[...] = total


def gram(lx, lz, rx, rz):
    _, rows, width = lx.shape
    cols = rx.shape[1]
    row_tile, col_tile = min(512, rows), min(256, cols)
    left = pl.BlockSpec((RANK, row_tile, width), lambda i, j: (0, i, 0))
    right = pl.BlockSpec((RANK, col_tile, width), lambda i, j: (0, j, 0))
    return pl.pallas_call(
        gram_kernel,
        grid=(rows // row_tile, cols // col_tile),
        out_shape=jax.ShapeDtypeStruct((rows, cols), jnp.float32),
        in_specs=[left, left, right, right],
        out_specs=pl.BlockSpec((row_tile, col_tile), lambda i, j: (i, j)),
        compiler_params=pltpu.CompilerParams(vmem_limit_bytes=56 * MIB),
        cost_estimate=pl.CostEstimate(flops=4 * RANK * RANK * rows * cols * width, bytes_accessed=4 * RANK * (rows + cols) * width + 4 * rows * cols, transcendentals=0),
    )(lx, lz, rx, rz)


def factor_block(block, u_ref, v_ref):
    count = BLK // SUB
    sub_iota = lax.broadcasted_iota(jnp.int32, (SUB, BLK), 0)
    lane_iota = lax.broadcasted_iota(jnp.int32, (SUB, BLK), 1)
    rows_a = [block[SUB * i:SUB * (i + 1), :] for i in range(count)]
    rows_v = [(lane_iota == sub_iota + SUB * i).astype(jnp.float32) for i in range(count)]

    def spread_lane(x, lane):
        return jnp.broadcast_to(x[:, lane:lane + 1], (SUB, BLK))

    def spread_row(x, row):
        return jnp.broadcast_to(x[row:row + 1, :], (SUB, BLK))

    for m in range(count):
        head_a, head_v = rows_a[m], rows_v[m]
        cols = [spread_lane(head_a, SUB * m + k) for k in range(SUB)]
        below = [[spread_lane(rows_a[i], SUB * m + k) for k in range(SUB)] for i in range(m + 1, count)]
        scale = jnp.zeros((SUB, BLK), jnp.float32)
        for j in range(SUB):
            pivot = spread_row(cols[j], j)
            root = lax.rsqrt(pivot)
            scale = jnp.where(sub_iota == j, root, scale)
            mult = jnp.where(sub_iota > j, cols[j] * root, 0.0)
            row_a = spread_row(head_a, j) * root
            row_v = spread_row(head_v, j) * root
            lead = [spread_row(cols[k], j) * root if k > j else None for k in range(SUB)]
            if j + 1 < SUB:
                head_a = head_a - mult * row_a
                head_v = head_v - mult * row_v
                for k in range(j + 1, SUB):
                    cols[k] = cols[k] - mult * lead[k]
            for n, i in enumerate(range(m + 1, count)):
                mult_i = below[n][j] * root
                rows_a[i] = rows_a[i] - mult_i * row_a
                rows_v[i] = rows_v[i] - mult_i * row_v
                for k in range(j + 1, SUB):
                    below[n][k] = below[n][k] - mult_i * lead[k]
        u = jnp.where(lane_iota >= sub_iota + SUB * m, head_a * scale, 0.0)
        v = jnp.where(lane_iota <= sub_iota + SUB * m, head_v * scale, 0.0)
        u_ref[SUB * m:SUB * (m + 1), :] = u
        v_ref[SUB * m:SUB * (m + 1), :] = v


def natural_tile(pieces, row_block, col_pair):
    prow, pcol = pieces.shape[:2]
    rows = pl.ds(row_block // prow * NB, NB)
    halves = []
    for block in (2 * col_pair, 2 * col_pair + 1):
        halves.append(pieces[row_block % prow, block % pcol, rows, pl.ds(block // pcol * NB, NB)])
    return jnp.concatenate(halves, axis=1)


def factor_kernel(pieces_ref, l_ref, d_ref, w_ref, u_ref, v_ref):
    order = l_ref.shape[0]
    steps = order // BLK
    for i in range(order // NB):
        for j in range(steps):
            w_ref[i * NB:(i + 1) * NB, j * BLK:(j + 1) * BLK] = natural_tile(pieces_ref, i, j)
    l_ref[...] = jnp.zeros_like(l_ref)

    def step(b, carry):
        at = pl.ds(pl.multiple_of(b * BLK, BLK), BLK)
        factor_block(w_ref[at, at], u_ref, v_ref)
        l_ref[at, at] = u_ref[...].T
        d_ref[at, :] = v_ref[...]
        for k in range(steps - 1):
            @pl.when(b == k)
            def _():
                first = (k + 1) * BLK
                inv = split(v_ref[...])
                def panel(t, c):
                    rows = pl.ds(pl.multiple_of(first + t * BLK, BLK), BLK)
                    l_ref[rows, k * BLK:first] = dot3(split(w_ref[rows, k * BLK:first]), inv, NT)
                    return c
                lax.fori_loop(0, steps - 1 - k, panel, 0)
                right = split(l_ref[first:, k * BLK:first])
                def update(t, c):
                    rows = pl.ds(pl.multiple_of(first + t * BLK, BLK), BLK)
                    left = split(l_ref[rows, k * BLK:first])
                    w_ref[rows, first:] = w_ref[rows, first:] - dot3(left, right, NT)
                    return c
                lax.fori_loop(0, steps - 1 - k, update, 0)
        return carry
    lax.fori_loop(0, steps, step, 0)


def factor(pieces):
    return pl.pallas_call(
        factor_kernel,
        out_shape=(jax.ShapeDtypeStruct((K, K), jnp.float32), jax.ShapeDtypeStruct((K, BLK), jnp.float32)),
        in_specs=[VMEM],
        out_specs=(VMEM, VMEM),
        scratch_shapes=[pltpu.VMEM((K, K), jnp.float32), pltpu.VMEM((BLK, BLK), jnp.float32), pltpu.VMEM((BLK, BLK), jnp.float32)],
        compiler_params=pltpu.CompilerParams(vmem_limit_bytes=48 * MIB),
        cost_estimate=pl.CostEstimate(flops=40 * 10**9, bytes_accessed=12 * MIB, transcendentals=0),
    )(pieces)


def solve_kernel(column_ref, l_ref, d_ref, pieces_ref, tops_ref, schur_ref, rest_ref, panel_ref, lh, ll, xh, xl, zh, zl):
    rows = schur_ref.shape[0]
    pcol = pieces_ref.shape[0]
    prow = tops_ref.shape[0]
    column = column_ref[0]
    low = l_ref[...]
    lh[...], ll[...] = split(low)
    for b in range(K // BLK):
        at = slice(b * BLK, (b + 1) * BLK)
        inverse = split(d_ref[at, :])
        halves = []
        for block in (2 * b, 2 * b + 1):
            halves.append(pieces_ref[block % pcol, :, block // pcol * NB:(block // pcol + 1) * NB])
        value = jnp.concatenate(halves, axis=1)
        lower = []
        for block in (2 * b, 2 * b + 1):
            lower.append(tops_ref[block % prow, block // prow * NB:(block // prow + 1) * NB, :])
        top = jnp.concatenate(lower, axis=0)
        if b > 0:
            done = slice(0, b * BLK)
            left = (lh[at, done], ll[at, done])
            value = value - dot3((xh[:, done], xl[:, done]), left, NT)
            top = top - dot3(left, (zh[done, :], zl[done, :]), NN)
        value = dot3(split(value), inverse, NT)
        top = dot3(inverse, split(top), NN)
        xh[:, at], xl[:, at] = split(value)
        zh[at, :], zl[at, :] = split(top)
        for half, block in enumerate((2 * b, 2 * b + 1)):
            @pl.when(column == block % pcol)
            def _():
                panel_ref[:, block // pcol * NB:(block // pcol + 1) * NB] = value[:, half * NB:(half + 1) * NB]
    rest_ref[...] = schur_ref[...] - dot3((xh[...], xl[...]), (zh[...], zl[...]), NN)


def solve(column, low, inverses, pieces, tops, schur):
    rows, cols = schur.shape
    lead = K // pieces.shape[0]
    bf16 = jnp.bfloat16
    return pl.pallas_call(
        solve_kernel,
        out_shape=(jax.ShapeDtypeStruct((rows, cols), jnp.float32), jax.ShapeDtypeStruct((rows, lead), jnp.float32)),
        in_specs=[SMEM] + [VMEM] * 5,
        out_specs=(VMEM, VMEM),
        scratch_shapes=[pltpu.VMEM((K, K), bf16)] * 2 + [pltpu.VMEM((rows, K), bf16)] * 2 + [pltpu.VMEM((K, cols), bf16)] * 2,
        compiler_params=pltpu.CompilerParams(vmem_limit_bytes=56 * MIB),
        cost_estimate=pl.CostEstimate(flops=12 * 10**9, bytes_accessed=24 * MIB, transcendentals=0),
    )(column, low, inverses, pieces, tops, schur)


def per_device(factors, x_factor, zinv_factor, placement):
    prow_count = lax.axis_size("prow")
    pcol_count = lax.axis_size("pcol")
    total_rows = placement.shape[0]
    local_rows = total_rows // prow_count
    local_cols = total_rows // pcol_count
    prow_id = lax.axis_index("prow")
    pcol_id = lax.axis_index("pcol")
    _, own, width = factors.shape
    every = lax.all_gather(factors.transpose(1, 0, 2).reshape(own, RANK * width), ("prow", "pcol"), axis=0, tiled=True)
    slot_k = jnp.arange(local_rows)
    natural_k = slot_k // NB * NB * prow_count + prow_id * NB + slot_k % NB
    slot_j = jnp.arange(local_cols)
    natural_j = slot_j // NB * NB * pcol_count + pcol_id * NB + slot_j % NB
    wanted = jnp.concatenate([natural_k, natural_j]).astype(jnp.int32)
    yx, yz = project(wanted, placement, every, x_factor, zinv_factor)
    schur_local = gram(yx[:, :local_rows], yz[:, :local_rows], yx[:, local_rows:], yz[:, local_rows:])
    lead_rows, lead_cols = K // prow_count, K // pcol_count
    front = schur_local[:, :lead_cols]
    lead = lax.all_gather(front[:lead_rows], ("prow", "pcol"), axis=0, tiled=False)
    lead = lead.reshape(prow_count, pcol_count, lead_rows, lead_cols)
    pieces = lax.all_gather(front, "pcol", axis=0, tiled=False)
    tops = lax.all_gather(schur_local[:lead_rows], "prow", axis=0, tiled=False)
    low, inverses = factor(lead)
    return solve(pcol_id.astype(jnp.int32).reshape(1), low, inverses, pieces, tops, schur_local)


def solution(mesh):
    in_specs = (P(None, ("prow", "pcol"), None), P(), P(), P())
    out_specs = (P("prow", "pcol"), P("prow", "pcol"))
    return jax.shard_map(
        per_device, mesh=mesh, in_specs=in_specs, out_specs=out_specs, check_vma=False
    )
```

```python
import functools

import jax
import jax.numpy as jnp
from jax import lax
from jax.experimental import pallas as pl
from jax.experimental.pallas import tpu as pltpu
from jax.sharding import PartitionSpec as P

RANK = 4
NB = 64
K = 1024
SUB = 8
BLK = 128
MIB = 2**20

rank_signs = (1.0, 1.0, -1.0, -1.0)
NT = ((1,), (1,))
NN = ((1,), (0,))
VMEM = pl.BlockSpec(memory_space=pltpu.VMEM)
SMEM = pl.BlockSpec(memory_space=pltpu.SMEM)


def split(x):
    hi = x.astype(jnp.bfloat16)
    lo = (x - hi.astype(jnp.float32)).astype(jnp.bfloat16)
    return hi, lo


def dot_bf16(a, b, dims):
    return lax.dot_general(a, b, (dims, ((), ())), preferred_element_type=jnp.float32)


def dot3(a, b, dims):
    return dot_bf16(a[0], b[0], dims) + (dot_bf16(a[0], b[1], dims) + dot_bf16(a[1], b[0], dims))


def assemble_kernel(slots_ref, own_ref, other_ref, x_ref, z_ref, lead_x_ref, lead_z_ref, schur_ref, front_ref, top_ref,
                    every_ref, picked_ref, yx_ref, yz_ref, sem_ref, *, lead_tiles, pick_tiles, row_tiles, col_tiles, rows):
    step = pl.program_id(0)
    half = own_ref.shape[0]
    tile, parts, lanes = picked_ref.shape
    width = x_ref.shape[0]
    per_rank = width // lanes

    @pl.when(step == 0)
    def _():
        first = pltpu.make_async_copy(own_ref, every_ref.at[pl.ds(0, half)], sem_ref.at[0])
        second = pltpu.make_async_copy(other_ref, every_ref.at[pl.ds(half, half)], sem_ref.at[1])
        first.start()
        second.start()
        first.wait()
        second.wait()

    @pl.when(step < pick_tiles)
    def _():
        def pick(group, carry):
            for k in range(16):
                i = group * 16 + k
                picked_ref[i] = every_ref[slots_ref[step * tile + i]]
            return carry
        lax.fori_loop(0, tile // 16, pick, 0)
        by_part = jnp.swapaxes(picked_ref[...], 0, 1)
        images = []
        for r in range(RANK):
            mine = jnp.concatenate([by_part[r * per_rank + k] for k in range(per_rank)], axis=1)
            images.append((dot_bf16(mine, x_ref[...], NN).astype(jnp.bfloat16), dot_bf16(mine, z_ref[...], NN).astype(jnp.bfloat16)))

        @pl.when(step < lead_tiles)
        def _():
            for r in range(RANK):
                lead_x_ref[r], lead_z_ref[r] = images[r]

        @pl.when(step >= lead_tiles)
        def _():
            at = pl.ds(pl.multiple_of((step - lead_tiles) * tile, tile), tile)
            for r in range(RANK):
                yx_ref[r, at, :], yz_ref[r, at, :] = images[r]

    @pl.when(step >= pick_tiles)
    def _():
        high, wide = schur_ref.shape
        i, j = (step - pick_tiles) // col_tiles, (step - pick_tiles) % col_tiles
        left = pl.ds(pl.multiple_of(i * high, high), high)
        right = pl.ds(pl.multiple_of(rows + j * wide, wide), wide)
        value = gram_tile(yx_ref, yz_ref, left, right)
        schur_ref[...] = value

        @pl.when(j == 0)
        def _():
            front_ref[...] = value[:, :front_ref.shape[1]]

        @pl.when(i == 0)
        def _():
            top_ref[...] = value[:top_ref.shape[0], :]


def gram_tile(yx_ref, yz_ref, left, right):
    total = None
    for q in range(RANK):
        for r in range(RANK):
            gx = dot_bf16(yx_ref[r, left, :], yx_ref[q, right, :], NT)
            gz = dot_bf16(yz_ref[r, left, :], yz_ref[q, right, :], NT)
            if total is None:
                total = gx * gz
            elif rank_signs[q] * rank_signs[r] > 0:
                total = total + gx * gz
            else:
                total = total - gx * gz
    return total


def assemble(slots, own, other, x_factor, z_factor, rows, cols, lead_rows, lead_cols):
    half, parts, lanes = own.shape
    width = x_factor.shape[0]
    tile = 256
    high, wide = min(512, rows), min(256, cols)
    lead_tiles, pick_tiles = K // tile, slots.shape[0] // tile
    row_tiles, col_tiles = rows // high, cols // wide
    whole = pl.BlockSpec((width, width), lambda s: (0, 0), pipeline_mode=pl.Buffered(1))
    lead = pl.BlockSpec((RANK, tile, width), lambda s: (0, jnp.minimum(s, lead_tiles - 1), 0))
    after = lambda s: jnp.maximum(s - pick_tiles, 0)
    bf16 = jnp.bfloat16
    any_space = pl.BlockSpec(memory_space=pl.ANY)
    body = functools.partial(assemble_kernel, lead_tiles=lead_tiles, pick_tiles=pick_tiles, row_tiles=row_tiles, col_tiles=col_tiles, rows=rows)
    return pl.pallas_call(
        body,
        grid=(pick_tiles + row_tiles * col_tiles,),
        out_shape=(jax.ShapeDtypeStruct((RANK, K, width), bf16),) * 2 + (
            jax.ShapeDtypeStruct((rows, cols), jnp.float32),
            jax.ShapeDtypeStruct((rows, lead_cols), jnp.float32),
            jax.ShapeDtypeStruct((lead_rows, cols), jnp.float32)),
        in_specs=[SMEM, any_space, any_space, whole, whole],
        out_specs=(lead, lead,
                   pl.BlockSpec((high, wide), lambda s: (after(s) // col_tiles, after(s) % col_tiles)),
                   pl.BlockSpec((high, lead_cols), lambda s: (after(s) // col_tiles, 0)),
                   pl.BlockSpec((lead_rows, wide), lambda s: (0, jnp.minimum(after(s), col_tiles - 1)))),
        scratch_shapes=[pltpu.VMEM((2 * half, parts, lanes), bf16), pltpu.VMEM((tile, parts, lanes), bf16)]
        + [pltpu.VMEM((RANK, rows + cols, width), bf16)] * 2 + [pltpu.SemaphoreType.DMA((2,))],
        compiler_params=pltpu.CompilerParams(vmem_limit_bytes=58 * MIB),
        cost_estimate=pl.CostEstimate(flops=28 * 10**9, bytes_accessed=30 * MIB, transcendentals=0),
    )(slots, own, other, x_factor, z_factor)


def factor_block(block, u_ref, v_ref):
    count = BLK // SUB
    sub_iota = lax.broadcasted_iota(jnp.int32, (SUB, BLK), 0)
    lane_iota = lax.broadcasted_iota(jnp.int32, (SUB, BLK), 1)
    rows_a = [block[SUB * i:SUB * (i + 1), :] for i in range(count)]
    rows_v = [(lane_iota == sub_iota + SUB * i).astype(jnp.float32) for i in range(count)]

    def spread_lane(x, lane):
        return jnp.broadcast_to(x[:, lane:lane + 1], (SUB, BLK))

    def spread_row(x, row):
        return jnp.broadcast_to(x[row:row + 1, :], (SUB, BLK))

    for m in range(count):
        head_a, head_v = rows_a[m], rows_v[m]
        cols = [spread_lane(head_a, SUB * m + k) for k in range(SUB)]
        below = [[spread_lane(rows_a[i], SUB * m + k) for k in range(SUB)] for i in range(m + 1, count)]
        scale = jnp.zeros((SUB, BLK), jnp.float32)
        for j in range(SUB):
            pivot = spread_row(cols[j], j)
            root = lax.rsqrt(pivot)
            scale = jnp.where(sub_iota == j, root, scale)
            mult = jnp.where(sub_iota > j, cols[j] * root, 0.0)
            row_a = spread_row(head_a, j) * root
            row_v = spread_row(head_v, j) * root
            lead = [spread_row(cols[k], j) * root if k > j else None for k in range(SUB)]
            if j + 1 < SUB:
                head_a = head_a - mult * row_a
                head_v = head_v - mult * row_v
                for k in range(j + 1, SUB):
                    cols[k] = cols[k] - mult * lead[k]
            for n, i in enumerate(range(m + 1, count)):
                mult_i = below[n][j] * root
                rows_a[i] = rows_a[i] - mult_i * row_a
                rows_v[i] = rows_v[i] - mult_i * row_v
                for k in range(j + 1, SUB):
                    below[n][k] = below[n][k] - mult_i * lead[k]
        u = jnp.where(lane_iota >= sub_iota + SUB * m, head_a * scale, 0.0)
        v = jnp.where(lane_iota <= sub_iota + SUB * m, head_v * scale, 0.0)
        u_ref[SUB * m:SUB * (m + 1), :] = u
        v_ref[SUB * m:SUB * (m + 1), :] = v


def factor_kernel(yx_ref, yz_ref, l_ref, d_ref, w_ref, u_ref, v_ref):
    order = l_ref.shape[0]
    steps = order // BLK
    tile = 256
    l_ref[...] = jnp.zeros_like(l_ref)
    w_ref[...] = jnp.zeros_like(w_ref)

    def columns(j, carry):
        right = pl.ds(pl.multiple_of(j * tile, tile), tile)

        def rows(i, carry):
            left = pl.ds(pl.multiple_of(i * tile, tile), tile)
            w_ref[left, right] = gram_tile(yx_ref, yz_ref, left, right)
            return carry
        return lax.fori_loop(j, order // tile, rows, carry)
    lax.fori_loop(0, order // tile, columns, 0)

    def step(b, carry):
        at = pl.ds(pl.multiple_of(b * BLK, BLK), BLK)
        factor_block(w_ref[at, at], u_ref, v_ref)
        l_ref[at, at] = u_ref[...].T
        d_ref[at, :] = v_ref[...]
        for k in range(steps - 1):
            @pl.when(b == k)
            def _():
                first = (k + 1) * BLK
                inv = split(v_ref[...])
                def panel(t, c):
                    rows = pl.ds(pl.multiple_of(first + t * BLK, BLK), BLK)
                    l_ref[rows, k * BLK:first] = dot3(split(w_ref[rows, k * BLK:first]), inv, NT)
                    return c
                lax.fori_loop(0, steps - 1 - k, panel, 0)
                right = split(l_ref[first:, k * BLK:first])
                def update(t, c):
                    rows = pl.ds(pl.multiple_of(first + t * BLK, BLK), BLK)
                    left = split(l_ref[rows, k * BLK:first])
                    w_ref[rows, first:] = w_ref[rows, first:] - dot3(left, right, NT)
                    return c
                lax.fori_loop(0, steps - 1 - k, update, 0)
        return carry
    lax.fori_loop(0, steps, step, 0)


def factor(yx, yz):
    return pl.pallas_call(
        factor_kernel,
        out_shape=(jax.ShapeDtypeStruct((K, K), jnp.float32), jax.ShapeDtypeStruct((K, BLK), jnp.float32)),
        in_specs=[VMEM] * 2,
        out_specs=(VMEM, VMEM),
        scratch_shapes=[pltpu.VMEM((K, K), jnp.float32), pltpu.VMEM((BLK, BLK), jnp.float32), pltpu.VMEM((BLK, BLK), jnp.float32)],
        compiler_params=pltpu.CompilerParams(vmem_limit_bytes=48 * MIB),
        cost_estimate=pl.CostEstimate(flops=40 * 10**9, bytes_accessed=12 * MIB, transcendentals=0),
    )(yx, yz)


def solve_kernel(column_ref, l_ref, d_ref, pieces_ref, tops_ref, schur_ref, rest_ref, panel_ref, lh, ll, xh, xl, zh, zl):
    pcol = pieces_ref.shape[0]
    prow = tops_ref.shape[0]
    column = column_ref[0]
    lh[...], ll[...] = split(l_ref[...])
    wide = 2 * BLK
    for b in range(K // wide):
        at = slice(b * wide, (b + 1) * wide)
        upper, lower = slice(b * wide, b * wide + BLK), slice(b * wide + BLK, (b + 1) * wide)
        first, second = split(d_ref[upper, :]), split(d_ref[lower, :])
        between = dot3((lh[lower, upper], ll[lower, upper]), first, NN)
        corner = -dot3(second, split(between), NN)
        inverse = split(jnp.concatenate([
            jnp.concatenate([d_ref[upper, :], jnp.zeros((BLK, BLK), jnp.float32)], axis=1),
            jnp.concatenate([corner, d_ref[lower, :]], axis=1)], axis=0))
        blocks = range(wide // NB * b, wide // NB * (b + 1))
        value = jnp.concatenate([pieces_ref[n % pcol, :, n // pcol * NB:(n // pcol + 1) * NB] for n in blocks], axis=1)
        top = jnp.concatenate([tops_ref[n % prow, n // prow * NB:(n // prow + 1) * NB, :] for n in blocks], axis=0)
        if b > 0:
            done = slice(0, b * wide)
            left = (lh[at, done], ll[at, done])
            value = value - dot3((xh[:, done], xl[:, done]), left, NT)
            top = top - dot3(left, (zh[done, :], zl[done, :]), NN)
        value = dot3(split(value), inverse, NT)
        top = dot3(inverse, split(top), NN)
        xh[:, at], xl[:, at] = split(value)
        zh[at, :], zl[at, :] = split(top)
        for place, block in enumerate(blocks):
            @pl.when(column == block % pcol)
            def _():
                panel_ref[:, block // pcol * NB:(block // pcol + 1) * NB] = value[:, place * NB:(place + 1) * NB]
    rest_ref[...] = schur_ref[...] - dot3((xh[...], xl[...]), (zh[...], zl[...]), NN)


def solve(column, low, inverses, pieces, tops, schur):
    rows, cols = schur.shape
    lead = K // pieces.shape[0]
    bf16 = jnp.bfloat16
    return pl.pallas_call(
        solve_kernel,
        out_shape=(jax.ShapeDtypeStruct((rows, cols), jnp.float32), jax.ShapeDtypeStruct((rows, lead), jnp.float32)),
        in_specs=[SMEM] + [VMEM] * 5,
        out_specs=(VMEM, VMEM),
        scratch_shapes=[pltpu.VMEM((K, K), bf16)] * 2 + [pltpu.VMEM((rows, K), bf16)] * 2 + [pltpu.VMEM((K, cols), bf16)] * 2,
        compiler_params=pltpu.CompilerParams(vmem_limit_bytes=56 * MIB),
        cost_estimate=pl.CostEstimate(flops=12 * 10**9, bytes_accessed=24 * MIB, transcendentals=0),
    )(column, low, inverses, pieces, tops, schur)


def per_device(factors, x_factor, zinv_factor, placement):
    prow_count = lax.axis_size("prow")
    pcol_count = lax.axis_size("pcol")
    total_rows = placement.shape[0]
    local_rows = total_rows // prow_count
    local_cols = total_rows // pcol_count
    prow_id = lax.axis_index("prow")
    pcol_id = lax.axis_index("pcol")
    _, own, width = factors.shape
    count = prow_count * pcol_count
    lanes = BLK
    mine = factors.transpose(1, 0, 2).reshape(own, RANK * width // lanes, lanes)
    alike = [[d for d in range(count) if d % 2 == parity] for parity in range(2)]
    near = lax.all_gather(mine, ("prow", "pcol"), axis=0, tiled=True, axis_index_groups=alike)
    far = lax.ppermute(near, "pcol", [(c, c ^ 1) for c in range(pcol_count)])
    slot_k = jnp.arange(local_rows)
    natural_k = slot_k // NB * NB * prow_count + prow_id * NB + slot_k % NB
    slot_j = jnp.arange(local_cols)
    natural_j = slot_j // NB * NB * pcol_count + pcol_id * NB + slot_j % NB
    inverse = jnp.zeros((total_rows,), jnp.int32).at[placement].set(jnp.arange(total_rows, dtype=jnp.int32))
    wanted = jnp.concatenate([jnp.arange(K), natural_k, natural_j]).astype(jnp.int32)
    slots = inverse[wanted]
    holder = slots // own
    places = holder // 2 * own + slots % own + jnp.where(holder % 2 == pcol_id % 2, 0, total_rows // 2)
    lead_rows, lead_cols = K // prow_count, K // pcol_count
    lead_x, lead_z, schur_local, front, top = assemble(
        places.astype(jnp.int32), near, far, x_factor, zinv_factor, local_rows, local_cols, lead_rows, lead_cols)
    pieces = lax.all_gather(front, "pcol", axis=0, tiled=False)
    tops = lax.all_gather(top, "prow", axis=0, tiled=False)
    low, inverses = factor(lead_x, lead_z)
    return solve(pcol_id.astype(jnp.int32).reshape(1), low, inverses, pieces, tops, schur_local)


def solution(mesh):
    in_specs = (P(None, ("prow", "pcol"), None), P(), P(), P())
    out_specs = (P("prow", "pcol"), P("prow", "pcol"))
    return jax.shard_map(
        per_device, mesh=mesh, in_specs=in_specs, out_specs=out_specs, check_vma=False
    )
```

```python
import functools

import jax
import jax.numpy as jnp
from jax import lax
from jax.experimental import pallas as pl
from jax.experimental.pallas import tpu as pltpu
from jax.sharding import PartitionSpec as P

RANK = 4
NB = 64
K = 1024
SUB = 8
BLK = 128
MIB = 2**20

rank_signs = (1.0, 1.0, -1.0, -1.0)
NT = ((1,), (1,))
NN = ((1,), (0,))
VMEM = pl.BlockSpec(memory_space=pltpu.VMEM)
SMEM = pl.BlockSpec(memory_space=pltpu.SMEM)


def split(x):
    hi = x.astype(jnp.bfloat16)
    lo = (x - hi.astype(jnp.float32)).astype(jnp.bfloat16)
    return hi, lo


def dot_bf16(a, b, dims):
    return lax.dot_general(a, b, (dims, ((), ())), preferred_element_type=jnp.float32)


def dot3(a, b, dims):
    return dot_bf16(a[0], b[0], dims) + (dot_bf16(a[0], b[1], dims) + dot_bf16(a[1], b[0], dims))


def assemble_kernel(slots_ref, x_ref, z_ref, *refs, sources, lead_tiles, pick_tiles, col_tiles, rows):
    source_refs, refs = refs[:sources], refs[sources:]
    lead_x_ref, lead_z_ref, schur_ref, front_ref, top_ref, every_ref, picked_ref, yx_ref, yz_ref, sem_ref = refs
    step = pl.program_id(0)
    share = every_ref.shape[0] // sources
    tile, parts, lanes = picked_ref.shape
    width = x_ref.shape[0]
    per_rank = width // lanes

    @pl.when(step == 0)
    def _():
        copies = [pltpu.make_async_copy(ref, every_ref.at[pl.ds(n * share, share)], sem_ref.at[n]) for n, ref in enumerate(source_refs)]
        for copy in copies:
            copy.start()
        for copy in copies:
            copy.wait()

    @pl.when(step < pick_tiles)
    def _():
        def pick(group, carry):
            for k in range(16):
                i = group * 16 + k
                picked_ref[i] = every_ref[slots_ref[step * tile + i]]
            return carry
        lax.fori_loop(0, tile // 16, pick, 0)
        by_part = jnp.swapaxes(picked_ref[...], 0, 1)
        images = []
        for r in range(RANK):
            mine = jnp.concatenate([by_part[r * per_rank + k] for k in range(per_rank)], axis=1)
            images.append((dot_bf16(mine, x_ref[...], NN).astype(jnp.bfloat16), dot_bf16(mine, z_ref[...], NN).astype(jnp.bfloat16)))

        @pl.when(step < lead_tiles)
        def _():
            for r in range(RANK):
                lead_x_ref[r], lead_z_ref[r] = images[r]

        @pl.when(step >= lead_tiles)
        def _():
            at = pl.ds(pl.multiple_of((step - lead_tiles) * tile, tile), tile)
            for r in range(RANK):
                yx_ref[r, at, :], yz_ref[r, at, :] = images[r]

    @pl.when(step >= pick_tiles)
    def _():
        high, wide = schur_ref.shape
        i, j = (step - pick_tiles) // col_tiles, (step - pick_tiles) % col_tiles
        left = pl.ds(pl.multiple_of(i * high, high), high)
        right = pl.ds(pl.multiple_of(rows + j * wide, wide), wide)
        value = gram_tile(yx_ref, yz_ref, left, right)
        schur_ref[...] = value

        @pl.when(j == 0)
        def _():
            front_ref[...] = value[:, :front_ref.shape[1]]

        @pl.when(i == 0)
        def _():
            top_ref[...] = value[:top_ref.shape[0], :]


def gram_tile(yx_ref, yz_ref, left, right):
    total = None
    for q in range(RANK):
        for r in range(RANK):
            gx = dot_bf16(yx_ref[r, left, :], yx_ref[q, right, :], NT)
            gz = dot_bf16(yz_ref[r, left, :], yz_ref[q, right, :], NT)
            if total is None:
                total = gx * gz
            elif rank_signs[q] * rank_signs[r] > 0:
                total = total + gx * gz
            else:
                total = total - gx * gz
    return total


def assemble(slots, sources, x_factor, z_factor, rows, cols, lead_rows, lead_cols):
    share, parts, lanes = sources[0].shape
    width = x_factor.shape[0]
    tile = 256
    high, wide = min(512, rows), min(256, cols)
    lead_tiles, pick_tiles = K // tile, slots.shape[0] // tile
    row_tiles, col_tiles = rows // high, cols // wide
    whole = pl.BlockSpec((width, width), lambda s: (0, 0), pipeline_mode=pl.Buffered(1))
    lead = pl.BlockSpec((RANK, tile, width), lambda s: (0, jnp.minimum(s, lead_tiles - 1), 0))
    after = lambda s: jnp.maximum(s - pick_tiles, 0)
    bf16 = jnp.bfloat16
    any_space = pl.BlockSpec(memory_space=pl.ANY)
    body = functools.partial(assemble_kernel, sources=len(sources), lead_tiles=lead_tiles, pick_tiles=pick_tiles, col_tiles=col_tiles, rows=rows)
    return pl.pallas_call(
        body,
        grid=(pick_tiles + row_tiles * col_tiles,),
        out_shape=(jax.ShapeDtypeStruct((RANK, K, width), bf16),) * 2 + (
            jax.ShapeDtypeStruct((rows, cols), jnp.float32),
            jax.ShapeDtypeStruct((rows, lead_cols), jnp.float32),
            jax.ShapeDtypeStruct((lead_rows, cols), jnp.float32)),
        in_specs=[SMEM, whole, whole] + [any_space] * len(sources),
        out_specs=(lead, lead,
                   pl.BlockSpec((high, wide), lambda s: (after(s) // col_tiles, after(s) % col_tiles)),
                   pl.BlockSpec((high, lead_cols), lambda s: (after(s) // col_tiles, 0)),
                   pl.BlockSpec((lead_rows, wide), lambda s: (0, jnp.minimum(after(s), col_tiles - 1)))),
        scratch_shapes=[pltpu.VMEM((len(sources) * share, parts, lanes), bf16), pltpu.VMEM((tile, parts, lanes), bf16)]
        + [pltpu.VMEM((RANK, rows + cols, width), bf16)] * 2 + [pltpu.SemaphoreType.DMA((len(sources),))],
        compiler_params=pltpu.CompilerParams(vmem_limit_bytes=58 * MIB),
        cost_estimate=pl.CostEstimate(flops=28 * 10**9, bytes_accessed=30 * MIB, transcendentals=0),
    )(slots, x_factor, z_factor, *sources)


def factor_block(block, u_ref, v_ref):
    count = BLK // SUB
    sub_iota = lax.broadcasted_iota(jnp.int32, (SUB, BLK), 0)
    lane_iota = lax.broadcasted_iota(jnp.int32, (SUB, BLK), 1)
    rows_a = [block[SUB * i:SUB * (i + 1), :] for i in range(count)]
    rows_v = [(lane_iota == sub_iota + SUB * i).astype(jnp.float32) for i in range(count)]

    def spread_lane(x, lane):
        return jnp.broadcast_to(x[:, lane:lane + 1], (SUB, BLK))

    def spread_row(x, row):
        return jnp.broadcast_to(x[row:row + 1, :], (SUB, BLK))

    for m in range(count):
        head_a, head_v = rows_a[m], rows_v[m]
        cols = [spread_lane(head_a, SUB * m + k) for k in range(SUB)]
        below = [[spread_lane(rows_a[i], SUB * m + k) for k in range(SUB)] for i in range(m + 1, count)]
        scale = jnp.zeros((SUB, BLK), jnp.float32)
        for j in range(SUB):
            pivot = spread_row(cols[j], j)
            root = lax.rsqrt(pivot)
            scale = jnp.where(sub_iota == j, root, scale)
            mult = jnp.where(sub_iota > j, cols[j] * root, 0.0)
            row_a = spread_row(head_a, j) * root
            row_v = spread_row(head_v, j) * root
            lead = [spread_row(cols[k], j) * root if k > j else None for k in range(SUB)]
            if j + 1 < SUB:
                head_a = head_a - mult * row_a
                head_v = head_v - mult * row_v
                for k in range(j + 1, SUB):
                    cols[k] = cols[k] - mult * lead[k]
            for n, i in enumerate(range(m + 1, count)):
                mult_i = below[n][j] * root
                rows_a[i] = rows_a[i] - mult_i * row_a
                rows_v[i] = rows_v[i] - mult_i * row_v
                for k in range(j + 1, SUB):
                    below[n][k] = below[n][k] - mult_i * lead[k]
        u = jnp.where(lane_iota >= sub_iota + SUB * m, head_a * scale, 0.0)
        v = jnp.where(lane_iota <= sub_iota + SUB * m, head_v * scale, 0.0)
        u_ref[SUB * m:SUB * (m + 1), :] = u
        v_ref[SUB * m:SUB * (m + 1), :] = v


def factor_kernel(yx_ref, yz_ref, l_ref, d_ref, w_ref, u_ref, v_ref):
    order = l_ref.shape[0]
    steps = order // BLK
    tile = 256
    l_ref[...] = jnp.zeros_like(l_ref)
    w_ref[...] = jnp.zeros_like(w_ref)

    def columns(j, carry):
        right = pl.ds(pl.multiple_of(j * tile, tile), tile)

        def rows(i, carry):
            left = pl.ds(pl.multiple_of(i * tile, tile), tile)
            w_ref[left, right] = gram_tile(yx_ref, yz_ref, left, right)
            return carry
        return lax.fori_loop(j, order // tile, rows, carry)
    lax.fori_loop(0, order // tile, columns, 0)

    def step(b, carry):
        at = pl.ds(pl.multiple_of(b * BLK, BLK), BLK)
        factor_block(w_ref[at, at], u_ref, v_ref)
        l_ref[at, at] = u_ref[...].T
        d_ref[at, :] = v_ref[...]
        for k in range(steps - 1):
            @pl.when(b == k)
            def _():
                first = (k + 1) * BLK
                inv = split(v_ref[...])
                def panel(t, c):
                    rows = pl.ds(pl.multiple_of(first + t * BLK, BLK), BLK)
                    l_ref[rows, k * BLK:first] = dot3(split(w_ref[rows, k * BLK:first]), inv, NT)
                    return c
                lax.fori_loop(0, steps - 1 - k, panel, 0)
                right = split(l_ref[first:, k * BLK:first])
                def update(t, c):
                    rows = pl.ds(pl.multiple_of(first + t * BLK, BLK), BLK)
                    left = split(l_ref[rows, k * BLK:first])
                    w_ref[rows, first:] = w_ref[rows, first:] - dot3(left, right, NT)
                    return c
                lax.fori_loop(0, steps - 1 - k, update, 0)
        return carry
    lax.fori_loop(0, steps, step, 0)


def factor(yx, yz):
    return pl.pallas_call(
        factor_kernel,
        out_shape=(jax.ShapeDtypeStruct((K, K), jnp.float32), jax.ShapeDtypeStruct((K, BLK), jnp.float32)),
        in_specs=[VMEM] * 2,
        out_specs=(VMEM, VMEM),
        scratch_shapes=[pltpu.VMEM((K, K), jnp.float32), pltpu.VMEM((BLK, BLK), jnp.float32), pltpu.VMEM((BLK, BLK), jnp.float32)],
        compiler_params=pltpu.CompilerParams(vmem_limit_bytes=48 * MIB),
        cost_estimate=pl.CostEstimate(flops=40 * 10**9, bytes_accessed=12 * MIB, transcendentals=0),
    )(yx, yz)


def solve_kernel(column_ref, l_ref, d_ref, pieces_ref, tops_ref, schur_ref, rest_ref, panel_ref, lh, ll, xh, xl, zh, zl):
    pcol = pieces_ref.shape[0]
    prow = tops_ref.shape[0]
    column = column_ref[0]
    lh[...], ll[...] = split(l_ref[...])
    wide = 2 * BLK
    for b in range(K // wide):
        at = slice(b * wide, (b + 1) * wide)
        upper, lower = slice(b * wide, b * wide + BLK), slice(b * wide + BLK, (b + 1) * wide)
        first, second = split(d_ref[upper, :]), split(d_ref[lower, :])
        between = dot3((lh[lower, upper], ll[lower, upper]), first, NN)
        corner = -dot3(second, split(between), NN)
        inverse = split(jnp.concatenate([
            jnp.concatenate([d_ref[upper, :], jnp.zeros((BLK, BLK), jnp.float32)], axis=1),
            jnp.concatenate([corner, d_ref[lower, :]], axis=1)], axis=0))
        blocks = range(wide // NB * b, wide // NB * (b + 1))
        value = jnp.concatenate([pieces_ref[n % pcol, :, n // pcol * NB:(n // pcol + 1) * NB] for n in blocks], axis=1)
        top = jnp.concatenate([tops_ref[n % prow, n // prow * NB:(n // prow + 1) * NB, :] for n in blocks], axis=0)
        if b > 0:
            done = slice(0, b * wide)
            left = (lh[at, done], ll[at, done])
            value = value - dot3((xh[:, done], xl[:, done]), left, NT)
            top = top - dot3(left, (zh[done, :], zl[done, :]), NN)
        value = dot3(split(value), inverse, NT)
        top = dot3(inverse, split(top), NN)
        xh[:, at], xl[:, at] = split(value)
        zh[at, :], zl[at, :] = split(top)
        for place, block in enumerate(blocks):
            @pl.when(column == block % pcol)
            def _():
                panel_ref[:, block // pcol * NB:(block // pcol + 1) * NB] = value[:, place * NB:(place + 1) * NB]
    rest_ref[...] = schur_ref[...] - dot3((xh[...], xl[...]), (zh[...], zl[...]), NN)


def solve(column, low, inverses, pieces, tops, schur):
    rows, cols = schur.shape
    lead = K // pieces.shape[0]
    bf16 = jnp.bfloat16
    return pl.pallas_call(
        solve_kernel,
        out_shape=(jax.ShapeDtypeStruct((rows, cols), jnp.float32), jax.ShapeDtypeStruct((rows, lead), jnp.float32)),
        in_specs=[SMEM] + [VMEM] * 5,
        out_specs=(VMEM, VMEM),
        scratch_shapes=[pltpu.VMEM((K, K), bf16)] * 2 + [pltpu.VMEM((rows, K), bf16)] * 2 + [pltpu.VMEM((K, cols), bf16)] * 2,
        compiler_params=pltpu.CompilerParams(vmem_limit_bytes=56 * MIB),
        cost_estimate=pl.CostEstimate(flops=12 * 10**9, bytes_accessed=24 * MIB, transcendentals=0),
    )(column, low, inverses, pieces, tops, schur)


def gather_factors(mine, prow_count, pcol_count):
    own = mine.shape[0]
    half = own // 2

    def swap(axis, count, turn, value):
        return lax.ppermute(value, axis, [(n, n ^ turn) for n in range(count)])

    items = {0: mine}
    for turn in range(1, prow_count, 2):
        items[turn] = swap("prow", prow_count, turn, mine)
    for turn in range(2, prow_count, 2):
        items[turn] = swap("prow", prow_count, 1, items[turn + 1])
    near, far = {}, {}
    for turn in [0] + list(range(1, prow_count, 2)) + list(range(2, prow_count, 2)):
        held = {0: items[turn]}
        for j in range(1, pcol_count // 2):
            low = j & -j
            high = 1 << (j.bit_length() - 1)
            if low == high:
                held[j] = swap("pcol", pcol_count, 2 * j, items[turn])
            else:
                held[j] = jnp.concatenate([swap("pcol", pcol_count, 2 * high, held[j ^ high][:half]), swap("pcol", pcol_count, 2 * low, held[j ^ low][half:])])
        near[turn] = jnp.concatenate([held[j] for j in range(pcol_count // 2)])
        far[turn] = swap("pcol", pcol_count, 1, near[turn])
    return [near[m] for m in range(prow_count)] + [far[m] for m in range(prow_count)]


def per_device(factors, x_factor, zinv_factor, placement):
    prow_count = lax.axis_size("prow")
    pcol_count = lax.axis_size("pcol")
    total_rows = placement.shape[0]
    local_rows = total_rows // prow_count
    local_cols = total_rows // pcol_count
    prow_id = lax.axis_index("prow")
    pcol_id = lax.axis_index("pcol")
    _, own, width = factors.shape
    count = prow_count * pcol_count
    lanes = BLK
    mine = factors.transpose(1, 0, 2).reshape(own, RANK * width // lanes, lanes)
    sources = gather_factors(mine, prow_count, pcol_count)
    slot_k = jnp.arange(local_rows)
    natural_k = slot_k // NB * NB * prow_count + prow_id * NB + slot_k % NB
    slot_j = jnp.arange(local_cols)
    natural_j = slot_j // NB * NB * pcol_count + pcol_id * NB + slot_j % NB
    inverse = jnp.zeros((total_rows,), jnp.int32).at[placement].set(jnp.arange(total_rows, dtype=jnp.int32))
    wanted = jnp.concatenate([jnp.arange(K), natural_k, natural_j]).astype(jnp.int32)
    slots = inverse[wanted]
    holder = slots // own
    row_turn, col_turn = (holder // pcol_count) ^ prow_id, (holder % pcol_count) ^ pcol_id
    places = (((col_turn % 2) * prow_count + row_turn) * (pcol_count // 2) + col_turn // 2) * own + slots % own
    lead_rows, lead_cols = K // prow_count, K // pcol_count
    lead_x, lead_z, schur_local, front, top = assemble(
        places.astype(jnp.int32), sources, x_factor, zinv_factor, local_rows, local_cols, lead_rows, lead_cols)
    pieces = lax.all_gather(front, "pcol", axis=0, tiled=False)
    tops = lax.all_gather(top, "prow", axis=0, tiled=False)
    low, inverses = factor(lead_x, lead_z)
    return solve(pcol_id.astype(jnp.int32).reshape(1), low, inverses, pieces, tops, schur_local)


def solution(mesh):
    in_specs = (P(None, ("prow", "pcol"), None), P(), P(), P())
    out_specs = (P("prow", "pcol"), P("prow", "pcol"))
    return jax.shard_map(
        per_device, mesh=mesh, in_specs=in_specs, out_specs=out_specs, check_vma=False
    )
```

```python
import functools

import jax
import jax.numpy as jnp
from jax import lax
from jax.experimental import pallas as pl
from jax.experimental.pallas import tpu as pltpu
from jax.sharding import PartitionSpec as P

RANK = 4
NB = 64
K = 1024
SUB = 8
BLK = 128
MIB = 2**20

rank_signs = (1.0, 1.0, -1.0, -1.0)
NT = ((1,), (1,))
NN = ((1,), (0,))
VMEM = pl.BlockSpec(memory_space=pltpu.VMEM)
SMEM = pl.BlockSpec(memory_space=pltpu.SMEM)


def split(x):
    hi = x.astype(jnp.bfloat16)
    lo = (x - hi.astype(jnp.float32)).astype(jnp.bfloat16)
    return hi, lo


def dot_bf16(a, b, dims):
    return lax.dot_general(a, b, (dims, ((), ())), preferred_element_type=jnp.float32)


def dot3(a, b, dims):
    return dot_bf16(a[0], b[0], dims) + (dot_bf16(a[0], b[1], dims) + dot_bf16(a[1], b[0], dims))


def assemble_kernel(slots_ref, x_ref, z_ref, *refs, sources, lead_tiles, pick_tiles, col_tiles, rows):
    source_refs, refs = refs[:sources], refs[sources:]
    lead_x_ref, lead_z_ref, schur_ref, front_ref, top_ref, every_ref, picked_ref, yx_ref, yz_ref, sem_ref = refs
    step = pl.program_id(0)
    tile, parts, lanes = picked_ref.shape
    width = x_ref.shape[0]
    per_rank = width // lanes

    @pl.when(step == 0)
    def _():
        copies, first = [], 0
        for n, ref in enumerate(source_refs):
            copies.append(pltpu.make_async_copy(ref, every_ref.at[pl.ds(first, ref.shape[0])], sem_ref.at[n]))
            first += ref.shape[0]
        for copy in copies:
            copy.start()
        for copy in copies:
            copy.wait()

    @pl.when(step < pick_tiles)
    def _():
        def pick(group, carry):
            for k in range(16):
                i = group * 16 + k
                picked_ref[i] = every_ref[slots_ref[step * tile + i]]
            return carry
        lax.fori_loop(0, tile // 16, pick, 0)
        by_part = jnp.swapaxes(picked_ref[...], 0, 1)
        images = []
        for r in range(RANK):
            mine = jnp.concatenate([by_part[r * per_rank + k] for k in range(per_rank)], axis=1)
            images.append((dot_bf16(mine, x_ref[...], NN).astype(jnp.bfloat16), dot_bf16(mine, z_ref[...], NN).astype(jnp.bfloat16)))

        @pl.when(step < lead_tiles)
        def _():
            for r in range(RANK):
                lead_x_ref[r], lead_z_ref[r] = images[r]

        @pl.when(step >= lead_tiles)
        def _():
            at = pl.ds(pl.multiple_of((step - lead_tiles) * tile, tile), tile)
            for r in range(RANK):
                yx_ref[r, at, :], yz_ref[r, at, :] = images[r]

    @pl.when(step >= pick_tiles)
    def _():
        high, wide = schur_ref.shape
        i, j = (step - pick_tiles) // col_tiles, (step - pick_tiles) % col_tiles
        left = pl.ds(pl.multiple_of(i * high, high), high)
        right = pl.ds(pl.multiple_of(rows + j * wide, wide), wide)
        value = gram_tile(yx_ref, yz_ref, left, right)
        schur_ref[...] = value

        @pl.when(j == 0)
        def _():
            front_ref[...] = value[:, :front_ref.shape[1]]

        @pl.when(i == 0)
        def _():
            top_ref[...] = value[:top_ref.shape[0], :]


def gram_tile(yx_ref, yz_ref, left, right):
    total = None
    for q in range(RANK):
        for r in range(RANK):
            gx = dot_bf16(yx_ref[r, left, :], yx_ref[q, right, :], NT)
            gz = dot_bf16(yz_ref[r, left, :], yz_ref[q, right, :], NT)
            if total is None:
                total = gx * gz
            elif rank_signs[q] * rank_signs[r] > 0:
                total = total + gx * gz
            else:
                total = total - gx * gz
    return total


def assemble(slots, sources, x_factor, z_factor, rows, cols, lead_rows, lead_cols):
    _, parts, lanes = sources[0].shape
    slots_held = sum(source.shape[0] for source in sources)
    width = x_factor.shape[0]
    tile = 256
    high, wide = min(512, rows), min(256, cols)
    lead_tiles, pick_tiles = K // tile, slots.shape[0] // tile
    row_tiles, col_tiles = rows // high, cols // wide
    whole = pl.BlockSpec((width, width), lambda s: (0, 0), pipeline_mode=pl.Buffered(1))
    lead = pl.BlockSpec((RANK, tile, width), lambda s: (0, jnp.minimum(s, lead_tiles - 1), 0))
    after = lambda s: jnp.maximum(s - pick_tiles, 0)
    bf16 = jnp.bfloat16
    any_space = pl.BlockSpec(memory_space=pl.ANY)
    body = functools.partial(assemble_kernel, sources=len(sources), lead_tiles=lead_tiles, pick_tiles=pick_tiles, col_tiles=col_tiles, rows=rows)
    return pl.pallas_call(
        body,
        grid=(pick_tiles + row_tiles * col_tiles,),
        out_shape=(jax.ShapeDtypeStruct((RANK, K, width), bf16),) * 2 + (
            jax.ShapeDtypeStruct((rows, cols), jnp.float32),
            jax.ShapeDtypeStruct((rows, lead_cols), jnp.float32),
            jax.ShapeDtypeStruct((lead_rows, cols), jnp.float32)),
        in_specs=[SMEM, whole, whole] + [any_space] * len(sources),
        out_specs=(lead, lead,
                   pl.BlockSpec((high, wide), lambda s: (after(s) // col_tiles, after(s) % col_tiles)),
                   pl.BlockSpec((high, lead_cols), lambda s: (after(s) // col_tiles, 0)),
                   pl.BlockSpec((lead_rows, wide), lambda s: (0, jnp.minimum(after(s), col_tiles - 1)))),
        scratch_shapes=[pltpu.VMEM((slots_held, parts, lanes), bf16), pltpu.VMEM((tile, parts, lanes), bf16)]
        + [pltpu.VMEM((RANK, rows + cols, width), bf16)] * 2 + [pltpu.SemaphoreType.DMA((len(sources),))],
        compiler_params=pltpu.CompilerParams(vmem_limit_bytes=58 * MIB),
        cost_estimate=pl.CostEstimate(flops=28 * 10**9, bytes_accessed=30 * MIB, transcendentals=0),
    )(slots, x_factor, z_factor, *sources)


def factor_block(block, u_ref, v_ref, beside):
    count = BLK // SUB
    sub_iota = lax.broadcasted_iota(jnp.int32, (SUB, BLK), 0)
    lane_iota = lax.broadcasted_iota(jnp.int32, (SUB, BLK), 1)
    rows_a = [block[SUB * i:SUB * (i + 1), :] for i in range(count)]
    rows_v = [(lane_iota == sub_iota + SUB * i).astype(jnp.float32) for i in range(count)]

    def spread_lane(x, lane):
        return jnp.broadcast_to(x[:, lane:lane + 1], (SUB, BLK))

    def spread_row(x, row):
        return jnp.broadcast_to(x[row:row + 1, :], (SUB, BLK))

    for m in range(count):
        beside(m)
        head_a, head_v = rows_a[m], rows_v[m]
        cols = [spread_lane(head_a, SUB * m + k) for k in range(SUB)]
        below = [[spread_lane(rows_a[i], SUB * m + k) for k in range(SUB)] for i in range(m + 1, count)]
        scale = jnp.zeros((SUB, BLK), jnp.float32)
        for j in range(SUB):
            pivot = spread_row(cols[j], j)
            root = lax.rsqrt(pivot)
            scale = jnp.where(sub_iota == j, root, scale)
            mult = jnp.where(sub_iota > j, cols[j] * root, 0.0)
            row_a = spread_row(head_a, j) * root
            row_v = spread_row(head_v, j) * root
            lead = [spread_row(cols[k], j) * root if k > j else None for k in range(SUB)]
            if j + 1 < SUB:
                head_a = head_a - mult * row_a
                head_v = head_v - mult * row_v
                for k in range(j + 1, SUB):
                    cols[k] = cols[k] - mult * lead[k]
            for n, i in enumerate(range(m + 1, count)):
                mult_i = below[n][j] * root
                rows_a[i] = rows_a[i] - mult_i * row_a
                rows_v[i] = rows_v[i] - mult_i * row_v
                for k in range(j + 1, SUB):
                    below[n][k] = below[n][k] - mult_i * lead[k]
        u = jnp.where(lane_iota >= sub_iota + SUB * m, head_a * scale, 0.0)
        v = jnp.where(lane_iota <= sub_iota + SUB * m, head_v * scale, 0.0)
        u_ref[SUB * m:SUB * (m + 1), :] = u
        v_ref[SUB * m:SUB * (m + 1), :] = v


def factor_kernel(yx_ref, yz_ref, l_ref, d_ref, w_ref, g_ref, u_ref, v_ref):
    order = l_ref.shape[0]
    steps = order // BLK
    tile = 2 * BLK
    window = 3 * BLK
    l_ref[...] = jnp.zeros_like(l_ref)
    w_ref[...] = jnp.zeros_like(w_ref)

    def rows_of(i, carry):
        left = pl.ds(pl.multiple_of(i * 2 * tile, 2 * tile), 2 * tile)
        w_ref[left, :tile] = gram_tile(yx_ref, yz_ref, left, pl.ds(0, tile))
        return carry
    lax.fori_loop(0, order // (2 * tile), rows_of, 0)

    def step(b, carry):
        at = pl.ds(pl.multiple_of(b * BLK, BLK), BLK)
        ahead = jnp.minimum(b // 2 + 1, order // tile - 1)
        left = pl.ds(pl.multiple_of(jnp.minimum(ahead * tile + (b % 2) * window, order - window), BLK), window)
        right = pl.ds(pl.multiple_of(ahead * tile, tile), tile)

        def beside(m):
            q, r = m // RANK, m % RANK
            term = dot_bf16(yx_ref[r, left, :], yx_ref[q, right, :], NT) * dot_bf16(yz_ref[r, left, :], yz_ref[q, right, :], NT)
            if m == 0:
                g_ref[left, :] = term
            elif rank_signs[q] * rank_signs[r] > 0:
                g_ref[left, :] = g_ref[left, :] + term
            else:
                g_ref[left, :] = g_ref[left, :] - term

        factor_block(w_ref[at, at], u_ref, v_ref, beside)
        l_ref[at, at] = u_ref[...].T
        d_ref[at, :] = v_ref[...]
        for k in range(steps - 1):
            @pl.when(b == k)
            def _():
                first = (k + 1) * BLK
                inv = split(v_ref[...])
                def panel(t, c):
                    rows = pl.ds(pl.multiple_of(first + t * BLK, BLK), BLK)
                    l_ref[rows, k * BLK:first] = dot3(split(w_ref[rows, k * BLK:first]), inv, NT)
                    return c
                lax.fori_loop(0, steps - 1 - k, panel, 0)
                right = split(l_ref[first:, k * BLK:first])
                def update(t, c):
                    rows = pl.ds(pl.multiple_of(first + t * BLK, BLK), BLK)
                    left = split(l_ref[rows, k * BLK:first])
                    w_ref[rows, first:] = w_ref[rows, first:] - dot3(left, right, NT)
                    return c
                lax.fori_loop(0, steps - 1 - k, update, 0)
                if k % 2 == 1:
                    w_ref[first:, first:first + tile] = w_ref[first:, first:first + tile] + g_ref[first:, :]
        return carry
    lax.fori_loop(0, steps, step, 0)


def factor(yx, yz):
    return pl.pallas_call(
        factor_kernel,
        out_shape=(jax.ShapeDtypeStruct((K, K), jnp.float32), jax.ShapeDtypeStruct((K, BLK), jnp.float32)),
        in_specs=[VMEM] * 2,
        out_specs=(VMEM, VMEM),
        scratch_shapes=[pltpu.VMEM((K, K), jnp.float32), pltpu.VMEM((K, 2 * BLK), jnp.float32), pltpu.VMEM((BLK, BLK), jnp.float32), pltpu.VMEM((BLK, BLK), jnp.float32)],
        compiler_params=pltpu.CompilerParams(vmem_limit_bytes=48 * MIB),
        cost_estimate=pl.CostEstimate(flops=40 * 10**9, bytes_accessed=12 * MIB, transcendentals=0),
    )(yx, yz)


def solve_kernel(place_ref, l_ref, d_ref, pieces_ref, tops_ref, schur_ref, rest_ref, panel_ref, lh, ll, xh, xl, zh, zl):
    pcol = pieces_ref.shape[0]
    prow = tops_ref.shape[0]
    row, column = place_ref[0], place_ref[1]
    lh[...], ll[...] = split(l_ref[...])
    wide = 2 * BLK
    for b in range(K // wide):
        at = slice(b * wide, (b + 1) * wide)
        upper, lower = slice(b * wide, b * wide + BLK), slice(b * wide + BLK, (b + 1) * wide)
        first, second = split(d_ref[upper, :]), split(d_ref[lower, :])
        between = dot3((lh[lower, upper], ll[lower, upper]), first, NN)
        corner = -dot3(second, split(between), NN)
        inverse = split(jnp.concatenate([
            jnp.concatenate([d_ref[upper, :], jnp.zeros((BLK, BLK), jnp.float32)], axis=1),
            jnp.concatenate([corner, d_ref[lower, :]], axis=1)], axis=0))
        blocks = range(wide // NB * b, wide // NB * (b + 1))
        value = jnp.concatenate([pieces_ref[n % pcol, :, n // pcol * NB:(n // pcol + 1) * NB] for n in blocks], axis=1)
        top = jnp.concatenate([tops_ref[(n % prow) ^ row, n // prow * NB:(n // prow + 1) * NB, :] for n in blocks], axis=0)
        if b > 0:
            done = slice(0, b * wide)
            left = (lh[at, done], ll[at, done])
            value = value - dot3((xh[:, done], xl[:, done]), left, NT)
            top = top - dot3(left, (zh[done, :], zl[done, :]), NN)
        value = dot3(split(value), inverse, NT)
        top = dot3(inverse, split(top), NN)
        xh[:, at], xl[:, at] = split(value)
        zh[at, :], zl[at, :] = split(top)
        for place, block in enumerate(blocks):
            @pl.when(column == block % pcol)
            def _():
                panel_ref[:, block // pcol * NB:(block // pcol + 1) * NB] = value[:, place * NB:(place + 1) * NB]
    rest_ref[...] = schur_ref[...] - dot3((xh[...], xl[...]), (zh[...], zl[...]), NN)


def solve(place, low, inverses, pieces, tops, schur):
    rows, cols = schur.shape
    lead = K // pieces.shape[0]
    bf16 = jnp.bfloat16
    return pl.pallas_call(
        solve_kernel,
        out_shape=(jax.ShapeDtypeStruct((rows, cols), jnp.float32), jax.ShapeDtypeStruct((rows, lead), jnp.float32)),
        in_specs=[SMEM] + [VMEM] * 5,
        out_specs=(VMEM, VMEM),
        scratch_shapes=[pltpu.VMEM((K, K), bf16)] * 2 + [pltpu.VMEM((rows, K), bf16)] * 2 + [pltpu.VMEM((K, cols), bf16)] * 2,
        compiler_params=pltpu.CompilerParams(vmem_limit_bytes=56 * MIB),
        cost_estimate=pl.CostEstimate(flops=12 * 10**9, bytes_accessed=24 * MIB, transcendentals=0),
    )(place, low, inverses, pieces, tops, schur)


def gather_factors(mine, prow_count, pcol_count):
    own = mine.shape[0]
    half = own // 2

    def swap(axis, count, turn, value):
        return lax.ppermute(value, axis, [(n, n ^ turn) for n in range(count)])

    items = {0: mine}
    for turn in range(1, prow_count, 2):
        items[turn] = swap("prow", prow_count, turn, mine)
    for turn in range(2, prow_count, 2):
        items[turn] = swap("prow", prow_count, 1, items[turn + 1])
    near, far, near_order, far_order = [], [], [], []
    groups = [[0], [1], [m ^ 1 for m in range(2, prow_count)]]
    for n, group in enumerate(groups):
        value = jnp.concatenate([items[m] for m in group]) if len(group) > 1 else items[group[0]]
        middle = len(group) * half
        held = {0: value}
        for j in range(1, pcol_count // 2):
            low = j & -j
            high = 1 << (j.bit_length() - 1)
            if low == high:
                held[j] = swap("pcol", pcol_count, 2 * j, value)
            else:
                held[j] = jnp.concatenate([swap("pcol", pcol_count, 2 * high, held[j ^ high][:middle]), swap("pcol", pcol_count, 2 * low, held[j ^ low][middle:])])
        direct = [j for j in held if j & (j - 1) == 0]
        relayed = [j for j in held if j & (j - 1) != 0]
        for part in [direct, relayed] if n == len(groups) - 1 else [direct + relayed]:
            whole = jnp.concatenate([held[j] for j in part]) if len(part) > 1 else held[part[0]]
            near.append(whole)
            near_order += [(m, 2 * j) for j in part for m in group]
            far.append(swap("pcol", pcol_count, 1, whole))
            far_order += [(m, 2 * j + 1) for j in part for m in group]
    return near + far, near_order + far_order


def places_of(placement, order, prow_id, pcol_id, pcol_count):
    total = placement.shape[0]
    own = total // len(order)
    unit_of = [0] * len(order)
    for unit, (row_turn, col_turn) in enumerate(order):
        unit_of[row_turn * pcol_count + col_turn] = unit
    holder = jnp.arange(len(order))
    turn = ((holder // pcol_count) ^ prow_id) * pcol_count + ((holder % pcol_count) ^ pcol_id)
    units = jnp.sum(jnp.where(turn[:, None] == jnp.arange(len(order))[None, :], jnp.array(unit_of)[None, :], 0), axis=1)
    place = (units[:, None] * own + jnp.arange(own)[None, :]).reshape(1, total)
    blocks = total // NB
    in_block = jnp.arange(blocks)[:, None] == placement[None, :] // NB
    digits = jnp.concatenate([jnp.where(in_block, place // NB, 0), jnp.where(in_block, place % NB, 0)]).astype(jnp.bfloat16)
    at_row = (jnp.arange(NB)[:, None] == placement[None, :] % NB).astype(jnp.bfloat16)
    found = dot_bf16(digits, at_row, NT).astype(jnp.int32)
    return found[:blocks] * NB + found[blocks:]


def per_device(factors, x_factor, zinv_factor, placement):
    prow_count = lax.axis_size("prow")
    pcol_count = lax.axis_size("pcol")
    total_rows = placement.shape[0]
    local_rows = total_rows // prow_count
    local_cols = total_rows // pcol_count
    prow_id = lax.axis_index("prow")
    pcol_id = lax.axis_index("pcol")
    _, own, width = factors.shape
    count = prow_count * pcol_count
    lanes = BLK
    mine = factors.transpose(1, 0, 2).reshape(own, RANK * width // lanes, lanes)
    sources, order = gather_factors(mine, prow_count, pcol_count)
    found = places_of(placement, order, prow_id, pcol_id, pcol_count)
    by_row = lax.dynamic_index_in_dim(found.reshape(local_rows // NB, prow_count, NB), prow_id, 1, keepdims=False)
    by_col = lax.dynamic_index_in_dim(found.reshape(local_cols // NB, pcol_count, NB), pcol_id, 1, keepdims=False)
    places = jnp.concatenate([found[:K // NB], by_row, by_col]).reshape(-1)
    lead_rows, lead_cols = K // prow_count, K // pcol_count
    lead_x, lead_z, schur_local, front, top = assemble(
        places.astype(jnp.int32), sources, x_factor, zinv_factor, local_rows, local_cols, lead_rows, lead_cols)
    pieces = lax.all_gather(front, "pcol", axis=0, tiled=False)
    turned = [lax.ppermute(top, "prow", [(n, n ^ turn) for n in range(prow_count)]) for turn in range(1, prow_count)]
    tops = jnp.stack([top] + turned)
    low, inverses = factor(lead_x, lead_z)
    return solve(jnp.stack([prow_id, pcol_id]).astype(jnp.int32), low, inverses, pieces, tops, schur_local)


def solution(mesh):
    in_specs = (P(None, ("prow", "pcol"), None), P(), P(), P())
    out_specs = (P("prow", "pcol"), P("prow", "pcol"))
    return jax.shard_map(
        per_device, mesh=mesh, in_specs=in_specs, out_specs=out_specs, check_vma=False
    )
```

```python
import functools

import jax
import jax.numpy as jnp
from jax import lax
from jax.experimental import pallas as pl
from jax.experimental.pallas import tpu as pltpu
from jax.sharding import PartitionSpec as P

RANK = 4
NB = 64
K = 1024
SUB = 8
BLK = 128
MIB = 2**20

rank_signs = (1.0, 1.0, -1.0, -1.0)
NT = ((1,), (1,))
NN = ((1,), (0,))
VMEM = pl.BlockSpec(memory_space=pltpu.VMEM)
SMEM = pl.BlockSpec(memory_space=pltpu.SMEM)


def split(x):
    hi = x.astype(jnp.bfloat16)
    lo = (x - hi.astype(jnp.float32)).astype(jnp.bfloat16)
    return hi, lo


def dot_bf16(a, b, dims):
    return lax.dot_general(a, b, (dims, ((), ())), preferred_element_type=jnp.float32)


def dot3(a, b, dims):
    return dot_bf16(a[0], b[0], dims) + (dot_bf16(a[0], b[1], dims) + dot_bf16(a[1], b[0], dims))


def assemble_kernel(slots_ref, x_ref, z_ref, *refs, sources, lead_tiles, pick_tiles, col_tiles, rows):
    source_refs, refs = refs[:sources], refs[sources:]
    lead_x_ref, lead_z_ref, schur_ref, front_ref, top_ref, every_ref, picked_ref, yx_ref, yz_ref, sem_ref = refs
    step = pl.program_id(0)
    tile, parts, lanes = picked_ref.shape
    width = x_ref.shape[0]
    per_rank = width // lanes

    @pl.when(step == 0)
    def _():
        copies, first = [], 0
        for n, ref in enumerate(source_refs):
            copies.append(pltpu.make_async_copy(ref, every_ref.at[pl.ds(first, ref.shape[0])], sem_ref.at[n]))
            first += ref.shape[0]
        for copy in copies:
            copy.start()
        for copy in copies:
            copy.wait()

    @pl.when(step < pick_tiles)
    def _():
        def pick(group, carry):
            for k in range(16):
                i = group * 16 + k
                picked_ref[i] = every_ref[slots_ref[step * tile + i]]
            return carry
        lax.fori_loop(0, tile // 16, pick, 0)
        by_part = jnp.swapaxes(picked_ref[...], 0, 1)
        mine = jnp.concatenate([
            jnp.concatenate([by_part[r * per_rank + k] for k in range(per_rank)], axis=1) for r in range(RANK)], axis=0)
        images_x = dot_bf16(mine, x_ref[...], NN).astype(jnp.bfloat16).reshape(RANK, tile, width)
        images_z = dot_bf16(mine, z_ref[...], NN).astype(jnp.bfloat16).reshape(RANK, tile, width)

        @pl.when(step < lead_tiles)
        def _():
            lead_x_ref[...], lead_z_ref[...] = images_x, images_z

        @pl.when(step >= lead_tiles)
        def _():
            at = pl.ds(pl.multiple_of((step - lead_tiles) * tile, tile), tile)
            yx_ref[:, at, :], yz_ref[:, at, :] = images_x, images_z

    @pl.when(step >= pick_tiles)
    def _():
        high, wide = schur_ref.shape
        i, j = (step - pick_tiles) // col_tiles, (step - pick_tiles) % col_tiles
        left = pl.ds(pl.multiple_of(i * high, high), high)
        right = pl.ds(pl.multiple_of(rows + j * wide, wide), wide)
        value = gram_tile(yx_ref, yz_ref, left, right)
        schur_ref[...] = value

        @pl.when(j == 0)
        def _():
            front_ref[...] = value[:, :front_ref.shape[1]]

        @pl.when(i == 0)
        def _():
            top_ref[...] = value[:top_ref.shape[0], :]


def gram_tile(yx_ref, yz_ref, left, right):
    left_x, left_z = yx_ref[:, left, :], yz_ref[:, left, :]
    _, high, width = left_x.shape
    left_x, left_z = left_x.reshape(RANK * high, width), left_z.reshape(RANK * high, width)
    total = None
    for q in range(RANK):
        gx = dot_bf16(left_x, yx_ref[q, right, :], NT)
        gz = dot_bf16(left_z, yz_ref[q, right, :], NT)
        for r in range(RANK):
            term = gx[r * high:(r + 1) * high] * gz[r * high:(r + 1) * high]
            if total is None:
                total = term
            elif rank_signs[q] * rank_signs[r] > 0:
                total = total + term
            else:
                total = total - term
    return total


def assemble(slots, sources, x_factor, z_factor, rows, cols, lead_rows, lead_cols):
    _, parts, lanes = sources[0].shape
    slots_held = sum(source.shape[0] for source in sources)
    width = x_factor.shape[0]
    tile = 256
    high, wide = min(512, rows), min(256, cols)
    lead_tiles, pick_tiles = K // tile, slots.shape[0] // tile
    row_tiles, col_tiles = rows // high, cols // wide
    whole = pl.BlockSpec((width, width), lambda s: (0, 0), pipeline_mode=pl.Buffered(1))
    lead = pl.BlockSpec((RANK, tile, width), lambda s: (0, jnp.minimum(s, lead_tiles - 1), 0))
    after = lambda s: jnp.maximum(s - pick_tiles, 0)
    bf16 = jnp.bfloat16
    any_space = pl.BlockSpec(memory_space=pl.ANY)
    body = functools.partial(assemble_kernel, sources=len(sources), lead_tiles=lead_tiles, pick_tiles=pick_tiles, col_tiles=col_tiles, rows=rows)
    return pl.pallas_call(
        body,
        grid=(pick_tiles + row_tiles * col_tiles,),
        out_shape=(jax.ShapeDtypeStruct((RANK, K, width), bf16),) * 2 + (
            jax.ShapeDtypeStruct((rows, cols), jnp.float32),
            jax.ShapeDtypeStruct((rows, lead_cols), jnp.float32),
            jax.ShapeDtypeStruct((lead_rows, cols), jnp.float32)),
        in_specs=[SMEM, whole, whole] + [any_space] * len(sources),
        out_specs=(lead, lead,
                   pl.BlockSpec((high, wide), lambda s: (after(s) // col_tiles, after(s) % col_tiles)),
                   pl.BlockSpec((high, lead_cols), lambda s: (after(s) // col_tiles, 0)),
                   pl.BlockSpec((lead_rows, wide), lambda s: (0, jnp.minimum(after(s), col_tiles - 1)))),
        scratch_shapes=[pltpu.VMEM((slots_held, parts, lanes), bf16), pltpu.VMEM((tile, parts, lanes), bf16)]
        + [pltpu.VMEM((RANK, rows + cols, width), bf16)] * 2 + [pltpu.SemaphoreType.DMA((len(sources),))],
        compiler_params=pltpu.CompilerParams(vmem_limit_bytes=58 * MIB),
        cost_estimate=pl.CostEstimate(flops=28 * 10**9, bytes_accessed=30 * MIB, transcendentals=0),
    )(slots, x_factor, z_factor, *sources)


def factor_block(block, u_ref, v_ref, beside):
    count = BLK // SUB
    sub_iota = lax.broadcasted_iota(jnp.int32, (SUB, BLK), 0)
    lane_iota = lax.broadcasted_iota(jnp.int32, (SUB, BLK), 1)
    rows_a = [block[SUB * i:SUB * (i + 1), :] for i in range(count)]
    rows_v = [(lane_iota == sub_iota + SUB * i).astype(jnp.float32) for i in range(count)]

    def spread_lane(x, lane):
        return jnp.broadcast_to(x[:, lane:lane + 1], (SUB, BLK))

    def spread_row(x, row):
        return jnp.broadcast_to(x[row:row + 1, :], (SUB, BLK))

    for m in range(count):
        beside(m)
        head_a, head_v = rows_a[m], rows_v[m]
        cols = [spread_lane(head_a, SUB * m + k) for k in range(SUB)]
        below = [[spread_lane(rows_a[i], SUB * m + k) for k in range(SUB)] for i in range(m + 1, count)]
        scale = jnp.zeros((SUB, BLK), jnp.float32)
        for j in range(SUB):
            pivot = spread_row(cols[j], j)
            root = lax.rsqrt(pivot)
            scale = jnp.where(sub_iota == j, root, scale)
            mult = jnp.where(sub_iota > j, cols[j] * root, 0.0)
            row_a = spread_row(head_a, j) * root
            row_v = spread_row(head_v, j) * root
            lead = [spread_row(cols[k], j) * root if k > j else None for k in range(SUB)]
            if j + 1 < SUB:
                head_a = head_a - mult * row_a
                head_v = head_v - mult * row_v
                for k in range(j + 1, SUB):
                    cols[k] = cols[k] - mult * lead[k]
            for n, i in enumerate(range(m + 1, count)):
                mult_i = below[n][j] * root
                rows_a[i] = rows_a[i] - mult_i * row_a
                rows_v[i] = rows_v[i] - mult_i * row_v
                for k in range(j + 1, SUB):
                    below[n][k] = below[n][k] - mult_i * lead[k]
        u = jnp.where(lane_iota >= sub_iota + SUB * m, head_a * scale, 0.0)
        v = jnp.where(lane_iota <= sub_iota + SUB * m, head_v * scale, 0.0)
        u_ref[SUB * m:SUB * (m + 1), :] = u
        v_ref[SUB * m:SUB * (m + 1), :] = v


def factor_kernel(yx_ref, yz_ref, l_ref, d_ref, w_ref, g_ref, u_ref, v_ref):
    order = l_ref.shape[0]
    steps = order // BLK
    tile = 2 * BLK
    window = 3 * BLK
    l_ref[...] = jnp.zeros_like(l_ref)
    w_ref[...] = jnp.zeros_like(w_ref)

    def rows_of(i, carry):
        left = pl.ds(pl.multiple_of(i * 2 * tile, 2 * tile), 2 * tile)
        w_ref[left, :tile] = gram_tile(yx_ref, yz_ref, left, pl.ds(0, tile))
        return carry
    lax.fori_loop(0, order // (2 * tile), rows_of, 0)

    def step(b, carry):
        at = pl.ds(pl.multiple_of(b * BLK, BLK), BLK)
        ahead = jnp.minimum(b // 2 + 1, order // tile - 1)
        left = pl.ds(pl.multiple_of(jnp.minimum(ahead * tile + (b % 2) * window, order - window), BLK), window)
        right = pl.ds(pl.multiple_of(ahead * tile, tile), tile)

        def beside(m):
            q, r = m // RANK, m % RANK
            term = dot_bf16(yx_ref[r, left, :], yx_ref[q, right, :], NT) * dot_bf16(yz_ref[r, left, :], yz_ref[q, right, :], NT)
            if m == 0:
                g_ref[left, :] = term
            elif rank_signs[q] * rank_signs[r] > 0:
                g_ref[left, :] = g_ref[left, :] + term
            else:
                g_ref[left, :] = g_ref[left, :] - term

        factor_block(w_ref[at, at], u_ref, v_ref, beside)
        l_ref[at, at] = u_ref[...].T
        d_ref[at, :] = v_ref[...]
        for k in range(steps - 1):
            @pl.when(b == k)
            def _():
                first = (k + 1) * BLK
                inv = split(v_ref[...])
                def panel(t, c):
                    rows = pl.ds(pl.multiple_of(first + t * BLK, BLK), BLK)
                    l_ref[rows, k * BLK:first] = dot3(split(w_ref[rows, k * BLK:first]), inv, NT)
                    return c
                lax.fori_loop(0, steps - 1 - k, panel, 0)
                right = split(l_ref[first:, k * BLK:first])
                def update(t, c):
                    rows = pl.ds(pl.multiple_of(first + t * BLK, BLK), BLK)
                    left = split(l_ref[rows, k * BLK:first])
                    w_ref[rows, first:] = w_ref[rows, first:] - dot3(left, right, NT)
                    return c
                lax.fori_loop(0, steps - 1 - k, update, 0)
                if k % 2 == 1:
                    w_ref[first:, first:first + tile] = w_ref[first:, first:first + tile] + g_ref[first:, :]
        return carry
    lax.fori_loop(0, steps, step, 0)


def factor(yx, yz):
    return pl.pallas_call(
        factor_kernel,
        out_shape=(jax.ShapeDtypeStruct((K, K), jnp.float32), jax.ShapeDtypeStruct((K, BLK), jnp.float32)),
        in_specs=[VMEM] * 2,
        out_specs=(VMEM, VMEM),
        scratch_shapes=[pltpu.VMEM((K, K), jnp.float32), pltpu.VMEM((K, 2 * BLK), jnp.float32), pltpu.VMEM((BLK, BLK), jnp.float32), pltpu.VMEM((BLK, BLK), jnp.float32)],
        compiler_params=pltpu.CompilerParams(vmem_limit_bytes=48 * MIB),
        cost_estimate=pl.CostEstimate(flops=40 * 10**9, bytes_accessed=12 * MIB, transcendentals=0),
    )(yx, yz)


def solve_kernel(place_ref, l_ref, d_ref, pieces_ref, tops_ref, schur_ref, rest_ref, panel_ref, lh, ll, xh, xl, zh, zl):
    pcol = pieces_ref.shape[0]
    prow = tops_ref.shape[0]
    row, column = place_ref[0], place_ref[1]
    lh[...], ll[...] = split(l_ref[...])
    wide = 2 * BLK
    for b in range(K // wide):
        at = slice(b * wide, (b + 1) * wide)
        upper, lower = slice(b * wide, b * wide + BLK), slice(b * wide + BLK, (b + 1) * wide)
        first, second = split(d_ref[upper, :]), split(d_ref[lower, :])
        between = dot3((lh[lower, upper], ll[lower, upper]), first, NN)
        corner = -dot3(second, split(between), NN)
        inverse = split(jnp.concatenate([
            jnp.concatenate([d_ref[upper, :], jnp.zeros((BLK, BLK), jnp.float32)], axis=1),
            jnp.concatenate([corner, d_ref[lower, :]], axis=1)], axis=0))
        blocks = range(wide // NB * b, wide // NB * (b + 1))
        value = jnp.concatenate([pieces_ref[n % pcol, :, n // pcol * NB:(n // pcol + 1) * NB] for n in blocks], axis=1)
        top = jnp.concatenate([tops_ref[(n % prow) ^ row, n // prow * NB:(n // prow + 1) * NB, :] for n in blocks], axis=0)
        if b > 0:
            done = slice(0, b * wide)
            left = (lh[at, done], ll[at, done])
            value = value - dot3((xh[:, done], xl[:, done]), left, NT)
            top = top - dot3(left, (zh[done, :], zl[done, :]), NN)
        value = dot3(split(value), inverse, NT)
        top = dot3(inverse, split(top), NN)
        xh[:, at], xl[:, at] = split(value)
        zh[at, :], zl[at, :] = split(top)
        for place, block in enumerate(blocks):
            @pl.when(column == block % pcol)
            def _():
                panel_ref[:, block // pcol * NB:(block // pcol + 1) * NB] = value[:, place * NB:(place + 1) * NB]
    rest_ref[...] = schur_ref[...] - dot3((xh[...], xl[...]), (zh[...], zl[...]), NN)


def solve(place, low, inverses, pieces, tops, schur):
    rows, cols = schur.shape
    lead = K // pieces.shape[0]
    bf16 = jnp.bfloat16
    return pl.pallas_call(
        solve_kernel,
        out_shape=(jax.ShapeDtypeStruct((rows, cols), jnp.float32), jax.ShapeDtypeStruct((rows, lead), jnp.float32)),
        in_specs=[SMEM] + [VMEM] * 5,
        out_specs=(VMEM, VMEM),
        scratch_shapes=[pltpu.VMEM((K, K), bf16)] * 2 + [pltpu.VMEM((rows, K), bf16)] * 2 + [pltpu.VMEM((K, cols), bf16)] * 2,
        compiler_params=pltpu.CompilerParams(vmem_limit_bytes=40 * MIB),
        cost_estimate=pl.CostEstimate(flops=12 * 10**9, bytes_accessed=24 * MIB, transcendentals=0),
    )(place, low, inverses, pieces, tops, schur)


def gather_factors(mine, prow_count, pcol_count):
    own = mine.shape[0]
    half = own // 2

    def swap(axis, count, turn, value):
        return lax.ppermute(value, axis, [(n, n ^ turn) for n in range(count)])

    items = {0: mine}
    for turn in range(1, prow_count, 2):
        items[turn] = swap("prow", prow_count, turn, mine)
    for turn in range(2, prow_count, 2):
        items[turn] = swap("prow", prow_count, 1, items[turn + 1])
    near, far, near_order, far_order = [], [], [], []
    groups = [[0]] + [[m] for m in range(1, prow_count, 2)] + [[m] for m in range(2, prow_count, 2)]
    for n, group in enumerate(groups):
        value = jnp.concatenate([items[m] for m in group]) if len(group) > 1 else items[group[0]]
        middle = len(group) * half
        held = {0: value}
        for j in range(1, pcol_count // 2):
            low = j & -j
            high = 1 << (j.bit_length() - 1)
            if low == high:
                held[j] = swap("pcol", pcol_count, 2 * j, value)
            else:
                held[j] = jnp.concatenate([swap("pcol", pcol_count, 2 * high, held[j ^ high][:middle]), swap("pcol", pcol_count, 2 * low, held[j ^ low][middle:])])
        direct = [j for j in held if j & (j - 1) == 0]
        relayed = [j for j in held if j & (j - 1) != 0]
        for part in [direct, relayed] if n == len(groups) - 1 else [direct + relayed]:
            whole = jnp.concatenate([held[j] for j in part]) if len(part) > 1 else held[part[0]]
            near.append(whole)
            near_order += [(m, 2 * j) for j in part for m in group]
            far.append(swap("pcol", pcol_count, 1, whole))
            far_order += [(m, 2 * j + 1) for j in part for m in group]
    return near + far, near_order + far_order


def places_of(placement, order, prow_id, pcol_id, pcol_count):
    total = placement.shape[0]
    own = total // len(order)
    unit_of = [0] * len(order)
    for unit, (row_turn, col_turn) in enumerate(order):
        unit_of[row_turn * pcol_count + col_turn] = unit
    holder = jnp.arange(len(order))
    turn = ((holder // pcol_count) ^ prow_id) * pcol_count + ((holder % pcol_count) ^ pcol_id)
    units = jnp.sum(jnp.where(turn[:, None] == jnp.arange(len(order))[None, :], jnp.array(unit_of)[None, :], 0), axis=1)
    place = (units[:, None] * own + jnp.arange(own)[None, :]).reshape(1, total)
    blocks = total // NB
    in_block = jnp.arange(blocks)[:, None] == placement[None, :] // NB
    digits = jnp.concatenate([jnp.where(in_block, place // NB, 0), jnp.where(in_block, place % NB, 0)]).astype(jnp.bfloat16)
    at_row = (jnp.arange(NB)[:, None] == placement[None, :] % NB).astype(jnp.bfloat16)
    found = dot_bf16(digits, at_row, NT).astype(jnp.int32)
    return found[:blocks] * NB + found[blocks:]


def per_device(factors, x_factor, zinv_factor, placement):
    prow_count = lax.axis_size("prow")
    pcol_count = lax.axis_size("pcol")
    total_rows = placement.shape[0]
    local_rows = total_rows // prow_count
    local_cols = total_rows // pcol_count
    prow_id = lax.axis_index("prow")
    pcol_id = lax.axis_index("pcol")
    _, own, width = factors.shape
    count = prow_count * pcol_count
    lanes = BLK
    mine = factors.transpose(1, 0, 2).reshape(own, RANK * width // lanes, lanes)
    sources, order = gather_factors(mine, prow_count, pcol_count)
    found = places_of(placement, order, prow_id, pcol_id, pcol_count)
    by_row = lax.dynamic_index_in_dim(found.reshape(local_rows // NB, prow_count, NB), prow_id, 1, keepdims=False)
    by_col = lax.dynamic_index_in_dim(found.reshape(local_cols // NB, pcol_count, NB), pcol_id, 1, keepdims=False)
    places = jnp.concatenate([found[:K // NB], by_row, by_col]).reshape(-1)
    lead_rows, lead_cols = K // prow_count, K // pcol_count
    lead_x, lead_z, schur_local, front, top = assemble(
        places.astype(jnp.int32), sources, x_factor, zinv_factor, local_rows, local_cols, lead_rows, lead_cols)
    pieces = lax.all_gather(front, "pcol", axis=0, tiled=False)
    turned = [lax.ppermute(top, "prow", [(n, n ^ turn) for n in range(prow_count)]) for turn in range(1, prow_count)]
    tops = jnp.stack([top] + turned)
    low, inverses = factor(lead_x, lead_z)
    return solve(jnp.stack([prow_id, pcol_id]).astype(jnp.int32), low, inverses, pieces, tops, schur_local)


def solution(mesh):
    in_specs = (P(None, ("prow", "pcol"), None), P(), P(), P())
    out_specs = (P("prow", "pcol"), P("prow", "pcol"))
    return jax.shard_map(
        per_device, mesh=mesh, in_specs=in_specs, out_specs=out_specs, check_vma=False
    )
```

```python
import functools

import jax
import jax.numpy as jnp
from jax import lax
from jax.experimental import pallas as pl
from jax.experimental.pallas import tpu as pltpu
from jax.sharding import PartitionSpec as P

RANK = 4
NB = 64
K = 1024
SUB = 8
BLK = 128
MIB = 2**20

rank_signs = (1.0, 1.0, -1.0, -1.0)
NT = ((1,), (1,))
NN = ((1,), (0,))
VMEM = pl.BlockSpec(memory_space=pltpu.VMEM)
SMEM = pl.BlockSpec(memory_space=pltpu.SMEM)


def split(x):
    hi = x.astype(jnp.bfloat16)
    lo = (x - hi.astype(jnp.float32)).astype(jnp.bfloat16)
    return hi, lo


def dot_bf16(a, b, dims):
    return lax.dot_general(a, b, (dims, ((), ())), preferred_element_type=jnp.float32)


def dot3(a, b, dims):
    return dot_bf16(a[0], b[0], dims) + (dot_bf16(a[0], b[1], dims) + dot_bf16(a[1], b[0], dims))


def assemble_kernel(slots_ref, x_ref, z_ref, *refs, sources, lead_tiles, pick_tiles, col_tiles, rows):
    source_refs, refs = refs[:sources], refs[sources:]
    lead_x_ref, lead_z_ref, schur_ref, front_ref, top_ref, every_ref, picked_ref, yx_ref, yz_ref, gx_ref, gz_ref, sem_ref = refs
    step = pl.program_id(0)
    tile, parts, lanes = picked_ref.shape
    width = x_ref.shape[0]
    per_rank = width // lanes

    @pl.when(step == 0)
    def _():
        copies, first = [], 0
        for n, ref in enumerate(source_refs):
            copies.append(pltpu.make_async_copy(ref, every_ref.at[pl.ds(first, ref.shape[0])], sem_ref.at[n]))
            first += ref.shape[0]
        for copy in copies:
            copy.start()
        for copy in copies:
            copy.wait()

    @pl.when(step < pick_tiles)
    def _():
        def pick(group, carry):
            for k in range(16):
                i = group * 16 + k
                picked_ref[i] = every_ref[slots_ref[step * tile + i]]
            return carry
        lax.fori_loop(0, tile // 16, pick, 0)
        by_part = jnp.swapaxes(picked_ref[...], 0, 1)
        mine = jnp.concatenate([
            jnp.concatenate([by_part[r * per_rank + k] for k in range(per_rank)], axis=1) for r in range(RANK)], axis=0)
        images_x = dot_bf16(mine, x_ref[...], NN).astype(jnp.bfloat16).reshape(RANK, tile, width)
        images_z = dot_bf16(mine, z_ref[...], NN).astype(jnp.bfloat16).reshape(RANK, tile, width)

        @pl.when(step < lead_tiles)
        def _():
            lead_x_ref[...], lead_z_ref[...] = images_x, images_z

        @pl.when(step >= lead_tiles)
        def _():
            at = pl.ds(pl.multiple_of((step - lead_tiles) * tile, tile), tile)
            yx_ref[:, at, :], yz_ref[:, at, :] = images_x, images_z

    @pl.when(step >= pick_tiles)
    def _():
        high, wide = schur_ref.shape
        i, j = (step - pick_tiles) // col_tiles, (step - pick_tiles) % col_tiles
        left = pl.ds(pl.multiple_of(i * high, high), high)
        right = pl.ds(pl.multiple_of(rows + j * wide, wide), wide)
        gram_tile(yx_ref, yz_ref, left, right, schur_ref, gx_ref, gz_ref)

        @pl.when(j == 0)
        def _():
            front_ref[...] = schur_ref[:, :front_ref.shape[1]]

        @pl.when(i == 0)
        def _():
            top_ref[...] = schur_ref[:top_ref.shape[0], :]


CHUNK = 32


def gram_tile(yx_ref, yz_ref, left, right, out_ref, gx_ref, gz_ref):
    left_x, left_z = yx_ref[:, left, :], yz_ref[:, left, :]
    _, high, width = left_x.shape
    left_x, left_z = left_x.reshape(RANK * high, width), left_z.reshape(RANK * high, width)

    def products(q):
        gx_ref[q % 2] = dot_bf16(left_x, yx_ref[q, right, :], NT)
        gz_ref[q % 2] = dot_bf16(left_z, yz_ref[q, right, :], NT)

    products(0)
    for q in range(RANK):
        if q + 1 < RANK:
            products(q + 1)
        for first in range(0, high, CHUNK):
            total = out_ref[first:first + CHUNK, :] if q > 0 else None
            for r in range(RANK):
                at = slice(r * high + first, r * high + first + CHUNK)
                total = signed(total, gx_ref[q % 2, at, :] * gz_ref[q % 2, at, :], q, r)
            out_ref[first:first + CHUNK, :] = total


def signed(total, term, q, r):
    if total is None:
        return term
    return total + term if rank_signs[q] * rank_signs[r] > 0 else total - term


def assemble(slots, sources, x_factor, z_factor, rows, cols, lead_rows, lead_cols):
    _, parts, lanes = sources[0].shape
    slots_held = sum(source.shape[0] for source in sources)
    width = x_factor.shape[0]
    tile = 256
    high, wide = min(512, rows), min(256, cols)
    lead_tiles, pick_tiles = K // tile, slots.shape[0] // tile
    row_tiles, col_tiles = rows // high, cols // wide
    whole = pl.BlockSpec((width, width), lambda s: (0, 0), pipeline_mode=pl.Buffered(1))
    lead = pl.BlockSpec((RANK, tile, width), lambda s: (0, jnp.minimum(s, lead_tiles - 1), 0))
    after = lambda s: jnp.maximum(s - pick_tiles, 0)
    bf16 = jnp.bfloat16
    any_space = pl.BlockSpec(memory_space=pl.ANY)
    body = functools.partial(assemble_kernel, sources=len(sources), lead_tiles=lead_tiles, pick_tiles=pick_tiles, col_tiles=col_tiles, rows=rows)
    return pl.pallas_call(
        body,
        grid=(pick_tiles + row_tiles * col_tiles,),
        out_shape=(jax.ShapeDtypeStruct((RANK, K, width), bf16),) * 2 + (
            jax.ShapeDtypeStruct((rows, cols), jnp.float32),
            jax.ShapeDtypeStruct((rows, lead_cols), jnp.float32),
            jax.ShapeDtypeStruct((lead_rows, cols), jnp.float32)),
        in_specs=[SMEM, whole, whole] + [any_space] * len(sources),
        out_specs=(lead, lead,
                   pl.BlockSpec((high, wide), lambda s: (after(s) // col_tiles, after(s) % col_tiles)),
                   pl.BlockSpec((high, lead_cols), lambda s: (after(s) // col_tiles, 0)),
                   pl.BlockSpec((lead_rows, wide), lambda s: (0, jnp.minimum(after(s), col_tiles - 1)))),
        scratch_shapes=[pltpu.VMEM((slots_held, parts, lanes), bf16), pltpu.VMEM((tile, parts, lanes), bf16)]
        + [pltpu.VMEM((RANK, rows + cols, width), bf16)] * 2 + [pltpu.VMEM((2, RANK * high, wide), jnp.float32)] * 2 + [pltpu.SemaphoreType.DMA((len(sources),))],
        compiler_params=pltpu.CompilerParams(vmem_limit_bytes=58 * MIB),
        cost_estimate=pl.CostEstimate(flops=28 * 10**9, bytes_accessed=30 * MIB, transcendentals=0),
    )(slots, x_factor, z_factor, *sources)


def factor_block(block, u_ref, v_ref, beside):
    count = BLK // SUB
    sub_iota = lax.broadcasted_iota(jnp.int32, (SUB, BLK), 0)
    lane_iota = lax.broadcasted_iota(jnp.int32, (SUB, BLK), 1)
    rows_a = [block[SUB * i:SUB * (i + 1), :] for i in range(count)]
    rows_v = [(lane_iota == sub_iota + SUB * i).astype(jnp.float32) for i in range(count)]

    def spread_lane(x, lane):
        return jnp.broadcast_to(x[:, lane:lane + 1], (SUB, BLK))

    def spread_row(x, row):
        return jnp.broadcast_to(x[row:row + 1, :], (SUB, BLK))

    cols = [spread_lane(rows_a[0], k) for k in range(SUB)]
    for m in range(count):
        beside(m)
        head_a, head_v = rows_a[m], rows_v[m]
        below = [[spread_lane(rows_a[i], SUB * m + k) for k in range(SUB)] for i in range(m + 1, count)]
        ahead, coming = [], []
        if m + 1 < count:
            ahead = [spread_lane(head_a, SUB * (m + 1) + k) for k in range(SUB)]
            coming = [spread_lane(rows_a[m + 1], SUB * (m + 1) + k) for k in range(SUB)]
        scale = jnp.zeros((SUB, BLK), jnp.float32)
        for j in range(SUB):
            pivot = spread_row(cols[j], j)
            root = lax.rsqrt(pivot)
            scale = jnp.where(sub_iota == j, root, scale)
            mult = jnp.where(sub_iota > j, cols[j] * root, 0.0)
            lead = [spread_row(cols[k], j) * root if k > j else None for k in range(SUB)]
            row_a = spread_row(head_a, j) * root
            row_v = spread_row(head_v, j) * root
            row_ahead = [spread_row(value, j) * root for value in ahead]
            if j + 1 < SUB:
                for k in range(j + 1, SUB):
                    cols[k] = cols[k] - mult * lead[k]
                head_a = head_a - mult * row_a
                head_v = head_v - mult * row_v
                ahead = [value - mult * row for value, row in zip(ahead, row_ahead)]
            for n, i in enumerate(range(m + 1, count)):
                mult_i = below[n][j] * root
                for k in range(j + 1, SUB):
                    below[n][k] = below[n][k] - mult_i * lead[k]
                if n == 0:
                    coming = [value - mult_i * row for value, row in zip(coming, row_ahead)]
                rows_a[i] = rows_a[i] - mult_i * row_a
                rows_v[i] = rows_v[i] - mult_i * row_v
        u_ref[SUB * m:SUB * (m + 1), :] = jnp.where(lane_iota >= sub_iota + SUB * m, head_a * scale, 0.0)
        v_ref[SUB * m:SUB * (m + 1), :] = jnp.where(lane_iota <= sub_iota + SUB * m, head_v * scale, 0.0)
        cols = coming


def factor_kernel(yx_ref, yz_ref, lh_ref, ll_ref, d_ref, w_ref, g_ref, u_ref, v_ref, gx_ref, gz_ref, px_ref, pz_ref):
    order = lh_ref.shape[0]
    steps = order // BLK
    tile = 2 * BLK
    window = 3 * BLK
    lh_ref[...] = jnp.zeros_like(lh_ref)
    ll_ref[...] = jnp.zeros_like(ll_ref)
    w_ref[:, tile:] = jnp.zeros((order, order - tile), jnp.float32)

    def rows_of(i, carry):
        left = pl.ds(pl.multiple_of(i * tile, tile), tile)
        gram_tile(yx_ref, yz_ref, left, pl.ds(0, tile), w_ref.at[left, pl.ds(0, tile)], gx_ref, gz_ref)
        return carry
    lax.fori_loop(0, order // tile, rows_of, 0)

    def step(b, carry):
        at = pl.ds(pl.multiple_of(b * BLK, BLK), BLK)
        after = jnp.minimum(b // 2 + 1, order // tile - 1)
        top = pl.multiple_of(jnp.minimum(after * tile + (b % 2) * window, order - window), BLK)
        left = pl.ds(top, window)
        right = pl.ds(pl.multiple_of(after * tile, tile), tile)
        pairs = RANK * RANK

        def products(m):
            q, r = m // RANK, m % RANK
            px_ref[m % 2] = dot_bf16(yx_ref[r, left, :], yx_ref[q, right, :], NT)
            pz_ref[m % 2] = dot_bf16(yz_ref[r, left, :], yz_ref[q, right, :], NT)

        def add_up(m):
            for first in range(0, window, CHUNK):
                rows = pl.ds(pl.multiple_of(top + first, CHUNK), CHUNK)
                total = g_ref[rows, :] if m > 0 else None
                g_ref[rows, :] = signed(total, px_ref[m % 2, first:first + CHUNK, :] * pz_ref[m % 2, first:first + CHUNK, :], m // RANK, m % RANK)

        def beside(m):
            if m < pairs:
                products(m)
            if 0 < m <= pairs:
                add_up(m - 1)

        factor_block(w_ref[at, at], u_ref, v_ref, beside)
        add_up(pairs - 1)
        lh_ref[at, at], ll_ref[at, at] = split(u_ref[...].T)
        d_ref[at, :] = v_ref[...]
        for k in range(steps - 1):
            @pl.when(b == k)
            def _():
                first = (k + 1) * BLK
                inv = split(v_ref[...])

                def panel(t, c):
                    rows = pl.ds(pl.multiple_of(first + t * BLK, BLK), BLK)
                    lh_ref[rows, k * BLK:first], ll_ref[rows, k * BLK:first] = split(dot3(split(w_ref[rows, k * BLK:first]), inv, NT))
                    return c
                lax.fori_loop(0, steps - 1 - k, panel, 0)
                right = (lh_ref[first:, k * BLK:first], ll_ref[first:, k * BLK:first])

                def update(t, c):
                    rows = pl.ds(pl.multiple_of(first + t * BLK, BLK), BLK)
                    left = (lh_ref[rows, k * BLK:first], ll_ref[rows, k * BLK:first])
                    w_ref[rows, first:] = w_ref[rows, first:] - dot3(left, right, NT)
                    return c
                lax.fori_loop(0, steps - 1 - k, update, 0)
                if k % 2 == 1:
                    w_ref[first:, first:first + tile] = w_ref[first:, first:first + tile] + g_ref[first:, :]
        return carry
    lax.fori_loop(0, steps, step, 0)


def factor(yx, yz):
    tile, window = 2 * BLK, 3 * BLK
    f32 = jnp.float32
    return pl.pallas_call(
        factor_kernel,
        out_shape=(jax.ShapeDtypeStruct((K, K), jnp.bfloat16),) * 2 + (jax.ShapeDtypeStruct((K, BLK), f32),),
        in_specs=[VMEM] * 2,
        out_specs=(VMEM,) * 3,
        scratch_shapes=[pltpu.VMEM((K, K), f32), pltpu.VMEM((K, tile), f32), pltpu.VMEM((BLK, BLK), f32), pltpu.VMEM((BLK, BLK), f32)]
        + [pltpu.VMEM((2, RANK * tile, tile), f32)] * 2 + [pltpu.VMEM((2, window, tile), f32)] * 2,
        compiler_params=pltpu.CompilerParams(vmem_limit_bytes=48 * MIB),
        cost_estimate=pl.CostEstimate(flops=40 * 10**9, bytes_accessed=12 * MIB, transcendentals=0),
    )(yx, yz)


def solve_kernel(place_ref, lh, ll, d_ref, pieces_any, schur_any, *refs, prow):
    top_refs, refs = refs[:prow], refs[prow:]
    rest_ref, panel_ref, pieces_ref, tops_ref, schur_ref, xh, xl, zh, zl, sem_ref = refs
    pcol = pieces_ref.shape[0]
    row, column = place_ref[0], place_ref[1]
    tops = [pltpu.make_async_copy(ref, tops_ref.at[turn ^ row], sem_ref.at[turn]) for turn, ref in enumerate(top_refs)]
    pieces = pltpu.make_async_copy(pieces_any, pieces_ref, sem_ref.at[prow])
    schur = pltpu.make_async_copy(schur_any, schur_ref, sem_ref.at[prow + 1])
    for copy in tops:
        copy.start()
    pieces.start()
    schur.start()
    wide = 2 * BLK
    inverses = []
    for b in range(K // wide):
        upper, lower = slice(b * wide, b * wide + BLK), slice(b * wide + BLK, (b + 1) * wide)
        first, second = split(d_ref[upper, :]), split(d_ref[lower, :])
        between = dot3((lh[lower, upper], ll[lower, upper]), first, NN)
        corner = -dot3(second, split(between), NN)
        inverses.append(split(jnp.concatenate([
            jnp.concatenate([d_ref[upper, :], jnp.zeros((BLK, BLK), jnp.float32)], axis=1),
            jnp.concatenate([corner, d_ref[lower, :]], axis=1)], axis=0)))
    for copy in tops:
        copy.wait()
    for b in range(K // wide):
        at, done = slice(b * wide, (b + 1) * wide), slice(0, b * wide)
        blocks = range(wide // NB * b, wide // NB * (b + 1))
        top = jnp.concatenate([tops_ref[n % prow, n // prow * NB:(n // prow + 1) * NB, :] for n in blocks], axis=0)
        if b > 0:
            top = top - dot3((lh[at, done], ll[at, done]), (zh[done, :], zl[done, :]), NN)
        zh[at, :], zl[at, :] = split(dot3(inverses[b], split(top), NN))
    pieces.wait()
    for b in range(K // wide):
        at, done = slice(b * wide, (b + 1) * wide), slice(0, b * wide)
        blocks = range(wide // NB * b, wide // NB * (b + 1))
        value = jnp.concatenate([pieces_ref[n % pcol, :, n // pcol * NB:(n // pcol + 1) * NB] for n in blocks], axis=1)
        if b > 0:
            value = value - dot3((xh[:, done], xl[:, done]), (lh[at, done], ll[at, done]), NT)
        value = dot3(split(value), inverses[b], NT)
        xh[:, at], xl[:, at] = split(value)
        for place, block in enumerate(blocks):
            @pl.when(column == block % pcol)
            def _():
                panel_ref[:, block // pcol * NB:(block // pcol + 1) * NB] = value[:, place * NB:(place + 1) * NB]
    schur.wait()
    rest_ref[...] = schur_ref[...] - dot3((xh[...], xl[...]), (zh[...], zl[...]), NN)


def solve(place, high, low, inverses, pieces, schur, tops):
    rows, cols = schur.shape
    lead = K // pieces.shape[0]
    bf16, f32 = jnp.bfloat16, jnp.float32
    any_space = pl.BlockSpec(memory_space=pl.ANY)
    return pl.pallas_call(
        functools.partial(solve_kernel, prow=len(tops)),
        out_shape=(jax.ShapeDtypeStruct((rows, cols), f32), jax.ShapeDtypeStruct((rows, lead), f32)),
        in_specs=[SMEM] + [VMEM] * 3 + [any_space] * (2 + len(tops)),
        out_specs=(VMEM, VMEM),
        scratch_shapes=[pltpu.VMEM(pieces.shape, f32), pltpu.VMEM((len(tops),) + tops[0].shape, f32), pltpu.VMEM(schur.shape, f32)]
        + [pltpu.VMEM((rows, K), bf16)] * 2 + [pltpu.VMEM((K, cols), bf16)] * 2 + [pltpu.SemaphoreType.DMA((len(tops) + 2,))],
        compiler_params=pltpu.CompilerParams(vmem_limit_bytes=44 * MIB),
        cost_estimate=pl.CostEstimate(flops=12 * 10**9, bytes_accessed=24 * MIB, transcendentals=0),
    )(place, high, low, inverses, pieces, schur, *tops)


def gather_factors(mine, prow_count, pcol_count):
    own = mine.shape[0]
    half = own // 2

    def swap(axis, count, turn, value):
        return lax.ppermute(value, axis, [(n, n ^ turn) for n in range(count)])

    items = {0: mine}
    for turn in range(1, prow_count, 2):
        items[turn] = swap("prow", prow_count, turn, mine)
    for turn in range(2, prow_count, 2):
        items[turn] = swap("prow", prow_count, 1, items[turn + 1])
    near, far, near_order, far_order = [], [], [], []
    groups = [[0]] + [[m] for m in range(1, prow_count, 2)] + [[m] for m in range(2, prow_count, 2)]
    for n, group in enumerate(groups):
        value = jnp.concatenate([items[m] for m in group]) if len(group) > 1 else items[group[0]]
        middle = len(group) * half
        held = {0: value}
        for j in range(1, pcol_count // 2):
            low = j & -j
            high = 1 << (j.bit_length() - 1)
            if low == high:
                held[j] = swap("pcol", pcol_count, 2 * j, value)
            else:
                held[j] = jnp.concatenate([swap("pcol", pcol_count, 2 * high, held[j ^ high][:middle]), swap("pcol", pcol_count, 2 * low, held[j ^ low][middle:])])
        direct = [j for j in held if j & (j - 1) == 0]
        relayed = [j for j in held if j & (j - 1) != 0]
        for part in [direct, relayed] if n == len(groups) - 1 else [direct + relayed]:
            whole = jnp.concatenate([held[j] for j in part]) if len(part) > 1 else held[part[0]]
            near.append(whole)
            near_order += [(m, 2 * j) for j in part for m in group]
            far.append(swap("pcol", pcol_count, 1, whole))
            far_order += [(m, 2 * j + 1) for j in part for m in group]
    return near + far, near_order + far_order


def places_of(placement, order, prow_id, pcol_id, pcol_count):
    total = placement.shape[0]
    own = total // len(order)
    unit_of = [0] * len(order)
    for unit, (row_turn, col_turn) in enumerate(order):
        unit_of[row_turn * pcol_count + col_turn] = unit
    holder = jnp.arange(len(order))
    turn = ((holder // pcol_count) ^ prow_id) * pcol_count + ((holder % pcol_count) ^ pcol_id)
    units = jnp.sum(jnp.where(turn[:, None] == jnp.arange(len(order))[None, :], jnp.array(unit_of)[None, :], 0), axis=1)
    place = (units[:, None] * own + jnp.arange(own)[None, :]).reshape(1, total)
    blocks = total // NB
    in_block = jnp.arange(blocks)[:, None] == placement[None, :] // NB
    digits = jnp.concatenate([jnp.where(in_block, place // NB, 0), jnp.where(in_block, place % NB, 0)]).astype(jnp.bfloat16)
    at_row = (jnp.arange(NB)[:, None] == placement[None, :] % NB).astype(jnp.bfloat16)
    found = dot_bf16(digits, at_row, NT).astype(jnp.int32)
    return found[:blocks] * NB + found[blocks:]


def per_device(factors, x_factor, zinv_factor, placement):
    prow_count = lax.axis_size("prow")
    pcol_count = lax.axis_size("pcol")
    total_rows = placement.shape[0]
    local_rows = total_rows // prow_count
    local_cols = total_rows // pcol_count
    prow_id = lax.axis_index("prow")
    pcol_id = lax.axis_index("pcol")
    _, own, width = factors.shape
    count = prow_count * pcol_count
    lanes = BLK
    mine = factors.transpose(1, 0, 2).reshape(own, RANK * width // lanes, lanes)
    sources, order = gather_factors(mine, prow_count, pcol_count)
    found = places_of(placement, order, prow_id, pcol_id, pcol_count)
    by_row = lax.dynamic_index_in_dim(found.reshape(local_rows // NB, prow_count, NB), prow_id, 1, keepdims=False)
    by_col = lax.dynamic_index_in_dim(found.reshape(local_cols // NB, pcol_count, NB), pcol_id, 1, keepdims=False)
    places = jnp.concatenate([found[:K // NB], by_row, by_col]).reshape(-1)
    lead_rows, lead_cols = K // prow_count, K // pcol_count
    lead_x, lead_z, schur_local, front, top = assemble(
        places.astype(jnp.int32), sources, x_factor, zinv_factor, local_rows, local_cols, lead_rows, lead_cols)
    pieces = lax.all_gather(front, "pcol", axis=0, tiled=False)
    tops = [top] + [lax.ppermute(top, "prow", [(n, n ^ turn) for n in range(prow_count)]) for turn in range(1, prow_count)]
    high, low, inverses = factor(lead_x, lead_z)
    return solve(jnp.stack([prow_id, pcol_id]).astype(jnp.int32), high, low, inverses, pieces, schur_local, tops)


def solution(mesh):
    in_specs = (P(None, ("prow", "pcol"), None), P(), P(), P())
    out_specs = (P("prow", "pcol"), P("prow", "pcol"))
    return jax.shard_map(
        per_device, mesh=mesh, in_specs=in_specs, out_specs=out_specs, check_vma=False
    )
```

```python
import functools

import jax
import jax.numpy as jnp
from jax import lax
from jax.experimental import pallas as pl
from jax.experimental.pallas import tpu as pltpu
from jax.sharding import PartitionSpec as P

RANK = 4
NB = 64
K = 1024
SUB = 8
BLK = 128
MIB = 2**20

rank_signs = (1.0, 1.0, -1.0, -1.0)
NT = ((1,), (1,))
NN = ((1,), (0,))
TN = ((0,), (0,))
VMEM = pl.BlockSpec(memory_space=pltpu.VMEM)
SMEM = pl.BlockSpec(memory_space=pltpu.SMEM)


def split(x):
    hi = x.astype(jnp.bfloat16)
    lo = (x - hi.astype(jnp.float32)).astype(jnp.bfloat16)
    return hi, lo


def dot_bf16(a, b, dims):
    return lax.dot_general(a, b, (dims, ((), ())), preferred_element_type=jnp.float32)


def dot3(a, b, dims):
    return dot_bf16(a[0], b[0], dims) + (dot_bf16(a[0], b[1], dims) + dot_bf16(a[1], b[0], dims))


def assemble_kernel(slots_ref, x_ref, z_ref, *refs, sources, lead_tiles, pick_tiles, col_tiles, rows):
    source_refs, refs = refs[:sources], refs[sources:]
    lead_x_ref, lead_z_ref, schur_ref, front_ref, top_ref, every_ref, picked_ref, yx_ref, yz_ref, gx_ref, gz_ref, sem_ref = refs
    step = pl.program_id(0)
    tile, parts, lanes = picked_ref.shape
    width = x_ref.shape[0]
    per_rank = width // lanes

    @pl.when(step == 0)
    def _():
        copies, first = [], 0
        for n, ref in enumerate(source_refs):
            copies.append(pltpu.make_async_copy(ref, every_ref.at[pl.ds(first, ref.shape[0])], sem_ref.at[n]))
            first += ref.shape[0]
        for copy in copies:
            copy.start()
        for copy in copies:
            copy.wait()

    @pl.when(step < pick_tiles)
    def _():
        def pick(group, carry):
            for k in range(16):
                i = group * 16 + k
                picked_ref[i] = every_ref[slots_ref[step * tile + i]]
            return carry
        lax.fori_loop(0, tile // 16, pick, 0)
        by_part = jnp.swapaxes(picked_ref[...], 0, 1)
        mine = jnp.concatenate([
            jnp.concatenate([by_part[r * per_rank + k] for k in range(per_rank)], axis=1) for r in range(RANK)], axis=0)
        images_x = dot_bf16(mine, x_ref[...], NN).astype(jnp.bfloat16).reshape(RANK, tile, width)
        images_z = dot_bf16(mine, z_ref[...], NN).astype(jnp.bfloat16).reshape(RANK, tile, width)

        @pl.when(step < lead_tiles)
        def _():
            lead_x_ref[...], lead_z_ref[...] = images_x, images_z

        @pl.when(step >= lead_tiles)
        def _():
            at = pl.ds(pl.multiple_of((step - lead_tiles) * tile, tile), tile)
            yx_ref[:, at, :], yz_ref[:, at, :] = images_x, images_z

    @pl.when(step >= pick_tiles)
    def _():
        high, wide = schur_ref.shape
        i, j = (step - pick_tiles) // col_tiles, (step - pick_tiles) % col_tiles
        left = pl.ds(pl.multiple_of(i * high, high), high)
        right = pl.ds(pl.multiple_of(rows + j * wide, wide), wide)
        gram_tile(yx_ref, yz_ref, left, right, schur_ref, gx_ref, gz_ref)

        @pl.when(j == 0)
        def _():
            front_ref[...] = schur_ref[:, :front_ref.shape[1]]

        @pl.when(i == 0)
        def _():
            top_ref[...] = schur_ref[:top_ref.shape[0], :]


CHUNK = 32


def gram_tile(yx_ref, yz_ref, left, right, out_ref, gx_ref, gz_ref):
    left_x, left_z = yx_ref[:, left, :], yz_ref[:, left, :]
    _, high, width = left_x.shape
    left_x, left_z = left_x.reshape(RANK * high, width), left_z.reshape(RANK * high, width)

    def products(q):
        gx_ref[q % 2] = dot_bf16(left_x, yx_ref[q, right, :], NT)
        gz_ref[q % 2] = dot_bf16(left_z, yz_ref[q, right, :], NT)

    products(0)
    for q in range(RANK):
        if q + 1 < RANK:
            products(q + 1)
        for first in range(0, high, CHUNK):
            total = out_ref[first:first + CHUNK, :] if q > 0 else None
            for r in range(RANK):
                at = slice(r * high + first, r * high + first + CHUNK)
                total = signed(total, gx_ref[q % 2, at, :] * gz_ref[q % 2, at, :], q, r)
            out_ref[first:first + CHUNK, :] = total


def signed(total, term, q, r):
    if total is None:
        return term
    return total + term if rank_signs[q] * rank_signs[r] > 0 else total - term


def assemble(slots, sources, x_factor, z_factor, rows, cols, lead_rows, lead_cols):
    _, parts, lanes = sources[0].shape
    slots_held = sum(source.shape[0] for source in sources)
    width = x_factor.shape[0]
    tile = 256
    high, wide = min(512, rows), min(256, cols)
    lead_tiles, pick_tiles = K // tile, slots.shape[0] // tile
    row_tiles, col_tiles = rows // high, cols // wide
    whole = pl.BlockSpec((width, width), lambda s: (0, 0), pipeline_mode=pl.Buffered(1))
    lead = pl.BlockSpec((RANK, tile, width), lambda s: (0, jnp.minimum(s, lead_tiles - 1), 0))
    after = lambda s: jnp.maximum(s - pick_tiles, 0)
    bf16 = jnp.bfloat16
    any_space = pl.BlockSpec(memory_space=pl.ANY)
    body = functools.partial(assemble_kernel, sources=len(sources), lead_tiles=lead_tiles, pick_tiles=pick_tiles, col_tiles=col_tiles, rows=rows)
    return pl.pallas_call(
        body,
        grid=(pick_tiles + row_tiles * col_tiles,),
        out_shape=(jax.ShapeDtypeStruct((RANK, K, width), bf16),) * 2 + (
            jax.ShapeDtypeStruct((rows, cols), jnp.float32),
            jax.ShapeDtypeStruct((rows, lead_cols), jnp.float32),
            jax.ShapeDtypeStruct((lead_rows, cols), jnp.float32)),
        in_specs=[SMEM, whole, whole] + [any_space] * len(sources),
        out_specs=(lead, lead,
                   pl.BlockSpec((high, wide), lambda s: (after(s) // col_tiles, after(s) % col_tiles)),
                   pl.BlockSpec((high, lead_cols), lambda s: (after(s) // col_tiles, 0)),
                   pl.BlockSpec((lead_rows, wide), lambda s: (0, jnp.minimum(after(s), col_tiles - 1)))),
        scratch_shapes=[pltpu.VMEM((slots_held, parts, lanes), bf16), pltpu.VMEM((tile, parts, lanes), bf16)]
        + [pltpu.VMEM((RANK, rows + cols, width), bf16)] * 2 + [pltpu.VMEM((2, RANK * high, wide), jnp.float32)] * 2 + [pltpu.SemaphoreType.DMA((len(sources),))],
        compiler_params=pltpu.CompilerParams(vmem_limit_bytes=58 * MIB),
        cost_estimate=pl.CostEstimate(flops=28 * 10**9, bytes_accessed=30 * MIB, transcendentals=0),
    )(slots, x_factor, z_factor, *sources)


def factor_block(block, u_ref, v_ref, beside):
    count = BLK // SUB
    sub_iota = lax.broadcasted_iota(jnp.int32, (SUB, BLK), 0)
    lane_iota = lax.broadcasted_iota(jnp.int32, (SUB, BLK), 1)
    rows_a = [block[SUB * i:SUB * (i + 1), :] for i in range(count)]
    rows_v = [(lane_iota == sub_iota + SUB * i).astype(jnp.float32) for i in range(count)]

    def spread_lane(x, lane):
        return jnp.broadcast_to(x[:, lane:lane + 1], (SUB, BLK))

    def spread_row(x, row):
        return jnp.broadcast_to(x[row:row + 1, :], (SUB, BLK))

    cols = [spread_lane(rows_a[0], k) for k in range(SUB)]
    for m in range(count):
        beside(m)
        head_a, head_v = rows_a[m], rows_v[m]
        more = m + 1 < count
        below, ahead, coming = [], [], []
        if more:
            next_a, next_v = rows_a[m + 1], rows_v[m + 1]
            below = [spread_lane(next_a, SUB * m + k) for k in range(SUB)]
            ahead = [spread_lane(head_a, SUB * (m + 1) + k) for k in range(SUB)]
            coming = [spread_lane(next_a, SUB * (m + 1) + k) for k in range(SUB)]
        scale = jnp.zeros((SUB, BLK), jnp.float32)
        for j in range(SUB):
            pivot = spread_row(cols[j], j)
            root = lax.rsqrt(pivot)
            scale = jnp.where(sub_iota == j, root, scale)
            mult = jnp.where(sub_iota > j, cols[j] * root, 0.0)
            lead = [spread_row(cols[k], j) * root if k > j else None for k in range(SUB)]
            row_a = spread_row(head_a, j) * root
            row_v = spread_row(head_v, j) * root
            row_ahead = [spread_row(value, j) * root for value in ahead]
            if j + 1 < SUB:
                for k in range(j + 1, SUB):
                    cols[k] = cols[k] - mult * lead[k]
                head_a = head_a - mult * row_a
                head_v = head_v - mult * row_v
                ahead = [value - mult * row for value, row in zip(ahead, row_ahead)]
            if more:
                mult_next = below[j] * root
                for k in range(j + 1, SUB):
                    below[k] = below[k] - mult_next * lead[k]
                coming = [value - mult_next * row for value, row in zip(coming, row_ahead)]
                next_a = next_a - mult_next * row_a
                next_v = next_v - mult_next * row_v
        u = jnp.where(lane_iota >= sub_iota + SUB * m, head_a * scale, 0.0)
        v = jnp.where(lane_iota <= sub_iota + SUB * m, head_v * scale, 0.0)
        u_ref[SUB * m:SUB * (m + 1), :] = u
        v_ref[SUB * m:SUB * (m + 1), :] = v
        if more:
            rows_a[m + 1], rows_v[m + 1] = next_a, next_v
        if m + 2 < count:
            both = jnp.concatenate([u, v], axis=1)
            u_hi, both_hi = u.astype(jnp.bfloat16).astype(jnp.float32), both.astype(jnp.bfloat16).astype(jnp.float32)
            u_lo, both_lo = u - u_hi, both - both_hi
            left = jnp.concatenate([u_hi, u_hi, u_lo, u_lo], axis=0).astype(jnp.bfloat16)
            right = jnp.concatenate([both_hi, both_lo, both_hi, both_lo], axis=0).astype(jnp.bfloat16)
            change = dot_bf16(left, right, TN)
            for i in range(m + 2, count):
                at = slice(SUB * i, SUB * (i + 1))
                rows_a[i] = rows_a[i] - change[at, :BLK]
                rows_v[i] = rows_v[i] - change[at, BLK:]
        cols = coming


def factor_kernel(yx_ref, yz_ref, lh_ref, ll_ref, d_ref, w_ref, g_ref, u_ref, v_ref, gx_ref, gz_ref):
    order = lh_ref.shape[0]
    steps = order // BLK
    tile = 2 * BLK
    window = 3 * BLK
    lh_ref[...] = jnp.zeros_like(lh_ref)
    ll_ref[...] = jnp.zeros_like(ll_ref)
    w_ref[:, tile:] = jnp.zeros((order, order - tile), jnp.float32)

    def rows_of(i, carry):
        left = pl.ds(pl.multiple_of(i * tile, tile), tile)
        gram_tile(yx_ref, yz_ref, left, pl.ds(0, tile), w_ref.at[left, pl.ds(0, tile)], gx_ref, gz_ref)
        return carry
    lax.fori_loop(0, order // tile, rows_of, 0)

    def step(b, carry):
        at = pl.ds(pl.multiple_of(b * BLK, BLK), BLK)
        after = jnp.minimum(b // 2 + 1, order // tile - 1)
        top = pl.multiple_of(jnp.minimum(after * tile + (b % 2) * window, order - window), BLK)
        left = pl.ds(top, window)
        right = pl.ds(pl.multiple_of(after * tile, tile), tile)

        def beside(m):
            q, r = m // RANK, m % RANK
            term = dot_bf16(yx_ref[r, left, :], yx_ref[q, right, :], NT) * dot_bf16(yz_ref[r, left, :], yz_ref[q, right, :], NT)
            g_ref[left, :] = signed(g_ref[left, :] if m > 0 else None, term, q, r)

        factor_block(w_ref[at, at], u_ref, v_ref, beside)
        lh_ref[at, at], ll_ref[at, at] = split(u_ref[...].T)
        d_ref[at, :] = v_ref[...]
        for k in range(steps - 1):
            @pl.when(b == k)
            def _():
                first = (k + 1) * BLK
                inv = split(v_ref[...])

                def panel(t, c):
                    rows = pl.ds(pl.multiple_of(first + t * BLK, BLK), BLK)
                    lh_ref[rows, k * BLK:first], ll_ref[rows, k * BLK:first] = split(dot3(split(w_ref[rows, k * BLK:first]), inv, NT))
                    return c
                lax.fori_loop(0, steps - 1 - k, panel, 0)
                right = (lh_ref[first:, k * BLK:first], ll_ref[first:, k * BLK:first])

                def update(t, c):
                    rows = pl.ds(pl.multiple_of(first + t * BLK, BLK), BLK)
                    left = (lh_ref[rows, k * BLK:first], ll_ref[rows, k * BLK:first])
                    w_ref[rows, first:] = w_ref[rows, first:] - dot3(left, right, NT)
                    return c
                lax.fori_loop(0, steps - 1 - k, update, 0)
                if k % 2 == 1:
                    w_ref[first:, first:first + tile] = w_ref[first:, first:first + tile] + g_ref[first:, :]
        return carry
    lax.fori_loop(0, steps, step, 0)


def factor(yx, yz):
    tile = 2 * BLK
    f32 = jnp.float32
    return pl.pallas_call(
        factor_kernel,
        out_shape=(jax.ShapeDtypeStruct((K, K), jnp.bfloat16),) * 2 + (jax.ShapeDtypeStruct((K, BLK), f32),),
        in_specs=[VMEM] * 2,
        out_specs=(VMEM,) * 3,
        scratch_shapes=[pltpu.VMEM((K, K), f32), pltpu.VMEM((K, tile), f32), pltpu.VMEM((BLK, BLK), f32), pltpu.VMEM((BLK, BLK), f32)]
        + [pltpu.VMEM((2, RANK * tile, tile), f32)] * 2,
        compiler_params=pltpu.CompilerParams(vmem_limit_bytes=58 * MIB),
        cost_estimate=pl.CostEstimate(flops=40 * 10**9, bytes_accessed=12 * MIB, transcendentals=0),
    )(yx, yz)


def solve_kernel(place_ref, lh_any, ll_any, d_any, pieces_any, schur_any, *refs, prow):
    top_refs, refs = refs[:prow], refs[prow:]
    rest_ref, panel_ref, lh, ll, d_ref, pieces_ref, tops_ref, schur_ref, xh, xl, zh, zl, sem_ref = refs
    pcol = pieces_ref.shape[0]
    row, column = place_ref[0], place_ref[1]
    pairs = [(d_any, d_ref), (lh_any, lh), (ll_any, ll)]
    pairs += [(ref, tops_ref.at[turn ^ row]) for turn, ref in enumerate(top_refs)]
    pairs += [(pieces_any, pieces_ref), (schur_any, schur_ref)]
    copies = [pltpu.make_async_copy(here, there, sem_ref.at[n]) for n, (here, there) in enumerate(pairs)]
    for copy in copies:
        copy.start()
    for copy in copies[:3]:
        copy.wait()
    wide = 2 * BLK
    inverses = []
    for b in range(K // wide):
        upper, lower = slice(b * wide, b * wide + BLK), slice(b * wide + BLK, (b + 1) * wide)
        first, second = split(d_ref[upper, :]), split(d_ref[lower, :])
        between = dot3((lh[lower, upper], ll[lower, upper]), first, NN)
        corner = -dot3(second, split(between), NN)
        inverses.append(split(jnp.concatenate([
            jnp.concatenate([d_ref[upper, :], jnp.zeros((BLK, BLK), jnp.float32)], axis=1),
            jnp.concatenate([corner, d_ref[lower, :]], axis=1)], axis=0)))
    for copy in copies[3:-1]:
        copy.wait()
    for b in range(K // wide):
        at, done = slice(b * wide, (b + 1) * wide), slice(0, b * wide)
        blocks = range(wide // NB * b, wide // NB * (b + 1))
        value = jnp.concatenate([pieces_ref[n % pcol, :, n // pcol * NB:(n // pcol + 1) * NB] for n in blocks], axis=1)
        top = jnp.concatenate([tops_ref[n % prow, n // prow * NB:(n // prow + 1) * NB, :] for n in blocks], axis=0)
        if b > 0:
            left = (lh[at, done], ll[at, done])
            value = value - dot3((xh[:, done], xl[:, done]), left, NT)
            top = top - dot3(left, (zh[done, :], zl[done, :]), NN)
        value = dot3(split(value), inverses[b], NT)
        top = dot3(inverses[b], split(top), NN)
        xh[:, at], xl[:, at] = split(value)
        zh[at, :], zl[at, :] = split(top)
        for place, block in enumerate(blocks):
            @pl.when(column == block % pcol)
            def _():
                panel_ref[:, block // pcol * NB:(block // pcol + 1) * NB] = value[:, place * NB:(place + 1) * NB]
    copies[-1].wait()
    rest_ref[...] = schur_ref[...] - dot3((xh[...], xl[...]), (zh[...], zl[...]), NN)


def solve(place, high, low, inverses, pieces, schur, tops):
    rows, cols = schur.shape
    lead = K // pieces.shape[0]
    bf16, f32 = jnp.bfloat16, jnp.float32
    any_space = pl.BlockSpec(memory_space=pl.ANY)
    return pl.pallas_call(
        functools.partial(solve_kernel, prow=len(tops)),
        out_shape=(jax.ShapeDtypeStruct((rows, cols), f32), jax.ShapeDtypeStruct((rows, lead), f32)),
        in_specs=[SMEM] + [any_space] * (5 + len(tops)),
        out_specs=(VMEM, VMEM),
        scratch_shapes=[pltpu.VMEM((K, K), bf16)] * 2 + [pltpu.VMEM((K, BLK), f32), pltpu.VMEM(pieces.shape, f32)]
        + [pltpu.VMEM((len(tops),) + tops[0].shape, f32), pltpu.VMEM(schur.shape, f32)]
        + [pltpu.VMEM((rows, K), bf16)] * 2 + [pltpu.VMEM((K, cols), bf16)] * 2 + [pltpu.SemaphoreType.DMA((len(tops) + 5,))],
        compiler_params=pltpu.CompilerParams(vmem_limit_bytes=58 * MIB),
        cost_estimate=pl.CostEstimate(flops=12 * 10**9, bytes_accessed=24 * MIB, transcendentals=0),
    )(place, high, low, inverses, pieces, schur, *tops)


def gather_factors(mine, prow_count, pcol_count):
    own = mine.shape[0]
    half = own // 2

    def swap(axis, count, turn, value):
        return lax.ppermute(value, axis, [(n, n ^ turn) for n in range(count)])

    def after(value, *others):
        return lax.optimization_barrier((value, *others))[0]

    span = pcol_count // 2
    items = {0: mine}
    order = [0] + list(range(1, prow_count, 2)) + list(range(2, prow_count, 2))
    for turn in range(1, prow_count, 2):
        items[turn] = swap("prow", prow_count, turn, mine)
    near, far, near_order, far_order, begun = [], [], [], [], []
    for turn in order:
        if turn not in items:
            items[turn] = swap("prow", prow_count, 1, after(items[turn + 1], *begun[1]))
        value, last = items[turn], turn == order[-1]
        held = {0: value}
        for j in range(1, span):
            low = j & -j
            high = 1 << (j.bit_length() - 1)
            if low == high or last:
                held[j] = swap("pcol", pcol_count, 2 * j, value)
            else:
                held[j] = jnp.concatenate([swap("pcol", pcol_count, 2 * high, held[j ^ high][:half]), swap("pcol", pcol_count, 2 * low, held[j ^ low][half:])])
        begun.append([held[j] for j in range(1, span) if j & (j - 1) == 0])
        for part in [[j] for j in held] if last else [list(held)]:
            whole = jnp.concatenate([held[j] for j in part]) if len(part) > 1 else held[part[0]]
            near.append(whole)
            near_order += [(turn, 2 * j) for j in part]
            far.append(swap("pcol", pcol_count, 1, whole))
            far_order += [(turn, 2 * j + 1) for j in part]
    return near + far, near_order + far_order


def places_of(placement, order, prow_id, pcol_id, pcol_count):
    total = placement.shape[0]
    own = total // len(order)
    unit_of = [0] * len(order)
    for unit, (row_turn, col_turn) in enumerate(order):
        unit_of[row_turn * pcol_count + col_turn] = unit
    holder = jnp.arange(len(order))
    turn = ((holder // pcol_count) ^ prow_id) * pcol_count + ((holder % pcol_count) ^ pcol_id)
    units = jnp.sum(jnp.where(turn[:, None] == jnp.arange(len(order))[None, :], jnp.array(unit_of)[None, :], 0), axis=1)
    place = (units[:, None] * own + jnp.arange(own)[None, :]).reshape(1, total)
    blocks = total // NB
    in_block = jnp.arange(blocks)[:, None] == placement[None, :] // NB
    digits = jnp.concatenate([jnp.where(in_block, place // NB, 0), jnp.where(in_block, place % NB, 0)]).astype(jnp.bfloat16)
    at_row = (jnp.arange(NB)[:, None] == placement[None, :] % NB).astype(jnp.bfloat16)
    found = dot_bf16(digits, at_row, NT).astype(jnp.int32)
    return found[:blocks] * NB + found[blocks:]


def per_device(factors, x_factor, zinv_factor, placement):
    prow_count = lax.axis_size("prow")
    pcol_count = lax.axis_size("pcol")
    total_rows = placement.shape[0]
    local_rows = total_rows // prow_count
    local_cols = total_rows // pcol_count
    prow_id = lax.axis_index("prow")
    pcol_id = lax.axis_index("pcol")
    _, own, width = factors.shape
    count = prow_count * pcol_count
    lanes = BLK
    mine = factors.transpose(1, 0, 2).reshape(own, RANK * width // lanes, lanes)
    sources, order = gather_factors(mine, prow_count, pcol_count)
    found = places_of(placement, order, prow_id, pcol_id, pcol_count)
    by_row = lax.dynamic_index_in_dim(found.reshape(local_rows // NB, prow_count, NB), prow_id, 1, keepdims=False)
    by_col = lax.dynamic_index_in_dim(found.reshape(local_cols // NB, pcol_count, NB), pcol_id, 1, keepdims=False)
    places = jnp.concatenate([found[:K // NB], by_row, by_col]).reshape(-1)
    lead_rows, lead_cols = K // prow_count, K // pcol_count
    lead_x, lead_z, schur_local, front, top = assemble(
        places.astype(jnp.int32), sources, x_factor, zinv_factor, local_rows, local_cols, lead_rows, lead_cols)
    pieces = lax.all_gather(front, "pcol", axis=0, tiled=False)
    tops = [top] + [lax.ppermute(top, "prow", [(n, n ^ turn) for n in range(prow_count)]) for turn in range(1, prow_count)]
    high, low, inverses = factor(lead_x, lead_z)
    return solve(jnp.stack([prow_id, pcol_id]).astype(jnp.int32), high, low, inverses, pieces, schur_local, tops)


def solution(mesh):
    in_specs = (P(None, ("prow", "pcol"), None), P(), P(), P())
    out_specs = (P("prow", "pcol"), P("prow", "pcol"))
    return jax.shard_map(
        per_device, mesh=mesh, in_specs=in_specs, out_specs=out_specs, check_vma=False
    )
```

```python
import functools

import jax
import jax.numpy as jnp
from jax import lax
from jax.experimental import pallas as pl
from jax.experimental.pallas import tpu as pltpu
from jax.sharding import PartitionSpec as P

RANK = 4
NB = 64
K = 1024
SUB = 8
BLK = 128
MIB = 2**20

rank_signs = (1.0, 1.0, -1.0, -1.0)
NT = ((1,), (1,))
NN = ((1,), (0,))
VMEM = pl.BlockSpec(memory_space=pltpu.VMEM)
SMEM = pl.BlockSpec(memory_space=pltpu.SMEM)


def split(x):
    hi = x.astype(jnp.bfloat16)
    lo = (x - hi.astype(jnp.float32)).astype(jnp.bfloat16)
    return hi, lo


def dot_bf16(a, b, dims):
    return lax.dot_general(a, b, (dims, ((), ())), preferred_element_type=jnp.float32)


def dot3(a, b, dims):
    return dot_bf16(a[0], b[0], dims) + (dot_bf16(a[0], b[1], dims) + dot_bf16(a[1], b[0], dims))


def assemble_kernel(slots_ref, x_ref, z_ref, *refs, sources, lead_tiles, pick_tiles, col_tiles, rows):
    source_refs, refs = refs[:sources], refs[sources:]
    lead_x_ref, lead_z_ref, schur_ref, front_ref, top_ref, every_ref, picked_ref, yx_ref, yz_ref, sem_ref = refs
    step = pl.program_id(0)
    tile, parts, lanes = picked_ref.shape
    width = x_ref.shape[0]
    per_rank = width // lanes

    @pl.when(step == 0)
    def _():
        copies, first = [], 0
        for n, ref in enumerate(source_refs):
            copies.append(pltpu.make_async_copy(ref, every_ref.at[pl.ds(first, ref.shape[0])], sem_ref.at[n]))
            first += ref.shape[0]
        for copy in copies:
            copy.start()
        for copy in copies:
            copy.wait()

    @pl.when(step < pick_tiles)
    def _():
        def pick(group, carry):
            for k in range(16):
                i = group * 16 + k
                picked_ref[i] = every_ref[slots_ref[step * tile + i]]
            return carry
        lax.fori_loop(0, tile // 16, pick, 0)
        by_part = jnp.swapaxes(picked_ref[...], 0, 1)
        mine = jnp.concatenate([
            jnp.concatenate([by_part[r * per_rank + k] for k in range(per_rank)], axis=1) for r in range(RANK)], axis=0)
        images_x = dot_bf16(mine, x_ref[...], NN).astype(jnp.bfloat16).reshape(RANK, tile, width)
        images_z = dot_bf16(mine, z_ref[...], NN).astype(jnp.bfloat16).reshape(RANK, tile, width)

        @pl.when(step < lead_tiles)
        def _():
            lead_x_ref[...], lead_z_ref[...] = images_x, images_z

        @pl.when(step >= lead_tiles)
        def _():
            at = pl.ds(pl.multiple_of((step - lead_tiles) * tile, tile), tile)
            yx_ref[:, at, :], yz_ref[:, at, :] = images_x, images_z

    @pl.when(step >= pick_tiles)
    def _():
        high, wide = schur_ref.shape
        i, j = (step - pick_tiles) // col_tiles, (step - pick_tiles) % col_tiles
        left = pl.ds(pl.multiple_of(i * high, high), high)
        right = pl.ds(pl.multiple_of(rows + j * wide, wide), wide)
        schur_ref[...] = gram_tile(yx_ref, yz_ref, left, right)

        @pl.when(j == 0)
        def _():
            front_ref[...] = schur_ref[:, :front_ref.shape[1]]

        @pl.when(i == 0)
        def _():
            top_ref[...] = schur_ref[:top_ref.shape[0], :]


def gram_tile(yx_ref, yz_ref, left, right):
    left_x, left_z = yx_ref[:, left, :], yz_ref[:, left, :]
    _, high, width = left_x.shape
    left_x, left_z = left_x.reshape(RANK * high, width), left_z.reshape(RANK * high, width)
    total = None
    for q in range(RANK):
        gx = dot_bf16(left_x, yx_ref[q, right, :], NT)
        gz = dot_bf16(left_z, yz_ref[q, right, :], NT)
        for r in range(RANK):
            term = gx[r * high:(r + 1) * high] * gz[r * high:(r + 1) * high]
            total = signed(total, term, q, r)
    return total


def signed(total, term, q, r):
    if total is None:
        return term
    return total + term if rank_signs[q] * rank_signs[r] > 0 else total - term


def assemble(slots, sources, x_factor, z_factor, rows, cols, lead_rows, lead_cols):
    _, parts, lanes = sources[0].shape
    slots_held = sum(source.shape[0] for source in sources)
    width = x_factor.shape[0]
    tile = 256
    high, wide = min(512, rows), min(256, cols)
    lead_tiles, pick_tiles = K // tile, slots.shape[0] // tile
    row_tiles, col_tiles = rows // high, cols // wide
    whole = pl.BlockSpec((width, width), lambda s: (0, 0), pipeline_mode=pl.Buffered(1))
    lead = pl.BlockSpec((RANK, tile, width), lambda s: (0, jnp.minimum(s, lead_tiles - 1), 0))
    after = lambda s: jnp.maximum(s - pick_tiles, 0)
    bf16 = jnp.bfloat16
    any_space = pl.BlockSpec(memory_space=pl.ANY)
    body = functools.partial(assemble_kernel, sources=len(sources), lead_tiles=lead_tiles, pick_tiles=pick_tiles, col_tiles=col_tiles, rows=rows)
    return pl.pallas_call(
        body,
        grid=(pick_tiles + row_tiles * col_tiles,),
        out_shape=(jax.ShapeDtypeStruct((RANK, K, width), bf16),) * 2 + (
            jax.ShapeDtypeStruct((rows, cols), jnp.float32),
            jax.ShapeDtypeStruct((rows, lead_cols), jnp.float32),
            jax.ShapeDtypeStruct((lead_rows, cols), jnp.float32)),
        in_specs=[SMEM, whole, whole] + [any_space] * len(sources),
        out_specs=(lead, lead,
                   pl.BlockSpec((high, wide), lambda s: (after(s) // col_tiles, after(s) % col_tiles)),
                   pl.BlockSpec((high, lead_cols), lambda s: (after(s) // col_tiles, 0)),
                   pl.BlockSpec((lead_rows, wide), lambda s: (0, jnp.minimum(after(s), col_tiles - 1)))),
        scratch_shapes=[pltpu.VMEM((slots_held, parts, lanes), bf16), pltpu.VMEM((tile, parts, lanes), bf16)]
        + [pltpu.VMEM((RANK, rows + cols, width), bf16)] * 2 + [pltpu.SemaphoreType.DMA((len(sources),))],
        compiler_params=pltpu.CompilerParams(vmem_limit_bytes=58 * MIB),
        cost_estimate=pl.CostEstimate(flops=28 * 10**9, bytes_accessed=30 * MIB, transcendentals=0),
    )(slots, x_factor, z_factor, *sources)


def factor_block(block, u_ref, v_ref, beside):
    count = BLK // SUB
    sub_iota = lax.broadcasted_iota(jnp.int32, (SUB, BLK), 0)
    lane_iota = lax.broadcasted_iota(jnp.int32, (SUB, BLK), 1)
    rows_a = [block[SUB * i:SUB * (i + 1), :] for i in range(count)]
    rows_v = [(lane_iota == sub_iota + SUB * i).astype(jnp.float32) for i in range(count)]

    def spread_lane(x, lane):
        return jnp.broadcast_to(x[:, lane:lane + 1], (SUB, BLK))

    def spread_row(x, row):
        return jnp.broadcast_to(x[row:row + 1, :], (SUB, BLK))

    for m in range(count):
        beside(m)
        head_a, head_v = rows_a[m], rows_v[m]
        cols = [spread_lane(head_a, SUB * m + k) for k in range(SUB)]
        below = [[spread_lane(rows_a[i], SUB * m + k) for k in range(SUB)] for i in range(m + 1, count)]
        scale = jnp.zeros((SUB, BLK), jnp.float32)
        for j in range(SUB):
            pivot = spread_row(cols[j], j)
            root = lax.rsqrt(pivot)
            scale = jnp.where(sub_iota == j, root, scale)
            mult = jnp.where(sub_iota > j, cols[j], 0.0) * root
            row_a = spread_row(head_a, j) * root
            row_v = spread_row(head_v, j) * root
            lead = [spread_row(cols[k], j) * root if k > j else None for k in range(SUB)]
            if j + 1 < SUB:
                head_a = head_a - mult * row_a
                head_v = head_v - mult * row_v
                for k in range(j + 1, SUB):
                    cols[k] = cols[k] - mult * lead[k]
            for n, i in enumerate(range(m + 1, count)):
                mult_i = below[n][j] * root
                rows_a[i] = rows_a[i] - mult_i * row_a
                rows_v[i] = rows_v[i] - mult_i * row_v
                for k in range(j + 1, SUB):
                    below[n][k] = below[n][k] - mult_i * lead[k]
        u = jnp.where(lane_iota >= sub_iota + SUB * m, head_a * scale, 0.0)
        v = jnp.where(lane_iota <= sub_iota + SUB * m, head_v * scale, 0.0)
        u_ref[SUB * m:SUB * (m + 1), :] = u
        v_ref[SUB * m:SUB * (m + 1), :] = v


def factor_kernel(yx_ref, yz_ref, lh_ref, ll_ref, d_ref, w_ref, g_ref, u_ref, v_ref):
    order = lh_ref.shape[0]
    steps = order // BLK
    tile = 2 * BLK
    window = 3 * BLK
    lh_ref[...] = jnp.zeros_like(lh_ref)
    ll_ref[...] = jnp.zeros_like(ll_ref)
    w_ref[:, tile:] = jnp.zeros((order, order - tile), jnp.float32)

    def rows_of(i, carry):
        left = pl.ds(pl.multiple_of(i * 2 * tile, 2 * tile), 2 * tile)
        w_ref[left, :tile] = gram_tile(yx_ref, yz_ref, left, pl.ds(0, tile))
        return carry
    lax.fori_loop(0, order // (2 * tile), rows_of, 0)

    def step(b, carry):
        at = pl.ds(pl.multiple_of(b * BLK, BLK), BLK)
        after = jnp.minimum(b // 2 + 1, order // tile - 1)
        top = pl.multiple_of(jnp.minimum(after * tile + (b % 2) * window, order - window), BLK)
        left = pl.ds(top, window)
        right = pl.ds(pl.multiple_of(after * tile, tile), tile)

        def beside(m):
            q, r = m // RANK, m % RANK
            term = dot_bf16(yx_ref[r, left, :], yx_ref[q, right, :], NT) * dot_bf16(yz_ref[r, left, :], yz_ref[q, right, :], NT)
            g_ref[left, :] = signed(g_ref[left, :] if m > 0 else None, term, q, r)

        factor_block(w_ref[at, at], u_ref, v_ref, beside)
        lh_ref[at, at], ll_ref[at, at] = split(u_ref[...].T)
        d_ref[at, :] = v_ref[...]
        for k in range(steps - 1):
            @pl.when(b == k)
            def _():
                first = (k + 1) * BLK
                inv = split(v_ref[...])

                def panel(t, c):
                    rows = pl.ds(pl.multiple_of(first + t * BLK, BLK), BLK)
                    lh_ref[rows, k * BLK:first], ll_ref[rows, k * BLK:first] = split(dot3(split(w_ref[rows, k * BLK:first]), inv, NT))
                    return c
                lax.fori_loop(0, steps - 1 - k, panel, 0)
                right = (lh_ref[first:, k * BLK:first], ll_ref[first:, k * BLK:first])

                def update(t, c):
                    rows = pl.ds(pl.multiple_of(first + t * BLK, BLK), BLK)
                    left = (lh_ref[rows, k * BLK:first], ll_ref[rows, k * BLK:first])
                    w_ref[rows, first:] = w_ref[rows, first:] - dot3(left, right, NT)
                    return c
                lax.fori_loop(0, steps - 1 - k, update, 0)
                if k % 2 == 1:
                    w_ref[first:, first:first + tile] = w_ref[first:, first:first + tile] + g_ref[first:, :]
        return carry
    lax.fori_loop(0, steps, step, 0)


def factor(yx, yz):
    tile = 2 * BLK
    f32 = jnp.float32
    return pl.pallas_call(
        factor_kernel,
        out_shape=(jax.ShapeDtypeStruct((K, K), jnp.bfloat16),) * 2 + (jax.ShapeDtypeStruct((K, BLK), f32),),
        in_specs=[VMEM] * 2,
        out_specs=(VMEM,) * 3,
        scratch_shapes=[pltpu.VMEM((K, K), f32), pltpu.VMEM((K, tile), f32), pltpu.VMEM((BLK, BLK), f32), pltpu.VMEM((BLK, BLK), f32)],
        compiler_params=pltpu.CompilerParams(vmem_limit_bytes=58 * MIB),
        cost_estimate=pl.CostEstimate(flops=40 * 10**9, bytes_accessed=12 * MIB, transcendentals=0),
    )(yx, yz)


def solve_kernel(place_ref, lh_any, ll_any, d_any, pieces_any, schur_any, *refs, prow):
    top_refs, refs = refs[:prow], refs[prow:]
    rest_ref, panel_ref, lh, ll, d_ref, pieces_ref, tops_ref, schur_ref, xh, xl, zh, zl, sem_ref = refs
    pcol = pieces_ref.shape[0]
    row, column = place_ref[0], place_ref[1]
    pairs = [(d_any, d_ref), (lh_any, lh), (ll_any, ll)]
    pairs += [(ref, tops_ref.at[turn ^ row]) for turn, ref in enumerate(top_refs)]
    pairs += [(pieces_any, pieces_ref), (schur_any, schur_ref)]
    copies = [pltpu.make_async_copy(here, there, sem_ref.at[n]) for n, (here, there) in enumerate(pairs)]
    for copy in copies:
        copy.start()
    for copy in copies[:3]:
        copy.wait()
    wide = 2 * BLK
    inverses = []
    for b in range(K // wide):
        upper, lower = slice(b * wide, b * wide + BLK), slice(b * wide + BLK, (b + 1) * wide)
        first, second = split(d_ref[upper, :]), split(d_ref[lower, :])
        between = dot3((lh[lower, upper], ll[lower, upper]), first, NN)
        corner = -dot3(second, split(between), NN)
        inverses.append(split(jnp.concatenate([
            jnp.concatenate([d_ref[upper, :], jnp.zeros((BLK, BLK), jnp.float32)], axis=1),
            jnp.concatenate([corner, d_ref[lower, :]], axis=1)], axis=0)))
    for copy in copies[3:-1]:
        copy.wait()
    for b in range(K // wide):
        at, done = slice(b * wide, (b + 1) * wide), slice(0, b * wide)
        blocks = range(wide // NB * b, wide // NB * (b + 1))
        value = jnp.concatenate([pieces_ref[n % pcol, :, n // pcol * NB:(n // pcol + 1) * NB] for n in blocks], axis=1)
        top = jnp.concatenate([tops_ref[n % prow, n // prow * NB:(n // prow + 1) * NB, :] for n in blocks], axis=0)
        if b > 0:
            left = (lh[at, done], ll[at, done])
            value = value - dot3((xh[:, done], xl[:, done]), left, NT)
            top = top - dot3(left, (zh[done, :], zl[done, :]), NN)
        value = dot3(split(value), inverses[b], NT)
        top = dot3(inverses[b], split(top), NN)
        xh[:, at], xl[:, at] = split(value)
        zh[at, :], zl[at, :] = split(top)
        for place, block in enumerate(blocks):
            @pl.when(column == block % pcol)
            def _():
                panel_ref[:, block // pcol * NB:(block // pcol + 1) * NB] = value[:, place * NB:(place + 1) * NB]
    copies[-1].wait()
    rest_ref[...] = schur_ref[...] - dot3((xh[...], xl[...]), (zh[...], zl[...]), NN)


def solve(place, high, low, inverses, pieces, schur, tops):
    rows, cols = schur.shape
    lead = K // pieces.shape[0]
    bf16, f32 = jnp.bfloat16, jnp.float32
    any_space = pl.BlockSpec(memory_space=pl.ANY)
    return pl.pallas_call(
        functools.partial(solve_kernel, prow=len(tops)),
        out_shape=(jax.ShapeDtypeStruct((rows, cols), f32), jax.ShapeDtypeStruct((rows, lead), f32)),
        in_specs=[SMEM] + [any_space] * (5 + len(tops)),
        out_specs=(VMEM, VMEM),
        scratch_shapes=[pltpu.VMEM((K, K), bf16)] * 2 + [pltpu.VMEM((K, BLK), f32), pltpu.VMEM(pieces.shape, f32)]
        + [pltpu.VMEM((len(tops),) + tops[0].shape, f32), pltpu.VMEM(schur.shape, f32)]
        + [pltpu.VMEM((rows, K), bf16)] * 2 + [pltpu.VMEM((K, cols), bf16)] * 2 + [pltpu.SemaphoreType.DMA((len(tops) + 5,))],
        compiler_params=pltpu.CompilerParams(vmem_limit_bytes=58 * MIB),
        cost_estimate=pl.CostEstimate(flops=12 * 10**9, bytes_accessed=24 * MIB, transcendentals=0),
    )(place, high, low, inverses, pieces, schur, *tops)


def gather_factors(mine, prow_count, pcol_count):
    own = mine.shape[0]
    half = own // 2

    def swap(axis, count, turn, value):
        return lax.ppermute(value, axis, [(n, n ^ turn) for n in range(count)])

    span = pcol_count // 2
    level_of = {j: bin(j).count("1") for j in range(1, span)}
    levels = max(level_of.values(), default=0)
    order = [0] + list(range(1, prow_count, 2)) + list(range(2, prow_count, 2))
    items = {0: mine}
    for turn in range(1, prow_count, 2):
        items[turn] = swap("prow", prow_count, turn, mine)
    held = {turn: {} for turn in order}
    parts = []

    def spread(turn, j):
        low, high = j & -j, 1 << (j.bit_length() - 1)
        if low == high:
            return [swap("pcol", pcol_count, 2 * j, held[turn][0])]
        return [swap("pcol", pcol_count, 2 * high, held[turn][j ^ high][:half]), swap("pcol", pcol_count, 2 * low, held[turn][j ^ low][half:])]

    def take(turn, which):
        whole = jnp.concatenate([held[turn][j] for j in which]) if len(which) > 1 else held[turn][which[0]]
        parts.append((turn, which, whole, swap("pcol", pcol_count, 1, whole)))

    for phase in range(len(order) + levels - 1):
        moved = {}
        if phase < len(order):
            turn = order[phase]
            held[turn][0] = items[turn]
            if turn % 2 == 1 and turn > 1:
                moved["z", turn - 1] = [swap("prow", prow_count, 1, items[turn])]
        for level in range(1, levels + 1):
            if 0 <= phase - level + 1 < len(order):
                turn = order[phase - level + 1]
                for j in range(1, span):
                    if level_of[j] == level:
                        moved[turn, j] = spread(turn, j)
        if phase + 1 < len(order) and order[phase + 1] in items:
            moved["z", order[phase + 1]] = [items[order[phase + 1]]]
        results = iter(lax.optimization_barrier([value for values in moved.values() for value in values]))
        for (turn, j), values in moved.items():
            arrived = [next(results) for _ in values]
            if turn == "z":
                items[j] = arrived[0]
            else:
                held[turn][j] = arrived[0] if len(arrived) == 1 else jnp.concatenate(arrived)
        if 0 <= phase - levels + 1 < len(order) - 1:
            take(order[phase - levels + 1], list(held[order[phase - levels + 1]]))
        if phase == len(order) + levels - 3:
            early = [j for j in held[order[-1]] if j == 0 or level_of[j] < levels]
            if len(early) == span or levels < 2:
                early = []
            else:
                take(order[-1], early)
    take(order[-1], [j for j in range(span) if j not in early])
    near = [whole for _, _, whole, _ in parts]
    far = [swapped for _, _, _, swapped in parts]
    places = [(turn, 2 * j) for turn, which, _, _ in parts for j in which]
    return near + far, places + [(turn, col + 1) for turn, col in places]


def places_of(placement, order, prow_id, pcol_id, pcol_count):
    total = placement.shape[0]
    own = total // len(order)
    unit_of = [0] * len(order)
    for unit, (row_turn, col_turn) in enumerate(order):
        unit_of[row_turn * pcol_count + col_turn] = unit
    holder = jnp.arange(len(order))
    turn = ((holder // pcol_count) ^ prow_id) * pcol_count + ((holder % pcol_count) ^ pcol_id)
    units = jnp.sum(jnp.where(turn[:, None] == jnp.arange(len(order))[None, :], jnp.array(unit_of)[None, :], 0), axis=1)
    place = (units[:, None] * own + jnp.arange(own)[None, :]).reshape(1, total)
    blocks = total // NB
    in_block = jnp.arange(blocks)[:, None] == placement[None, :] // NB
    digits = jnp.concatenate([jnp.where(in_block, place // NB, 0), jnp.where(in_block, place % NB, 0)]).astype(jnp.bfloat16)
    at_row = (jnp.arange(NB)[:, None] == placement[None, :] % NB).astype(jnp.bfloat16)
    found = dot_bf16(digits, at_row, NT).astype(jnp.int32)
    return found[:blocks] * NB + found[blocks:]


def per_device(factors, x_factor, zinv_factor, placement):
    prow_count = lax.axis_size("prow")
    pcol_count = lax.axis_size("pcol")
    total_rows = placement.shape[0]
    local_rows = total_rows // prow_count
    local_cols = total_rows // pcol_count
    prow_id = lax.axis_index("prow")
    pcol_id = lax.axis_index("pcol")
    _, own, width = factors.shape
    count = prow_count * pcol_count
    lanes = BLK
    mine = factors.transpose(1, 0, 2).reshape(own, RANK * width // lanes, lanes)
    sources, order = gather_factors(mine, prow_count, pcol_count)
    found = places_of(placement, order, prow_id, pcol_id, pcol_count)
    by_row = lax.dynamic_index_in_dim(found.reshape(local_rows // NB, prow_count, NB), prow_id, 1, keepdims=False)
    by_col = lax.dynamic_index_in_dim(found.reshape(local_cols // NB, pcol_count, NB), pcol_id, 1, keepdims=False)
    places = jnp.concatenate([found[:K // NB], by_row, by_col]).reshape(-1)
    lead_rows, lead_cols = K // prow_count, K // pcol_count
    lead_x, lead_z, schur_local, front, top = assemble(
        places.astype(jnp.int32), sources, x_factor, zinv_factor, local_rows, local_cols, lead_rows, lead_cols)
    pieces = lax.all_gather(front, "pcol", axis=0, tiled=False)
    tops = [top] + [lax.ppermute(top, "prow", [(n, n ^ turn) for n in range(prow_count)]) for turn in range(1, prow_count)]
    high, low, inverses = factor(lead_x, lead_z)
    return solve(jnp.stack([prow_id, pcol_id]).astype(jnp.int32), high, low, inverses, pieces, schur_local, tops)


def solution(mesh):
    in_specs = (P(None, ("prow", "pcol"), None), P(), P(), P())
    out_specs = (P("prow", "pcol"), P("prow", "pcol"))
    return jax.shard_map(
        per_device, mesh=mesh, in_specs=in_specs, out_specs=out_specs, check_vma=False
    )
```

```python
import functools

import jax
import jax.numpy as jnp
from jax import lax
from jax.experimental import pallas as pl
from jax.experimental.pallas import tpu as pltpu
from jax.sharding import PartitionSpec as P

RANK = 4
NB = 64
K = 1024
SUB = 8
BLK = 128
MIB = 2**20

rank_signs = (1.0, 1.0, -1.0, -1.0)
NT = ((1,), (1,))
NN = ((1,), (0,))
VMEM = pl.BlockSpec(memory_space=pltpu.VMEM)
SMEM = pl.BlockSpec(memory_space=pltpu.SMEM)


def split(x):
    hi = x.astype(jnp.bfloat16)
    lo = (x - hi.astype(jnp.float32)).astype(jnp.bfloat16)
    return hi, lo


def dot_bf16(a, b, dims):
    return lax.dot_general(a, b, (dims, ((), ())), preferred_element_type=jnp.float32)


def dot3(a, b, dims):
    return dot_bf16(a[0], b[0], dims) + (dot_bf16(a[0], b[1], dims) + dot_bf16(a[1], b[0], dims))


def assemble_kernel(slots_ref, x_ref, z_ref, *refs, sources, lead_tiles, pick_tiles, col_tiles, rows):
    source_refs, refs = refs[:sources], refs[sources:]
    lead_x_ref, lead_z_ref, schur_ref, front_ref, top_ref, every_ref, picked_ref, yx_ref, yz_ref, sem_ref = refs
    step = pl.program_id(0)
    tile, parts, lanes = picked_ref.shape
    width = x_ref.shape[0]
    per_rank = width // lanes

    @pl.when(step == 0)
    def _():
        copies, first = [], 0
        for n, ref in enumerate(source_refs):
            copies.append(pltpu.make_async_copy(ref, every_ref.at[pl.ds(first, ref.shape[0])], sem_ref.at[n]))
            first += ref.shape[0]
        for copy in copies:
            copy.start()
        for copy in copies:
            copy.wait()

    @pl.when(step < pick_tiles)
    def _():
        def pick(group, carry):
            for k in range(16):
                i = group * 16 + k
                picked_ref[i] = every_ref[slots_ref[step * tile + i]]
            return carry
        lax.fori_loop(0, tile // 16, pick, 0)
        by_part = jnp.swapaxes(picked_ref[...], 0, 1)
        mine = jnp.concatenate([
            jnp.concatenate([by_part[r * per_rank + k] for k in range(per_rank)], axis=1) for r in range(RANK)], axis=0)
        images_x = dot_bf16(mine, x_ref[...], NN).astype(jnp.bfloat16).reshape(RANK, tile, width)
        images_z = dot_bf16(mine, z_ref[...], NN).astype(jnp.bfloat16).reshape(RANK, tile, width)

        @pl.when(step < lead_tiles)
        def _():
            lead_x_ref[...], lead_z_ref[...] = images_x, images_z

        @pl.when(step >= lead_tiles)
        def _():
            at = pl.ds(pl.multiple_of((step - lead_tiles) * tile, tile), tile)
            yx_ref[:, at, :], yz_ref[:, at, :] = images_x, images_z

    @pl.when(step >= pick_tiles)
    def _():
        high, wide = schur_ref.shape
        i, j = (step - pick_tiles) // col_tiles, (step - pick_tiles) % col_tiles
        left = pl.ds(pl.multiple_of(i * high, high), high)
        right = pl.ds(pl.multiple_of(rows + j * wide, wide), wide)
        schur_ref[...] = gram_tile(yx_ref, yz_ref, left, right)

        @pl.when(j == 0)
        def _():
            front_ref[...] = schur_ref[:, :front_ref.shape[1]]

        @pl.when(i == 0)
        def _():
            top_ref[...] = schur_ref[:top_ref.shape[0], :]


def gram_tile(yx_ref, yz_ref, left, right):
    left_x, left_z = yx_ref[:, left, :], yz_ref[:, left, :]
    _, high, width = left_x.shape
    left_x, left_z = left_x.reshape(RANK * high, width), left_z.reshape(RANK * high, width)
    total = None
    for q in range(RANK):
        gx = dot_bf16(left_x, yx_ref[q, right, :], NT)
        gz = dot_bf16(left_z, yz_ref[q, right, :], NT)
        for r in range(RANK):
            term = gx[r * high:(r + 1) * high] * gz[r * high:(r + 1) * high]
            total = signed(total, term, q, r)
    return total


def signed(total, term, q, r):
    if total is None:
        return term
    return total + term if rank_signs[q] * rank_signs[r] > 0 else total - term


def assemble(slots, sources, x_factor, z_factor, rows, cols, lead_rows, lead_cols):
    _, parts, lanes = sources[0].shape
    slots_held = sum(source.shape[0] for source in sources)
    width = x_factor.shape[0]
    tile = 256
    high, wide = min(512, rows), min(256, cols)
    lead_tiles, pick_tiles = K // tile, slots.shape[0] // tile
    row_tiles, col_tiles = rows // high, cols // wide
    whole = pl.BlockSpec((width, width), lambda s: (0, 0), pipeline_mode=pl.Buffered(1))
    lead = pl.BlockSpec((RANK, tile, width), lambda s: (0, jnp.minimum(s, lead_tiles - 1), 0))
    after = lambda s: jnp.maximum(s - pick_tiles, 0)
    bf16 = jnp.bfloat16
    any_space = pl.BlockSpec(memory_space=pl.ANY)
    body = functools.partial(assemble_kernel, sources=len(sources), lead_tiles=lead_tiles, pick_tiles=pick_tiles, col_tiles=col_tiles, rows=rows)
    return pl.pallas_call(
        body,
        grid=(pick_tiles + row_tiles * col_tiles,),
        out_shape=(jax.ShapeDtypeStruct((RANK, K, width), bf16),) * 2 + (
            jax.ShapeDtypeStruct((rows, cols), jnp.float32),
            jax.ShapeDtypeStruct((rows, lead_cols), jnp.float32),
            jax.ShapeDtypeStruct((lead_rows, cols), jnp.float32)),
        in_specs=[SMEM, whole, whole] + [any_space] * len(sources),
        out_specs=(lead, lead,
                   pl.BlockSpec((high, wide), lambda s: (after(s) // col_tiles, after(s) % col_tiles)),
                   pl.BlockSpec((high, lead_cols), lambda s: (after(s) // col_tiles, 0)),
                   pl.BlockSpec((lead_rows, wide), lambda s: (0, jnp.minimum(after(s), col_tiles - 1)))),
        scratch_shapes=[pltpu.VMEM((slots_held, parts, lanes), bf16), pltpu.VMEM((tile, parts, lanes), bf16)]
        + [pltpu.VMEM((RANK, rows + cols, width), bf16)] * 2 + [pltpu.SemaphoreType.DMA((len(sources),))],
        compiler_params=pltpu.CompilerParams(vmem_limit_bytes=58 * MIB),
        cost_estimate=pl.CostEstimate(flops=28 * 10**9, bytes_accessed=30 * MIB, transcendentals=0),
    )(slots, x_factor, z_factor, *sources)


def factor_block(block, u_ref, v_ref, beside):
    count = BLK // SUB
    sub_iota = lax.broadcasted_iota(jnp.int32, (SUB, BLK), 0)
    lane_iota = lax.broadcasted_iota(jnp.int32, (SUB, BLK), 1)
    rows_a = [block[SUB * i:SUB * (i + 1), :] for i in range(count)]
    rows_v = [(lane_iota == sub_iota + SUB * i).astype(jnp.float32) for i in range(count)]

    def spread_lane(x, lane):
        return jnp.broadcast_to(x[:, lane:lane + 1], (SUB, BLK))

    def spread_row(x, row):
        return jnp.broadcast_to(x[row:row + 1, :], (SUB, BLK))

    for m in range(count):
        beside(m)
        head_a, head_v = rows_a[m], rows_v[m]
        cols = [spread_lane(head_a, SUB * m + k) for k in range(SUB)]
        more = m + 1 < count
        if more:
            next_a, next_v = rows_a[m + 1], rows_v[m + 1]
            below = [spread_lane(next_a, SUB * m + k) for k in range(SUB)]
        scale = jnp.zeros((SUB, BLK), jnp.float32)
        done_a, done_v = [], []
        for j in range(SUB):
            pivot = spread_row(cols[j], j)
            root = lax.rsqrt(pivot)
            scale = jnp.where(sub_iota == j, root, scale)
            mult = jnp.where(sub_iota > j, cols[j], 0.0) * root
            row_a = spread_row(head_a, j) * root
            row_v = spread_row(head_v, j) * root
            lead = [spread_row(cols[k], j) * root if k > j else None for k in range(SUB)]
            done_a.append(row_a)
            done_v.append(row_v)
            if j + 1 < SUB:
                for k in range(j + 1, SUB):
                    cols[k] = cols[k] - mult * lead[k]
                head_a = head_a - mult * row_a
                head_v = head_v - mult * row_v
            if more:
                mult_next = below[j] * root
                for k in range(j + 1, SUB):
                    below[k] = below[k] - mult_next * lead[k]
                next_a = next_a - mult_next * row_a
                next_v = next_v - mult_next * row_v
        u = head_a * scale
        u_ref[SUB * m:SUB * (m + 1), :] = jnp.where(lane_iota >= sub_iota + SUB * m, u, 0.0)
        v_ref[SUB * m:SUB * (m + 1), :] = jnp.where(lane_iota <= sub_iota + SUB * m, head_v * scale, 0.0)
        if more:
            rows_a[m + 1], rows_v[m + 1] = next_a, next_v
        if m + 2 < count:
            turned = u.T
            for i in range(m + 2, count):
                mine = turned[SUB * i:SUB * (i + 1), :]
                for j in range(SUB):
                    mult_i = spread_lane(mine, j)
                    rows_a[i] = rows_a[i] - mult_i * done_a[j]
                    rows_v[i] = rows_v[i] - mult_i * done_v[j]


def factor_kernel(yx_ref, yz_ref, lh_ref, ll_ref, d_ref, w_ref, g_ref, u_ref, v_ref):
    order = lh_ref.shape[0]
    steps = order // BLK
    tile = 2 * BLK
    window = 3 * BLK
    lh_ref[...] = jnp.zeros_like(lh_ref)
    ll_ref[...] = jnp.zeros_like(ll_ref)
    w_ref[:, tile:] = jnp.zeros((order, order - tile), jnp.float32)

    def rows_of(i, carry):
        left = pl.ds(pl.multiple_of(i * 2 * tile, 2 * tile), 2 * tile)
        w_ref[left, :tile] = gram_tile(yx_ref, yz_ref, left, pl.ds(0, tile))
        return carry
    lax.fori_loop(0, order // (2 * tile), rows_of, 0)

    def step(b, carry):
        at = pl.ds(pl.multiple_of(b * BLK, BLK), BLK)
        after = jnp.minimum(b // 2 + 1, order // tile - 1)
        top = pl.multiple_of(jnp.minimum(after * tile + (b % 2) * window, order - window), BLK)
        left = pl.ds(top, window)
        right = pl.ds(pl.multiple_of(after * tile, tile), tile)

        def beside(m):
            q, r = m // RANK, m % RANK
            term = dot_bf16(yx_ref[r, left, :], yx_ref[q, right, :], NT) * dot_bf16(yz_ref[r, left, :], yz_ref[q, right, :], NT)
            g_ref[left, :] = signed(g_ref[left, :] if m > 0 else None, term, q, r)

        factor_block(w_ref[at, at], u_ref, v_ref, beside)
        lh_ref[at, at], ll_ref[at, at] = split(u_ref[...].T)
        d_ref[at, :] = v_ref[...]
        for k in range(steps - 1):
            @pl.when(b == k)
            def _():
                first = (k + 1) * BLK
                inv = split(v_ref[...])

                def panel(t, c):
                    rows = pl.ds(pl.multiple_of(first + t * BLK, BLK), BLK)
                    lh_ref[rows, k * BLK:first], ll_ref[rows, k * BLK:first] = split(dot3(split(w_ref[rows, k * BLK:first]), inv, NT))
                    return c
                lax.fori_loop(0, steps - 1 - k, panel, 0)
                right = (lh_ref[first:, k * BLK:first], ll_ref[first:, k * BLK:first])

                def update(t, c):
                    rows = pl.ds(pl.multiple_of(first + t * BLK, BLK), BLK)
                    left = (lh_ref[rows, k * BLK:first], ll_ref[rows, k * BLK:first])
                    w_ref[rows, first:] = w_ref[rows, first:] - dot3(left, right, NT)
                    return c
                lax.fori_loop(0, steps - 1 - k, update, 0)
                if k % 2 == 1:
                    w_ref[first:, first:first + tile] = w_ref[first:, first:first + tile] + g_ref[first:, :]
        return carry
    lax.fori_loop(0, steps, step, 0)


def factor(yx, yz):
    tile = 2 * BLK
    f32 = jnp.float32
    return pl.pallas_call(
        factor_kernel,
        out_shape=(jax.ShapeDtypeStruct((K, K), jnp.bfloat16),) * 2 + (jax.ShapeDtypeStruct((K, BLK), f32),),
        in_specs=[VMEM] * 2,
        out_specs=(VMEM,) * 3,
        scratch_shapes=[pltpu.VMEM((K, K), f32), pltpu.VMEM((K, tile), f32), pltpu.VMEM((BLK, BLK), f32), pltpu.VMEM((BLK, BLK), f32)],
        compiler_params=pltpu.CompilerParams(vmem_limit_bytes=58 * MIB),
        cost_estimate=pl.CostEstimate(flops=40 * 10**9, bytes_accessed=12 * MIB, transcendentals=0),
    )(yx, yz)


def solve_kernel(place_ref, lh_any, ll_any, d_any, pieces_any, schur_any, *refs, prow):
    top_refs, refs = refs[:prow], refs[prow:]
    rest_ref, panel_ref, lh, ll, d_ref, pieces_ref, tops_ref, schur_ref, xh, xl, zh, zl, sem_ref = refs
    pcol = pieces_ref.shape[0]
    row, column = place_ref[0], place_ref[1]
    pairs = [(d_any, d_ref), (lh_any, lh), (ll_any, ll)]
    pairs += [(ref, tops_ref.at[turn ^ row]) for turn, ref in enumerate(top_refs)]
    pairs += [(pieces_any, pieces_ref), (schur_any, schur_ref)]
    copies = [pltpu.make_async_copy(here, there, sem_ref.at[n]) for n, (here, there) in enumerate(pairs)]
    for copy in copies:
        copy.start()
    for copy in copies[:3]:
        copy.wait()
    wide = 2 * BLK
    inverses = []
    for b in range(K // wide):
        upper, lower = slice(b * wide, b * wide + BLK), slice(b * wide + BLK, (b + 1) * wide)
        first, second = split(d_ref[upper, :]), split(d_ref[lower, :])
        between = dot3((lh[lower, upper], ll[lower, upper]), first, NN)
        corner = -dot3(second, split(between), NN)
        inverses.append(split(jnp.concatenate([
            jnp.concatenate([d_ref[upper, :], jnp.zeros((BLK, BLK), jnp.float32)], axis=1),
            jnp.concatenate([corner, d_ref[lower, :]], axis=1)], axis=0)))
    for copy in copies[3:-1]:
        copy.wait()
    for b in range(K // wide):
        at, done = slice(b * wide, (b + 1) * wide), slice(0, b * wide)
        blocks = range(wide // NB * b, wide // NB * (b + 1))
        value = jnp.concatenate([pieces_ref[n % pcol, :, n // pcol * NB:(n // pcol + 1) * NB] for n in blocks], axis=1)
        top = jnp.concatenate([tops_ref[n % prow, n // prow * NB:(n // prow + 1) * NB, :] for n in blocks], axis=0)
        if b > 0:
            left = (lh[at, done], ll[at, done])
            value = value - dot3((xh[:, done], xl[:, done]), left, NT)
            top = top - dot3(left, (zh[done, :], zl[done, :]), NN)
        value = dot3(split(value), inverses[b], NT)
        top = dot3(inverses[b], split(top), NN)
        xh[:, at], xl[:, at] = split(value)
        zh[at, :], zl[at, :] = split(top)
        for place, block in enumerate(blocks):
            @pl.when(column == block % pcol)
            def _():
                panel_ref[:, block // pcol * NB:(block // pcol + 1) * NB] = value[:, place * NB:(place + 1) * NB]
    copies[-1].wait()
    rest_ref[...] = schur_ref[...] - dot3((xh[...], xl[...]), (zh[...], zl[...]), NN)


def solve(place, high, low, inverses, pieces, schur, tops):
    rows, cols = schur.shape
    lead = K // pieces.shape[0]
    bf16, f32 = jnp.bfloat16, jnp.float32
    any_space = pl.BlockSpec(memory_space=pl.ANY)
    return pl.pallas_call(
        functools.partial(solve_kernel, prow=len(tops)),
        out_shape=(jax.ShapeDtypeStruct((rows, cols), f32), jax.ShapeDtypeStruct((rows, lead), f32)),
        in_specs=[SMEM] + [any_space] * (5 + len(tops)),
        out_specs=(VMEM, VMEM),
        scratch_shapes=[pltpu.VMEM((K, K), bf16)] * 2 + [pltpu.VMEM((K, BLK), f32), pltpu.VMEM(pieces.shape, f32)]
        + [pltpu.VMEM((len(tops),) + tops[0].shape, f32), pltpu.VMEM(schur.shape, f32)]
        + [pltpu.VMEM((rows, K), bf16)] * 2 + [pltpu.VMEM((K, cols), bf16)] * 2 + [pltpu.SemaphoreType.DMA((len(tops) + 5,))],
        compiler_params=pltpu.CompilerParams(vmem_limit_bytes=58 * MIB),
        cost_estimate=pl.CostEstimate(flops=12 * 10**9, bytes_accessed=24 * MIB, transcendentals=0),
    )(place, high, low, inverses, pieces, schur, *tops)


def gather_factors(mine, prow_count, pcol_count):
    own = mine.shape[0]
    half = own // 2

    def swap(axis, count, turn, value):
        return lax.ppermute(value, axis, [(n, n ^ turn) for n in range(count)])

    span = pcol_count // 2
    level_of = {j: bin(j).count("1") for j in range(1, span)}
    levels = max(level_of.values(), default=0)
    order = [0] + list(range(1, prow_count, 2)) + list(range(2, prow_count, 2))
    items = {0: mine}
    held = {turn: {} for turn in order}
    parts = []

    def spread(turn, j):
        low, high = j & -j, 1 << (j.bit_length() - 1)
        if low == high:
            return [swap("pcol", pcol_count, 2 * j, held[turn][0])]
        return [swap("pcol", pcol_count, 2 * high, held[turn][j ^ high][:half]), swap("pcol", pcol_count, 2 * low, held[turn][j ^ low][half:])]

    def take(turn, which):
        whole = jnp.concatenate([held[turn][j] for j in which]) if len(which) > 1 else held[turn][which[0]]
        parts.append((turn, which, whole, swap("pcol", pcol_count, 1, whole)))

    for phase in range(len(order) + levels - 1):
        moved = {}
        if phase < len(order):
            turn = order[phase]
            held[turn][0] = items[turn]
            if turn % 2 == 1 and turn > 1:
                moved["z", turn - 1] = [swap("prow", prow_count, 1, items[turn])]
        for level in range(1, levels + 1):
            if 0 <= phase - level + 1 < len(order):
                turn = order[phase - level + 1]
                for j in range(1, span):
                    if level_of[j] == level:
                        moved[turn, j] = spread(turn, j)
        if phase + 1 < len(order):
            turn = order[phase + 1]
            if turn % 2 == 1:
                moved["z", turn] = [swap("prow", prow_count, turn, mine)]
            elif turn in items:
                moved["z", turn] = [items[turn]]
        mine, *results = lax.optimization_barrier([mine] + [value for values in moved.values() for value in values])
        results = iter(results)
        for (turn, j), values in moved.items():
            arrived = [next(results) for _ in values]
            if turn == "z":
                items[j] = arrived[0]
            else:
                held[turn][j] = arrived[0] if len(arrived) == 1 else jnp.concatenate(arrived)
        if 0 <= phase - levels + 1 < len(order) - 1:
            take(order[phase - levels + 1], list(held[order[phase - levels + 1]]))
        if phase == len(order) + levels - 3:
            early = [j for j in held[order[-1]] if j == 0 or level_of[j] < levels]
            if len(early) == span or levels < 2:
                early = []
            else:
                take(order[-1], early)
    take(order[-1], [j for j in range(span) if j not in early])
    near = [whole for _, _, whole, _ in parts]
    far = [swapped for _, _, _, swapped in parts]
    places = [(turn, 2 * j) for turn, which, _, _ in parts for j in which]
    return near + far, places + [(turn, col + 1) for turn, col in places]


def places_of(placement, order, prow_id, pcol_id, pcol_count):
    total = placement.shape[0]
    own = total // len(order)
    unit_of = [0] * len(order)
    for unit, (row_turn, col_turn) in enumerate(order):
        unit_of[row_turn * pcol_count + col_turn] = unit
    holder = jnp.arange(len(order))
    turn = ((holder // pcol_count) ^ prow_id) * pcol_count + ((holder % pcol_count) ^ pcol_id)
    units = jnp.sum(jnp.where(turn[:, None] == jnp.arange(len(order))[None, :], jnp.array(unit_of)[None, :], 0), axis=1)
    place = (units[:, None] * own + jnp.arange(own)[None, :]).reshape(1, total)
    blocks = total // NB
    in_block = jnp.arange(blocks)[:, None] == placement[None, :] // NB
    digits = jnp.concatenate([jnp.where(in_block, place // NB, 0), jnp.where(in_block, place % NB, 0)]).astype(jnp.bfloat16)
    at_row = (jnp.arange(NB)[:, None] == placement[None, :] % NB).astype(jnp.bfloat16)
    found = dot_bf16(digits, at_row, NT).astype(jnp.int32)
    return found[:blocks] * NB + found[blocks:]


def per_device(factors, x_factor, zinv_factor, placement):
    prow_count = lax.axis_size("prow")
    pcol_count = lax.axis_size("pcol")
    total_rows = placement.shape[0]
    local_rows = total_rows // prow_count
    local_cols = total_rows // pcol_count
    prow_id = lax.axis_index("prow")
    pcol_id = lax.axis_index("pcol")
    _, own, width = factors.shape
    count = prow_count * pcol_count
    lanes = BLK
    mine = factors.transpose(1, 0, 2).reshape(own, RANK * width // lanes, lanes)
    sources, order = gather_factors(mine, prow_count, pcol_count)
    found = places_of(placement, order, prow_id, pcol_id, pcol_count)
    by_row = lax.dynamic_index_in_dim(found.reshape(local_rows // NB, prow_count, NB), prow_id, 1, keepdims=False)
    by_col = lax.dynamic_index_in_dim(found.reshape(local_cols // NB, pcol_count, NB), pcol_id, 1, keepdims=False)
    places = jnp.concatenate([found[:K // NB], by_row, by_col]).reshape(-1)
    lead_rows, lead_cols = K // prow_count, K // pcol_count
    lead_x, lead_z, schur_local, front, top = assemble(
        places.astype(jnp.int32), sources, x_factor, zinv_factor, local_rows, local_cols, lead_rows, lead_cols)
    pieces = lax.all_gather(front, "pcol", axis=0, tiled=False)
    tops = [top] + [lax.ppermute(top, "prow", [(n, n ^ turn) for n in range(prow_count)]) for turn in range(1, prow_count)]
    high, low, inverses = factor(lead_x, lead_z)
    return solve(jnp.stack([prow_id, pcol_id]).astype(jnp.int32), high, low, inverses, pieces, schur_local, tops)


def solution(mesh):
    in_specs = (P(None, ("prow", "pcol"), None), P(), P(), P())
    out_specs = (P("prow", "pcol"), P("prow", "pcol"))
    return jax.shard_map(
        per_device, mesh=mesh, in_specs=in_specs, out_specs=out_specs, check_vma=False
    )
```

```python
import functools

import jax
import jax.numpy as jnp
from jax import lax
from jax.experimental import pallas as pl
from jax.experimental.pallas import tpu as pltpu
from jax.sharding import PartitionSpec as P

RANK = 4
NB = 64
K = 1024
SUB = 8
BLK = 128
MIB = 2**20

rank_signs = (1.0, 1.0, -1.0, -1.0)
NT = ((1,), (1,))
NN = ((1,), (0,))
TN = ((0,), (0,))
VMEM = pl.BlockSpec(memory_space=pltpu.VMEM)
SMEM = pl.BlockSpec(memory_space=pltpu.SMEM)


def split(x):
    hi = x.astype(jnp.bfloat16)
    lo = (x - hi.astype(jnp.float32)).astype(jnp.bfloat16)
    return hi, lo


def dot_bf16(a, b, dims):
    return lax.dot_general(a, b, (dims, ((), ())), preferred_element_type=jnp.float32)


def dot3(a, b, dims):
    return dot_bf16(a[0], b[0], dims) + (dot_bf16(a[0], b[1], dims) + dot_bf16(a[1], b[0], dims))


def assemble_kernel(slots_ref, x_ref, z_ref, *refs, sources, lead_tiles, pick_tiles, col_tiles, rows):
    source_refs, refs = refs[:sources], refs[sources:]
    lead_x_ref, lead_z_ref, schur_ref, front_ref, top_ref, every_ref, picked_ref, yx_ref, yz_ref, sem_ref = refs
    step = pl.program_id(0)
    tile, parts, lanes = picked_ref.shape
    width = x_ref.shape[0]
    per_rank = width // lanes

    @pl.when(step == 0)
    def _():
        copies, first = [], 0
        for n, ref in enumerate(source_refs):
            copies.append(pltpu.make_async_copy(ref, every_ref.at[pl.ds(first, ref.shape[0])], sem_ref.at[n]))
            first += ref.shape[0]
        for copy in copies:
            copy.start()
        for copy in copies:
            copy.wait()

    @pl.when(step < pick_tiles)
    def _():
        def pick(group, carry):
            for k in range(16):
                i = group * 16 + k
                picked_ref[i] = every_ref[slots_ref[step * tile + i]]
            return carry
        lax.fori_loop(0, tile // 16, pick, 0)
        by_part = jnp.swapaxes(picked_ref[...], 0, 1)
        mine = jnp.concatenate([
            jnp.concatenate([by_part[r * per_rank + k] for k in range(per_rank)], axis=1) for r in range(RANK)], axis=0)
        images_x = dot_bf16(mine, x_ref[...], NN).astype(jnp.bfloat16).reshape(RANK, tile, width)
        images_z = dot_bf16(mine, z_ref[...], NN).astype(jnp.bfloat16).reshape(RANK, tile, width)

        @pl.when(step < lead_tiles)
        def _():
            lead_x_ref[...], lead_z_ref[...] = images_x, images_z

        @pl.when(step >= lead_tiles)
        def _():
            at = pl.ds(pl.multiple_of((step - lead_tiles) * tile, tile), tile)
            yx_ref[:, at, :], yz_ref[:, at, :] = images_x, images_z

    @pl.when(step >= pick_tiles)
    def _():
        high, wide = schur_ref.shape
        i, j = (step - pick_tiles) // col_tiles, (step - pick_tiles) % col_tiles
        left = pl.ds(pl.multiple_of(i * high, high), high)
        right = pl.ds(pl.multiple_of(rows + j * wide, wide), wide)
        schur_ref[...] = gram_tile(yx_ref, yz_ref, left, right)

        @pl.when(j == 0)
        def _():
            front_ref[...] = schur_ref[:, :front_ref.shape[1]]

        @pl.when(i == 0)
        def _():
            top_ref[...] = schur_ref[:top_ref.shape[0], :]


def gram_tile(yx_ref, yz_ref, left, right):
    left_x, left_z = yx_ref[:, left, :], yz_ref[:, left, :]
    _, high, width = left_x.shape
    left_x, left_z = left_x.reshape(RANK * high, width), left_z.reshape(RANK * high, width)
    total = None
    for q in range(RANK):
        gx = dot_bf16(left_x, yx_ref[q, right, :], NT)
        gz = dot_bf16(left_z, yz_ref[q, right, :], NT)
        for r in range(RANK):
            term = gx[r * high:(r + 1) * high] * gz[r * high:(r + 1) * high]
            total = signed(total, term, q, r)
    return total


def signed(total, term, q, r):
    if total is None:
        return term
    return total + term if rank_signs[q] * rank_signs[r] > 0 else total - term


def assemble(slots, sources, x_factor, z_factor, rows, cols, lead_rows, lead_cols):
    _, parts, lanes = sources[0].shape
    slots_held = sum(source.shape[0] for source in sources)
    width = x_factor.shape[0]
    tile = 256
    high, wide = min(512, rows), min(256, cols)
    lead_tiles, pick_tiles = K // tile, slots.shape[0] // tile
    row_tiles, col_tiles = rows // high, cols // wide
    whole = pl.BlockSpec((width, width), lambda s: (0, 0), pipeline_mode=pl.Buffered(1))
    lead = pl.BlockSpec((RANK, tile, width), lambda s: (0, jnp.minimum(s, lead_tiles - 1), 0))
    after = lambda s: jnp.maximum(s - pick_tiles, 0)
    bf16 = jnp.bfloat16
    any_space = pl.BlockSpec(memory_space=pl.ANY)
    body = functools.partial(assemble_kernel, sources=len(sources), lead_tiles=lead_tiles, pick_tiles=pick_tiles, col_tiles=col_tiles, rows=rows)
    return pl.pallas_call(
        body,
        grid=(pick_tiles + row_tiles * col_tiles,),
        out_shape=(jax.ShapeDtypeStruct((RANK, K, width), bf16),) * 2 + (
            jax.ShapeDtypeStruct((rows, cols), jnp.float32),
            jax.ShapeDtypeStruct((rows, lead_cols), jnp.float32),
            jax.ShapeDtypeStruct((lead_rows, cols), jnp.float32)),
        in_specs=[SMEM, whole, whole] + [any_space] * len(sources),
        out_specs=(lead, lead,
                   pl.BlockSpec((high, wide), lambda s: (after(s) // col_tiles, after(s) % col_tiles)),
                   pl.BlockSpec((high, lead_cols), lambda s: (after(s) // col_tiles, 0)),
                   pl.BlockSpec((lead_rows, wide), lambda s: (0, jnp.minimum(after(s), col_tiles - 1)))),
        scratch_shapes=[pltpu.VMEM((slots_held, parts, lanes), bf16), pltpu.VMEM((tile, parts, lanes), bf16)]
        + [pltpu.VMEM((RANK, rows + cols, width), bf16)] * 2 + [pltpu.SemaphoreType.DMA((len(sources),))],
        compiler_params=pltpu.CompilerParams(vmem_limit_bytes=58 * MIB),
        cost_estimate=pl.CostEstimate(flops=28 * 10**9, bytes_accessed=30 * MIB, transcendentals=0),
    )(slots, x_factor, z_factor, *sources)


def factor_block(block, u_ref, v_ref, beside):
    count = BLK // SUB
    sub_iota = lax.broadcasted_iota(jnp.int32, (SUB, BLK), 0)
    lane_iota = lax.broadcasted_iota(jnp.int32, (SUB, BLK), 1)
    rows_a = [block[SUB * i:SUB * (i + 1), :] for i in range(count)]
    rows_v = [(lane_iota == sub_iota + SUB * i).astype(jnp.float32) for i in range(count)]

    def spread_lane(x, lane):
        return jnp.broadcast_to(x[:, lane:lane + 1], (SUB, BLK))

    def spread_row(x, row):
        return jnp.broadcast_to(x[row:row + 1, :], (SUB, BLK))

    cols = [spread_lane(rows_a[0], k) for k in range(SUB)]
    for m in range(count):
        beside(m)
        head_a, head_v = rows_a[m], rows_v[m]
        more = m + 1 < count
        below, ahead, coming, later = [], [], [], []
        beyond = m + 2 < count
        if beyond:
            later_a, later_v = rows_a[m + 2], rows_v[m + 2]
            later = [spread_lane(later_a, SUB * m + k) for k in range(SUB)]
        if more:
            next_a, next_v = rows_a[m + 1], rows_v[m + 1]
            below = [spread_lane(next_a, SUB * m + k) for k in range(SUB)]
            ahead = [spread_lane(head_a, SUB * (m + 1) + k) for k in range(SUB)]
            coming = [spread_lane(next_a, SUB * (m + 1) + k) for k in range(SUB)]
        scale = jnp.zeros((SUB, BLK), jnp.float32)
        for j in range(SUB):
            pivot = spread_row(cols[j], j)
            root = lax.rsqrt(pivot)
            scale = jnp.where(sub_iota == j, root, scale)
            mult = jnp.where(sub_iota > j, cols[j], 0.0) * root
            lead = [spread_row(cols[k], j) * root if k > j else None for k in range(SUB)]
            row_a = spread_row(head_a, j) * root
            row_v = spread_row(head_v, j) * root
            row_ahead = [spread_row(value, j) * root for value in ahead]
            if j + 1 < SUB:
                for k in range(j + 1, SUB):
                    cols[k] = cols[k] - mult * lead[k]
                head_a = head_a - mult * row_a
                head_v = head_v - mult * row_v
                ahead = [value - mult * row for value, row in zip(ahead, row_ahead)]
            if more:
                mult_next = below[j] * root
                for k in range(j + 1, SUB):
                    below[k] = below[k] - mult_next * lead[k]
                coming = [value - mult_next * row for value, row in zip(coming, row_ahead)]
                next_a = next_a - mult_next * row_a
                next_v = next_v - mult_next * row_v
            if beyond:
                mult_later = later[j] * root
                for k in range(j + 1, SUB):
                    later[k] = later[k] - mult_later * lead[k]
                later_a = later_a - mult_later * row_a
                later_v = later_v - mult_later * row_v
        u = jnp.where(lane_iota >= sub_iota + SUB * m, head_a * scale, 0.0)
        v = jnp.where(lane_iota <= sub_iota + SUB * m, head_v * scale, 0.0)
        u_ref[SUB * m:SUB * (m + 1), :] = u
        v_ref[SUB * m:SUB * (m + 1), :] = v
        if more:
            rows_a[m + 1], rows_v[m + 1] = next_a, next_v
        if beyond:
            rows_a[m + 2], rows_v[m + 2] = later_a, later_v
        if m + 3 < count:
            both = jnp.concatenate([u, v], axis=1)
            u_hi, both_hi = u.astype(jnp.bfloat16).astype(jnp.float32), both.astype(jnp.bfloat16).astype(jnp.float32)
            u_lo, both_lo = u - u_hi, both - both_hi
            left = jnp.concatenate([u_hi, u_hi, u_lo, u_lo], axis=0).astype(jnp.bfloat16)
            right = jnp.concatenate([both_hi, both_lo, both_hi, both_lo], axis=0).astype(jnp.bfloat16)
            change = dot_bf16(left, right, TN)
            for i in range(m + 3, count):
                at = slice(SUB * i, SUB * (i + 1))
                rows_a[i] = rows_a[i] - change[at, :BLK]
                rows_v[i] = rows_v[i] - change[at, BLK:]
        cols = coming


def factor_kernel(yx_ref, yz_ref, lh_ref, ll_ref, d_ref, w_ref, g_ref, u_ref, v_ref):
    order = lh_ref.shape[0]
    steps = order // BLK
    tile = 2 * BLK
    window = 3 * BLK
    lh_ref[...] = jnp.zeros_like(lh_ref)
    ll_ref[...] = jnp.zeros_like(ll_ref)
    w_ref[:, tile:] = jnp.zeros((order, order - tile), jnp.float32)

    def rows_of(i, carry):
        left = pl.ds(pl.multiple_of(i * 2 * tile, 2 * tile), 2 * tile)
        w_ref[left, :tile] = gram_tile(yx_ref, yz_ref, left, pl.ds(0, tile))
        return carry
    lax.fori_loop(0, order // (2 * tile), rows_of, 0)

    def step(b, carry):
        at = pl.ds(pl.multiple_of(b * BLK, BLK), BLK)
        after = jnp.minimum(b // 2 + 1, order // tile - 1)
        top = pl.multiple_of(jnp.minimum(after * tile + (b % 2) * window, order - window), BLK)
        left = pl.ds(top, window)
        right = pl.ds(pl.multiple_of(after * tile, tile), tile)

        def beside(m):
            q, r = m // RANK, m % RANK
            term = dot_bf16(yx_ref[r, left, :], yx_ref[q, right, :], NT) * dot_bf16(yz_ref[r, left, :], yz_ref[q, right, :], NT)
            g_ref[left, :] = signed(g_ref[left, :] if m > 0 else None, term, q, r)

        factor_block(w_ref[at, at], u_ref, v_ref, beside)
        lh_ref[at, at], ll_ref[at, at] = split(u_ref[...].T)
        d_ref[at, :] = v_ref[...]
        for k in range(steps - 1):
            @pl.when(b == k)
            def _():
                first = (k + 1) * BLK
                inv = split(v_ref[...])

                def panel(t, c):
                    rows = pl.ds(pl.multiple_of(first + t * BLK, BLK), BLK)
                    lh_ref[rows, k * BLK:first], ll_ref[rows, k * BLK:first] = split(dot3(split(w_ref[rows, k * BLK:first]), inv, NT))
                    return c
                lax.fori_loop(0, steps - 1 - k, panel, 0)
                right = (lh_ref[first:, k * BLK:first], ll_ref[first:, k * BLK:first])

                def update(t, c):
                    rows = pl.ds(pl.multiple_of(first + t * BLK, BLK), BLK)
                    left = (lh_ref[rows, k * BLK:first], ll_ref[rows, k * BLK:first])
                    w_ref[rows, first:] = w_ref[rows, first:] - dot3(left, right, NT)
                    return c
                lax.fori_loop(0, steps - 1 - k, update, 0)
                if k % 2 == 1:
                    w_ref[first:, first:first + tile] = w_ref[first:, first:first + tile] + g_ref[first:, :]
        return carry
    lax.fori_loop(0, steps, step, 0)


def factor(yx, yz):
    tile = 2 * BLK
    f32 = jnp.float32
    return pl.pallas_call(
        factor_kernel,
        out_shape=(jax.ShapeDtypeStruct((K, K), jnp.bfloat16),) * 2 + (jax.ShapeDtypeStruct((K, BLK), f32),),
        in_specs=[VMEM] * 2,
        out_specs=(VMEM,) * 3,
        scratch_shapes=[pltpu.VMEM((K, K), f32), pltpu.VMEM((K, tile), f32), pltpu.VMEM((BLK, BLK), f32), pltpu.VMEM((BLK, BLK), f32)],
        compiler_params=pltpu.CompilerParams(vmem_limit_bytes=58 * MIB),
        cost_estimate=pl.CostEstimate(flops=40 * 10**9, bytes_accessed=12 * MIB, transcendentals=0),
    )(yx, yz)


def solve_kernel(place_ref, lh_any, ll_any, d_any, pieces_any, schur_any, *refs, prow):
    top_refs, refs = refs[:prow], refs[prow:]
    rest_ref, panel_ref, lh, ll, d_ref, pieces_ref, tops_ref, schur_ref, xh, xl, zh, zl, sem_ref = refs
    pcol = pieces_ref.shape[0]
    row, column = place_ref[0], place_ref[1]
    pairs = [(d_any, d_ref), (lh_any, lh), (ll_any, ll)]
    pairs += [(ref, tops_ref.at[turn ^ row]) for turn, ref in enumerate(top_refs)]
    pairs += [(pieces_any, pieces_ref), (schur_any, schur_ref)]
    copies = [pltpu.make_async_copy(here, there, sem_ref.at[n]) for n, (here, there) in enumerate(pairs)]
    for copy in copies:
        copy.start()
    for copy in copies[:3]:
        copy.wait()
    wide = 2 * BLK
    inverses = []
    for b in range(K // wide):
        upper, lower = slice(b * wide, b * wide + BLK), slice(b * wide + BLK, (b + 1) * wide)
        first, second = split(d_ref[upper, :]), split(d_ref[lower, :])
        between = dot3((lh[lower, upper], ll[lower, upper]), first, NN)
        corner = -dot3(second, split(between), NN)
        inverses.append(split(jnp.concatenate([
            jnp.concatenate([d_ref[upper, :], jnp.zeros((BLK, BLK), jnp.float32)], axis=1),
            jnp.concatenate([corner, d_ref[lower, :]], axis=1)], axis=0)))
    for copy in copies[3:-1]:
        copy.wait()
    for b in range(K // wide):
        at, done = slice(b * wide, (b + 1) * wide), slice(0, b * wide)
        blocks = range(wide // NB * b, wide // NB * (b + 1))
        value = jnp.concatenate([pieces_ref[n % pcol, :, n // pcol * NB:(n // pcol + 1) * NB] for n in blocks], axis=1)
        top = jnp.concatenate([tops_ref[n % prow, n // prow * NB:(n // prow + 1) * NB, :] for n in blocks], axis=0)
        if b > 0:
            left = (lh[at, done], ll[at, done])
            value = value - dot3((xh[:, done], xl[:, done]), left, NT)
            top = top - dot3(left, (zh[done, :], zl[done, :]), NN)
        value = dot3(split(value), inverses[b], NT)
        top = dot3(inverses[b], split(top), NN)
        xh[:, at], xl[:, at] = split(value)
        zh[at, :], zl[at, :] = split(top)
        for place, block in enumerate(blocks):
            @pl.when(column == block % pcol)
            def _():
                panel_ref[:, block // pcol * NB:(block // pcol + 1) * NB] = value[:, place * NB:(place + 1) * NB]
    copies[-1].wait()
    rest_ref[...] = schur_ref[...] - dot3((xh[...], xl[...]), (zh[...], zl[...]), NN)


def solve(place, high, low, inverses, pieces, schur, tops):
    rows, cols = schur.shape
    lead = K // pieces.shape[0]
    bf16, f32 = jnp.bfloat16, jnp.float32
    any_space = pl.BlockSpec(memory_space=pl.ANY)
    return pl.pallas_call(
        functools.partial(solve_kernel, prow=len(tops)),
        out_shape=(jax.ShapeDtypeStruct((rows, cols), f32), jax.ShapeDtypeStruct((rows, lead), f32)),
        in_specs=[SMEM] + [any_space] * (5 + len(tops)),
        out_specs=(VMEM, VMEM),
        scratch_shapes=[pltpu.VMEM((K, K), bf16)] * 2 + [pltpu.VMEM((K, BLK), f32), pltpu.VMEM(pieces.shape, f32)]
        + [pltpu.VMEM((len(tops),) + tops[0].shape, f32), pltpu.VMEM(schur.shape, f32)]
        + [pltpu.VMEM((rows, K), bf16)] * 2 + [pltpu.VMEM((K, cols), bf16)] * 2 + [pltpu.SemaphoreType.DMA((len(tops) + 5,))],
        compiler_params=pltpu.CompilerParams(vmem_limit_bytes=58 * MIB),
        cost_estimate=pl.CostEstimate(flops=12 * 10**9, bytes_accessed=24 * MIB, transcendentals=0),
    )(place, high, low, inverses, pieces, schur, *tops)


def gather_factors(mine, prow_count, pcol_count):
    own = mine.shape[0]
    half = own // 2

    def swap(axis, count, turn, value):
        return lax.ppermute(value, axis, [(n, n ^ turn) for n in range(count)])

    span = pcol_count // 2
    level_of = {j: bin(j).count("1") for j in range(1, span)}
    levels = max(level_of.values(), default=0)
    order = [0] + [1] * (prow_count > 1) + list(range(2, prow_count, 2)) + list(range(3, prow_count, 2))
    items = {0: mine}
    held = {turn: {} for turn in order}
    parts = []

    def spread(turn, j):
        low, high = j & -j, 1 << (j.bit_length() - 1)
        if low == high:
            return [swap("pcol", pcol_count, 2 * j, held[turn][0])]
        return [swap("pcol", pcol_count, 2 * high, held[turn][j ^ high][:half]), swap("pcol", pcol_count, 2 * low, held[turn][j ^ low][half:])]

    def take(turn, which):
        whole = jnp.concatenate([held[turn][j] for j in which]) if len(which) > 1 else held[turn][which[0]]
        parts.append((turn, which, whole, swap("pcol", pcol_count, 1, whole)))

    for phase in range(len(order) + levels - 1):
        moved = {}
        if phase < len(order):
            turn = order[phase]
            held[turn][0] = items[turn]
            if turn % 2 == 0 and turn > 0:
                moved["z", turn + 1] = [swap("prow", prow_count, 1, items[turn])]
        for level in range(1, levels + 1):
            if 0 <= phase - level + 1 < len(order):
                turn = order[phase - level + 1]
                for j in range(1, span):
                    if level_of[j] == level:
                        moved[turn, j] = spread(turn, j)
        if phase + 1 < len(order):
            turn = order[phase + 1]
            if turn == 1 or turn % 2 == 0:
                moved["z", turn] = [swap("prow", prow_count, turn, mine)]
            elif turn in items:
                moved["z", turn] = [items[turn]]
        mine, *results = lax.optimization_barrier([mine] + [value for values in moved.values() for value in values])
        results = iter(results)
        for (turn, j), values in moved.items():
            arrived = [next(results) for _ in values]
            if turn == "z":
                items[j] = arrived[0]
            else:
                held[turn][j] = arrived[0] if len(arrived) == 1 else jnp.concatenate(arrived)
        if 0 <= phase - levels + 1 < len(order) - 1:
            take(order[phase - levels + 1], list(held[order[phase - levels + 1]]))
        if phase == len(order) + levels - 3:
            early = [j for j in held[order[-1]] if j == 0 or level_of[j] < levels]
            if len(early) == span or levels < 2:
                early = []
            else:
                take(order[-1], early)
    take(order[-1], [j for j in range(span) if j not in early])
    near = [whole for _, _, whole, _ in parts]
    far = [swapped for _, _, _, swapped in parts]
    places = [(turn, 2 * j) for turn, which, _, _ in parts for j in which]
    return near + far, places + [(turn, col + 1) for turn, col in places]


def places_of(placement, order, prow_id, pcol_id, pcol_count):
    total = placement.shape[0]
    own = total // len(order)
    unit_of = [0] * len(order)
    for unit, (row_turn, col_turn) in enumerate(order):
        unit_of[row_turn * pcol_count + col_turn] = unit
    holder = jnp.arange(len(order))
    turn = ((holder // pcol_count) ^ prow_id) * pcol_count + ((holder % pcol_count) ^ pcol_id)
    units = jnp.sum(jnp.where(turn[:, None] == jnp.arange(len(order))[None, :], jnp.array(unit_of)[None, :], 0), axis=1)
    place = (units[:, None] * own + jnp.arange(own)[None, :]).reshape(1, total)
    blocks = total // NB
    in_block = jnp.arange(blocks)[:, None] == placement[None, :] // NB
    digits = jnp.concatenate([jnp.where(in_block, place // NB, 0), jnp.where(in_block, place % NB, 0)]).astype(jnp.bfloat16)
    at_row = (jnp.arange(NB)[:, None] == placement[None, :] % NB).astype(jnp.bfloat16)
    found = dot_bf16(digits, at_row, NT).astype(jnp.int32)
    return found[:blocks] * NB + found[blocks:]


def per_device(factors, x_factor, zinv_factor, placement):
    prow_count = lax.axis_size("prow")
    pcol_count = lax.axis_size("pcol")
    total_rows = placement.shape[0]
    local_rows = total_rows // prow_count
    local_cols = total_rows // pcol_count
    prow_id = lax.axis_index("prow")
    pcol_id = lax.axis_index("pcol")
    _, own, width = factors.shape
    count = prow_count * pcol_count
    lanes = BLK
    mine = factors.transpose(1, 0, 2).reshape(own, RANK * width // lanes, lanes)
    sources, order = gather_factors(mine, prow_count, pcol_count)
    found = places_of(placement, order, prow_id, pcol_id, pcol_count)
    by_row = lax.dynamic_index_in_dim(found.reshape(local_rows // NB, prow_count, NB), prow_id, 1, keepdims=False)
    by_col = lax.dynamic_index_in_dim(found.reshape(local_cols // NB, pcol_count, NB), pcol_id, 1, keepdims=False)
    places = jnp.concatenate([found[:K // NB], by_row, by_col]).reshape(-1)
    lead_rows, lead_cols = K // prow_count, K // pcol_count
    lead_x, lead_z, schur_local, front, top = assemble(
        places.astype(jnp.int32), sources, x_factor, zinv_factor, local_rows, local_cols, lead_rows, lead_cols)
    pieces = lax.all_gather(front, "pcol", axis=0, tiled=False)
    tops = [top] + [lax.ppermute(top, "prow", [(n, n ^ turn) for n in range(prow_count)]) for turn in range(1, prow_count)]
    high, low, inverses = factor(lead_x, lead_z)
    return solve(jnp.stack([prow_id, pcol_id]).astype(jnp.int32), high, low, inverses, pieces, schur_local, tops)


def solution(mesh):
    in_specs = (P(None, ("prow", "pcol"), None), P(), P(), P())
    out_specs = (P("prow", "pcol"), P("prow", "pcol"))
    return jax.shard_map(
        per_device, mesh=mesh, in_specs=in_specs, out_specs=out_specs, check_vma=False
    )
```

```python
import functools

import jax
import jax.numpy as jnp
from jax import lax
from jax.experimental import pallas as pl
from jax.experimental.pallas import tpu as pltpu
from jax.sharding import PartitionSpec as P

RANK = 4
NB = 64
K = 1024
SUB = 8
BLK = 128
MIB = 2**20

rank_signs = (1.0, 1.0, -1.0, -1.0)
NT = ((1,), (1,))
NN = ((1,), (0,))
VMEM = pl.BlockSpec(memory_space=pltpu.VMEM)
SMEM = pl.BlockSpec(memory_space=pltpu.SMEM)


def split(x):
    hi = x.astype(jnp.bfloat16)
    lo = (x - hi.astype(jnp.float32)).astype(jnp.bfloat16)
    return hi, lo


def dot_bf16(a, b, dims):
    return lax.dot_general(a, b, (dims, ((), ())), preferred_element_type=jnp.float32)


def dot3(a, b, dims):
    return dot_bf16(a[0], b[0], dims) + (dot_bf16(a[0], b[1], dims) + dot_bf16(a[1], b[0], dims))


def assemble_kernel(place_ref, slots_ref, x_ref, z_ref, *refs, sources, lead_tiles, pick_tiles, col_tiles, rows, prow, pcol):
    source_refs, refs = refs[:sources], refs[sources:]
    lead_x_ref, lead_z_ref, schur_ref, front_ref, top_ref, every_ref, picked_ref, yx_ref, yz_ref, sem_ref = refs
    step = pl.program_id(0)
    tile, parts, lanes = picked_ref.shape
    width = x_ref.shape[0]
    per_rank = width // lanes

    @pl.when(step == 0)
    def _():
        copies, first = [], 0
        for n, ref in enumerate(source_refs):
            copies.append(pltpu.make_async_copy(ref, every_ref.at[pl.ds(first, ref.shape[0])], sem_ref.at[n]))
            first += ref.shape[0]
        for copy in copies:
            copy.start()
        for copy in copies:
            copy.wait()

    @pl.when(step < pick_tiles)
    def _():
        def pick(group, carry):
            for k in range(16):
                i = group * 16 + k
                picked_ref[i] = every_ref[slots_ref[step * tile + i]]
            return carry
        lax.fori_loop(0, tile // 16, pick, 0)
        by_part = jnp.swapaxes(picked_ref[...], 0, 1)
        mine = jnp.concatenate([
            jnp.concatenate([by_part[r * per_rank + k] for k in range(per_rank)], axis=1) for r in range(RANK)], axis=0)
        images_x = dot_bf16(mine, x_ref[...], NN).astype(jnp.bfloat16).reshape(RANK, tile, width)
        images_z = dot_bf16(mine, z_ref[...], NN).astype(jnp.bfloat16).reshape(RANK, tile, width)

        def keep(block, s):
            at = pl.ds(pl.multiple_of(block * NB, NB), NB)
            yx_ref[:, at, :] = images_x[:, s * NB:(s + 1) * NB, :]
            yz_ref[:, at, :] = images_z[:, s * NB:(s + 1) * NB, :]

        @pl.when(step < lead_tiles)
        def _():
            lead_x_ref[...], lead_z_ref[...] = images_x, images_z
            for s in range(tile // NB):
                block = step * (tile // NB) + s

                @pl.when(block % prow == place_ref[0])
                def _():
                    keep(block // prow, s)

                @pl.when(block % pcol == place_ref[1])
                def _():
                    keep(rows // NB + block // pcol, s)

        @pl.when(step >= lead_tiles)
        def _():
            lead = K // NB
            row_rest, col_rest = rows // NB - lead // prow, (yx_ref.shape[1] - rows) // NB - lead // pcol
            for s in range(tile // NB):
                block = (step - lead_tiles) * (tile // NB) + s

                @pl.when(block < row_rest + col_rest)
                def _():
                    keep(jnp.where(block < row_rest, lead // prow + block, rows // NB + lead // pcol + block - row_rest), s)

    @pl.when(step >= pick_tiles)
    def _():
        high, wide = schur_ref.shape
        i, j = (step - pick_tiles) // col_tiles, (step - pick_tiles) % col_tiles
        left = pl.ds(pl.multiple_of(i * high, high), high)
        right = pl.ds(pl.multiple_of(rows + j * wide, wide), wide)
        schur_ref[...] = gram_tile(yx_ref, yz_ref, left, right)

        @pl.when(j == 0)
        def _():
            front_ref[...] = schur_ref[:, :front_ref.shape[1]]

        @pl.when(i == 0)
        def _():
            top_ref[...] = schur_ref[:top_ref.shape[0], :]


def gram_tile(yx_ref, yz_ref, left, right):
    left_x, left_z = yx_ref[:, left, :], yz_ref[:, left, :]
    _, high, width = left_x.shape
    left_x, left_z = left_x.reshape(RANK * high, width), left_z.reshape(RANK * high, width)
    total = None
    for q in range(RANK):
        gx = dot_bf16(left_x, yx_ref[q, right, :], NT)
        gz = dot_bf16(left_z, yz_ref[q, right, :], NT)
        for r in range(RANK):
            term = gx[r * high:(r + 1) * high] * gz[r * high:(r + 1) * high]
            total = signed(total, term, q, r)
    return total


def signed(total, term, q, r):
    if total is None:
        return term
    return total + term if rank_signs[q] * rank_signs[r] > 0 else total - term


def assemble(place, slots, sources, x_factor, z_factor, rows, cols, lead_rows, lead_cols):
    _, parts, lanes = sources[0].shape
    slots_held = sum(source.shape[0] for source in sources)
    width = x_factor.shape[0]
    tile = 256
    high, wide = min(512, rows), min(256, cols)
    lead_tiles, pick_tiles = K // tile, slots.shape[0] // tile
    row_tiles, col_tiles = rows // high, cols // wide
    whole = pl.BlockSpec((width, width), lambda s: (0, 0), pipeline_mode=pl.Buffered(1))
    lead = pl.BlockSpec((RANK, tile, width), lambda s: (0, jnp.minimum(s, lead_tiles - 1), 0))
    after = lambda s: jnp.maximum(s - pick_tiles, 0)
    bf16 = jnp.bfloat16
    any_space = pl.BlockSpec(memory_space=pl.ANY)
    body = functools.partial(assemble_kernel, sources=len(sources), lead_tiles=lead_tiles, pick_tiles=pick_tiles, col_tiles=col_tiles, rows=rows, prow=K // lead_rows, pcol=K // lead_cols)
    return pl.pallas_call(
        body,
        grid=(pick_tiles + row_tiles * col_tiles,),
        out_shape=(jax.ShapeDtypeStruct((RANK, K, width), bf16),) * 2 + (
            jax.ShapeDtypeStruct((rows, cols), jnp.float32),
            jax.ShapeDtypeStruct((rows, lead_cols), jnp.float32),
            jax.ShapeDtypeStruct((lead_rows, cols), jnp.float32)),
        in_specs=[SMEM, SMEM, whole, whole] + [any_space] * len(sources),
        out_specs=(lead, lead,
                   pl.BlockSpec((high, wide), lambda s: (after(s) // col_tiles, after(s) % col_tiles)),
                   pl.BlockSpec((high, lead_cols), lambda s: (after(s) // col_tiles, 0)),
                   pl.BlockSpec((lead_rows, wide), lambda s: (0, jnp.minimum(after(s), col_tiles - 1)))),
        scratch_shapes=[pltpu.VMEM((slots_held, parts, lanes), bf16), pltpu.VMEM((tile, parts, lanes), bf16)]
        + [pltpu.VMEM((RANK, rows + cols, width), bf16)] * 2 + [pltpu.SemaphoreType.DMA((len(sources),))],
        compiler_params=pltpu.CompilerParams(vmem_limit_bytes=58 * MIB),
        cost_estimate=pl.CostEstimate(flops=28 * 10**9, bytes_accessed=30 * MIB, transcendentals=0),
    )(place, slots, x_factor, z_factor, *sources)


def factor_block(block, u_ref, v_ref, beside):
    count = BLK // SUB
    sub_iota = lax.broadcasted_iota(jnp.int32, (SUB, BLK), 0)
    lane_iota = lax.broadcasted_iota(jnp.int32, (SUB, BLK), 1)
    rows_a = [block[SUB * i:SUB * (i + 1), :] for i in range(count)]
    rows_v = [(lane_iota == sub_iota + SUB * i).astype(jnp.float32) for i in range(count)]

    def spread_lane(x, lane):
        return jnp.broadcast_to(x[:, lane:lane + 1], (SUB, BLK))

    def spread_row(x, row):
        return jnp.broadcast_to(x[row:row + 1, :], (SUB, BLK))

    for m in range(count):
        beside(m)
        head_a, head_v = rows_a[m], rows_v[m]
        cols = [spread_lane(head_a, SUB * m + k) for k in range(SUB)]
        below = [[spread_lane(rows_a[i], SUB * m + k) for k in range(SUB)] for i in range(m + 1, count)]
        scale = jnp.zeros((SUB, BLK), jnp.float32)
        for j in range(SUB):
            pivot = spread_row(cols[j], j)
            root = lax.rsqrt(pivot)
            scale = jnp.where(sub_iota == j, root, scale)
            mult = jnp.where(sub_iota > j, cols[j], 0.0) * root
            row_a = spread_row(head_a, j) * root
            row_v = spread_row(head_v, j) * root
            lead = [spread_row(cols[k], j) * root if k > j else None for k in range(SUB)]
            if j + 1 < SUB:
                head_a = head_a - mult * row_a
                head_v = head_v - mult * row_v
                for k in range(j + 1, SUB):
                    cols[k] = cols[k] - mult * lead[k]
            for n, i in enumerate(range(m + 1, count)):
                mult_i = below[n][j] * root
                rows_a[i] = rows_a[i] - mult_i * row_a
                rows_v[i] = rows_v[i] - mult_i * row_v
                for k in range(j + 1, SUB):
                    below[n][k] = below[n][k] - mult_i * lead[k]
        u = jnp.where(lane_iota >= sub_iota + SUB * m, head_a * scale, 0.0)
        v = jnp.where(lane_iota <= sub_iota + SUB * m, head_v * scale, 0.0)
        u_ref[SUB * m:SUB * (m + 1), :] = u
        v_ref[SUB * m:SUB * (m + 1), :] = v


def factor_kernel(yx_ref, yz_ref, lh_ref, ll_ref, d_ref, w_ref, g_ref, u_ref, v_ref):
    order = lh_ref.shape[0]
    steps = order // BLK
    tile = 2 * BLK
    window = 3 * BLK
    lh_ref[...] = jnp.zeros_like(lh_ref)
    ll_ref[...] = jnp.zeros_like(ll_ref)
    w_ref[:, tile:] = jnp.zeros((order, order - tile), jnp.float32)

    def rows_of(i, carry):
        left = pl.ds(pl.multiple_of(i * 2 * tile, 2 * tile), 2 * tile)
        w_ref[left, :tile] = gram_tile(yx_ref, yz_ref, left, pl.ds(0, tile))
        return carry
    lax.fori_loop(0, order // (2 * tile), rows_of, 0)

    def step(b, carry):
        at = pl.ds(pl.multiple_of(b * BLK, BLK), BLK)
        after = jnp.minimum(b // 2 + 1, order // tile - 1)
        top = pl.multiple_of(jnp.minimum(after * tile + (b % 2) * window, order - window), BLK)
        left = pl.ds(top, window)
        right = pl.ds(pl.multiple_of(after * tile, tile), tile)

        def beside(m):
            q, r = m // RANK, m % RANK
            term = dot_bf16(yx_ref[r, left, :], yx_ref[q, right, :], NT) * dot_bf16(yz_ref[r, left, :], yz_ref[q, right, :], NT)
            g_ref[left, :] = signed(g_ref[left, :] if m > 0 else None, term, q, r)

        factor_block(w_ref[at, at], u_ref, v_ref, beside)
        lh_ref[at, at], ll_ref[at, at] = split(u_ref[...].T)
        d_ref[at, :] = v_ref[...]
        for k in range(steps - 1):
            @pl.when(b == k)
            def _():
                first = (k + 1) * BLK
                column = slice(k * BLK, first)
                lh_ref[first:, column], ll_ref[first:, column] = split(dot3(split(w_ref[first:, column]), split(v_ref[...]), NT))
                for top in range(first, order, tile):
                    bottom = min(top + tile, order)
                    left = (lh_ref[top:bottom, column], ll_ref[top:bottom, column])
                    right = (lh_ref[first:bottom, column], ll_ref[first:bottom, column])
                    w_ref[top:bottom, first:bottom] = w_ref[top:bottom, first:bottom] - dot3(left, right, NT)
                if k % 2 == 1:
                    w_ref[first:, first:first + tile] = w_ref[first:, first:first + tile] + g_ref[first:, :]
        return carry
    lax.fori_loop(0, steps, step, 0)


def factor(yx, yz):
    tile = 2 * BLK
    f32 = jnp.float32
    return pl.pallas_call(
        factor_kernel,
        out_shape=(jax.ShapeDtypeStruct((K, K), jnp.bfloat16),) * 2 + (jax.ShapeDtypeStruct((K, BLK), f32),),
        in_specs=[VMEM] * 2,
        out_specs=(VMEM,) * 3,
        scratch_shapes=[pltpu.VMEM((K, K), f32), pltpu.VMEM((K, tile), f32), pltpu.VMEM((BLK, BLK), f32), pltpu.VMEM((BLK, BLK), f32)],
        compiler_params=pltpu.CompilerParams(vmem_limit_bytes=58 * MIB),
        cost_estimate=pl.CostEstimate(flops=40 * 10**9, bytes_accessed=12 * MIB, transcendentals=0),
    )(yx, yz)


def solve_kernel(place_ref, lh_any, ll_any, d_any, pieces_any, schur_any, *refs, prow):
    top_refs, refs = refs[:prow], refs[prow:]
    rest_ref, panel_ref, lh, ll, d_ref, pieces_ref, tops_ref, schur_ref, xh, xl, zh, zl, sem_ref = refs
    pcol = pieces_ref.shape[0]
    row, column = place_ref[0], place_ref[1]
    pairs = [(d_any, d_ref), (lh_any, lh), (ll_any, ll)]
    pairs += [(ref, tops_ref.at[turn ^ row]) for turn, ref in enumerate(top_refs)]
    pairs += [(pieces_any, pieces_ref), (schur_any, schur_ref)]
    copies = [pltpu.make_async_copy(here, there, sem_ref.at[n]) for n, (here, there) in enumerate(pairs)]
    for copy in copies:
        copy.start()
    for copy in copies[:3]:
        copy.wait()
    wide = 2 * BLK
    inverses = []
    for b in range(K // wide):
        upper, lower = slice(b * wide, b * wide + BLK), slice(b * wide + BLK, (b + 1) * wide)
        first, second = split(d_ref[upper, :]), split(d_ref[lower, :])
        between = dot3((lh[lower, upper], ll[lower, upper]), first, NN)
        corner = -dot3(second, split(between), NN)
        inverses.append(split(jnp.concatenate([
            jnp.concatenate([d_ref[upper, :], jnp.zeros((BLK, BLK), jnp.float32)], axis=1),
            jnp.concatenate([corner, d_ref[lower, :]], axis=1)], axis=0)))
    for copy in copies[3:-1]:
        copy.wait()
    for b in range(K // wide):
        at, done = slice(b * wide, (b + 1) * wide), slice(0, b * wide)
        blocks = range(wide // NB * b, wide // NB * (b + 1))
        value = jnp.concatenate([pieces_ref[n % pcol, :, n // pcol * NB:(n // pcol + 1) * NB] for n in blocks], axis=1)
        top = jnp.concatenate([tops_ref[n % prow, n // prow * NB:(n // prow + 1) * NB, :] for n in blocks], axis=0)
        if b > 0:
            left = (lh[at, done], ll[at, done])
            value = value - dot3((xh[:, done], xl[:, done]), left, NT)
            top = top - dot3(left, (zh[done, :], zl[done, :]), NN)
        value = dot3(split(value), inverses[b], NT)
        top = dot3(inverses[b], split(top), NN)
        xh[:, at], xl[:, at] = split(value)
        zh[at, :], zl[at, :] = split(top)
        for place, block in enumerate(blocks):
            @pl.when(column == block % pcol)
            def _():
                panel_ref[:, block // pcol * NB:(block // pcol + 1) * NB] = value[:, place * NB:(place + 1) * NB]
    copies[-1].wait()
    rest_ref[...] = schur_ref[...] - dot3((xh[...], xl[...]), (zh[...], zl[...]), NN)


def solve(place, high, low, inverses, pieces, schur, tops):
    rows, cols = schur.shape
    lead = K // pieces.shape[0]
    bf16, f32 = jnp.bfloat16, jnp.float32
    any_space = pl.BlockSpec(memory_space=pl.ANY)
    return pl.pallas_call(
        functools.partial(solve_kernel, prow=len(tops)),
        out_shape=(jax.ShapeDtypeStruct((rows, cols), f32), jax.ShapeDtypeStruct((rows, lead), f32)),
        in_specs=[SMEM] + [any_space] * (5 + len(tops)),
        out_specs=(VMEM, VMEM),
        scratch_shapes=[pltpu.VMEM((K, K), bf16)] * 2 + [pltpu.VMEM((K, BLK), f32), pltpu.VMEM(pieces.shape, f32)]
        + [pltpu.VMEM((len(tops),) + tops[0].shape, f32), pltpu.VMEM(schur.shape, f32)]
        + [pltpu.VMEM((rows, K), bf16)] * 2 + [pltpu.VMEM((K, cols), bf16)] * 2 + [pltpu.SemaphoreType.DMA((len(tops) + 5,))],
        compiler_params=pltpu.CompilerParams(vmem_limit_bytes=58 * MIB),
        cost_estimate=pl.CostEstimate(flops=12 * 10**9, bytes_accessed=24 * MIB, transcendentals=0),
    )(place, high, low, inverses, pieces, schur, *tops)


def gather_factors(mine, prow_count, pcol_count):
    own = mine.shape[0]
    half = own // 2

    def swap(axis, count, turn, value):
        return lax.ppermute(value, axis, [(n, n ^ turn) for n in range(count)])

    span = pcol_count // 2
    level_of = {j: bin(j).count("1") for j in range(1, span)}
    levels = max(level_of.values(), default=0)
    order = [0] + list(range(1, prow_count, 2)) + list(range(2, prow_count, 2))
    items = {0: mine}
    held = {turn: {} for turn in order}
    parts = []

    def spread(turn, j):
        low, high = j & -j, 1 << (j.bit_length() - 1)
        if low == high:
            return [swap("pcol", pcol_count, 2 * j, held[turn][0])]
        return [swap("pcol", pcol_count, 2 * high, held[turn][j ^ high][:half]), swap("pcol", pcol_count, 2 * low, held[turn][j ^ low][half:])]

    def take(turn, which):
        whole = jnp.concatenate([held[turn][j] for j in which]) if len(which) > 1 else held[turn][which[0]]
        parts.append((turn, which, whole, swap("pcol", pcol_count, 1, whole)))

    for phase in range(len(order) + levels - 1):
        moved = {}
        if phase < len(order):
            turn = order[phase]
            held[turn][0] = items[turn]
            if turn % 2 == 1 and turn > 1:
                moved["z", turn - 1] = [swap("prow", prow_count, 1, items[turn])]
        for level in range(1, levels + 1):
            if 0 <= phase - level + 1 < len(order):
                turn = order[phase - level + 1]
                for j in range(1, span):
                    if level_of[j] == level:
                        moved[turn, j] = spread(turn, j)
        if phase + 1 < len(order):
            turn = order[phase + 1]
            if turn % 2 == 1:
                moved["z", turn] = [swap("prow", prow_count, turn, mine)]
            elif turn in items:
                moved["z", turn] = [items[turn]]
        mine, *results = lax.optimization_barrier([mine] + [value for values in moved.values() for value in values])
        results = iter(results)
        for (turn, j), values in moved.items():
            arrived = [next(results) for _ in values]
            if turn == "z":
                items[j] = arrived[0]
            else:
                held[turn][j] = arrived[0] if len(arrived) == 1 else jnp.concatenate(arrived)
        if 0 <= phase - levels + 1 < len(order) - 1:
            take(order[phase - levels + 1], list(held[order[phase - levels + 1]]))
        if phase == len(order) + levels - 3:
            early = [j for j in held[order[-1]] if j == 0 or level_of[j] < levels]
            if len(early) == span or levels < 2:
                early = []
            else:
                take(order[-1], early)
    take(order[-1], [j for j in range(span) if j not in early])
    near = [whole for _, _, whole, _ in parts]
    far = [swapped for _, _, _, swapped in parts]
    places = [(turn, 2 * j) for turn, which, _, _ in parts for j in which]
    return near + far, places + [(turn, col + 1) for turn, col in places]


def places_of(placement, order, prow_id, pcol_id, pcol_count):
    total = placement.shape[0]
    own = total // len(order)
    unit_of = [0] * len(order)
    for unit, (row_turn, col_turn) in enumerate(order):
        unit_of[row_turn * pcol_count + col_turn] = unit
    holder = jnp.arange(len(order))
    turn = ((holder // pcol_count) ^ prow_id) * pcol_count + ((holder % pcol_count) ^ pcol_id)
    units = jnp.sum(jnp.where(turn[:, None] == jnp.arange(len(order))[None, :], jnp.array(unit_of)[None, :], 0), axis=1)
    place = (units[:, None] * own + jnp.arange(own)[None, :]).reshape(1, total)
    blocks = total // NB
    in_block = jnp.arange(blocks)[:, None] == placement[None, :] // NB
    digits = jnp.concatenate([jnp.where(in_block, place // NB, 0), jnp.where(in_block, place % NB, 0)]).astype(jnp.bfloat16)
    at_row = (jnp.arange(NB)[:, None] == placement[None, :] % NB).astype(jnp.bfloat16)
    found = dot_bf16(digits, at_row, NT).astype(jnp.int32)
    return found[:blocks] * NB + found[blocks:]


def per_device(factors, x_factor, zinv_factor, placement):
    prow_count = lax.axis_size("prow")
    pcol_count = lax.axis_size("pcol")
    total_rows = placement.shape[0]
    local_rows = total_rows // prow_count
    local_cols = total_rows // pcol_count
    prow_id = lax.axis_index("prow")
    pcol_id = lax.axis_index("pcol")
    _, own, width = factors.shape
    count = prow_count * pcol_count
    lanes = BLK
    mine = factors.transpose(1, 0, 2).reshape(own, RANK * width // lanes, lanes)
    sources, order = gather_factors(mine, prow_count, pcol_count)
    found = places_of(placement, order, prow_id, pcol_id, pcol_count)
    by_row = lax.dynamic_index_in_dim(found.reshape(local_rows // NB, prow_count, NB), prow_id, 1, keepdims=False)
    by_col = lax.dynamic_index_in_dim(found.reshape(local_cols // NB, pcol_count, NB), pcol_id, 1, keepdims=False)
    lead_rows, lead_cols = K // prow_count, K // pcol_count
    places = jnp.concatenate([found[:K // NB], by_row[lead_rows // NB:], by_col[lead_cols // NB:]])
    places = jnp.pad(places, ((0, -places.shape[0] % (256 // NB)), (0, 0))).reshape(-1)
    place = jnp.stack([prow_id, pcol_id]).astype(jnp.int32)
    lead_x, lead_z, schur_local, front, top = assemble(
        place, places.astype(jnp.int32), sources, x_factor, zinv_factor, local_rows, local_cols, lead_rows, lead_cols)
    pieces = lax.all_gather(front, "pcol", axis=0, tiled=False)
    tops = [top] + [lax.ppermute(top, "prow", [(n, n ^ turn) for n in range(prow_count)]) for turn in range(1, prow_count)]
    high, low, inverses = factor(lead_x, lead_z)
    return solve(place, high, low, inverses, pieces, schur_local, tops)


def solution(mesh):
    in_specs = (P(None, ("prow", "pcol"), None), P(), P(), P())
    out_specs = (P("prow", "pcol"), P("prow", "pcol"))
    return jax.shard_map(
        per_device, mesh=mesh, in_specs=in_specs, out_specs=out_specs, check_vma=False
    )
```

```python
import functools

import jax
import jax.numpy as jnp
from jax import lax
from jax.experimental import pallas as pl
from jax.experimental.pallas import tpu as pltpu
from jax.sharding import PartitionSpec as P

RANK = 4
NB = 64
K = 1024
SUB = 8
BLK = 128
MIB = 2**20

rank_signs = (1.0, 1.0, -1.0, -1.0)
NT = ((1,), (1,))
NN = ((1,), (0,))
VMEM = pl.BlockSpec(memory_space=pltpu.VMEM)
SMEM = pl.BlockSpec(memory_space=pltpu.SMEM)


def split(x):
    hi = x.astype(jnp.bfloat16)
    lo = (x - hi.astype(jnp.float32)).astype(jnp.bfloat16)
    return hi, lo


def dot_bf16(a, b, dims):
    return lax.dot_general(a, b, (dims, ((), ())), preferred_element_type=jnp.float32)


def dot3(a, b, dims):
    return dot_bf16(a[0], b[0], dims) + (dot_bf16(a[0], b[1], dims) + dot_bf16(a[1], b[0], dims))


def assemble_kernel(place_ref, slots_ref, x_ref, z_ref, *refs, sources, lead_tiles, pick_tiles, row_tiles, rows, prow, pcol):
    source_refs, refs = refs[:sources], refs[sources:]
    lead_x_ref, lead_z_ref, early_ref, front_ref, top_ref, rest_x, rest_z, every_ref, picked_ref, yx_ref, yz_ref, sem_ref = refs
    step = pl.program_id(0)
    tile, parts, lanes = picked_ref.shape
    width = x_ref.shape[0]
    per_rank = width // lanes

    @pl.when(step == 0)
    def _():
        copies, first = [], 0
        for n, ref in enumerate(source_refs):
            copies.append(pltpu.make_async_copy(ref, every_ref.at[pl.ds(first, ref.shape[0])], sem_ref.at[n]))
            first += ref.shape[0]
        for copy in copies:
            copy.start()
        for copy in copies:
            copy.wait()

    @pl.when(step < pick_tiles)
    def _():
        def pick(group, carry):
            for k in range(16):
                i = group * 16 + k
                picked_ref[i] = every_ref[slots_ref[step * tile + i]]
            return carry
        lax.fori_loop(0, tile // 16, pick, 0)
        by_part = jnp.swapaxes(picked_ref[...], 0, 1)
        mine = jnp.concatenate([
            jnp.concatenate([by_part[r * per_rank + k] for k in range(per_rank)], axis=1) for r in range(RANK)], axis=0)
        images_x = dot_bf16(mine, x_ref[...], NN).astype(jnp.bfloat16).reshape(RANK, tile, width)
        images_z = dot_bf16(mine, z_ref[...], NN).astype(jnp.bfloat16).reshape(RANK, tile, width)

        def keep(block, s):
            at = pl.ds(pl.multiple_of(block * NB, NB), NB)
            yx_ref[:, at, :] = images_x[:, s * NB:(s + 1) * NB, :]
            yz_ref[:, at, :] = images_z[:, s * NB:(s + 1) * NB, :]

        @pl.when(step < lead_tiles)
        def _():
            lead_x_ref[...], lead_z_ref[...] = images_x, images_z
            for s in range(tile // NB):
                block = step * (tile // NB) + s

                @pl.when(block % prow == place_ref[0])
                def _():
                    keep(block // prow, s)

                @pl.when(block % pcol == place_ref[1])
                def _():
                    keep(rows // NB + block // pcol, s)

        @pl.when(step >= lead_tiles)
        def _():
            lead = K // NB
            row_rest, col_rest = rows // NB - lead // prow, (yx_ref.shape[1] - rows) // NB - lead // pcol
            for s in range(tile // NB):
                block = (step - lead_tiles) * (tile // NB) + s

                @pl.when(block < row_rest + col_rest)
                def _():
                    keep(jnp.where(block < row_rest, lead // prow + block, rows // NB + lead // pcol + block - row_rest), s)

    skipped, wide = top_ref.shape[0], early_ref.shape[1]
    kept, beyond = rows - skipped, rows + wide
    hand_over = []
    for n, (mine, out) in enumerate(((yx_ref, rest_x), (yz_ref, rest_z))):
        count = mine.shape[1] - beyond
        hand_over.append(pltpu.make_async_copy(mine.at[:, pl.ds(skipped, kept), :], out.at[:, pl.ds(0, kept), :], sem_ref.at[sources + 2 * n]))
        hand_over.append(pltpu.make_async_copy(mine.at[:, pl.ds(beyond, count), :], out.at[:, pl.ds(kept, count), :], sem_ref.at[sources + 2 * n + 1]))

    @pl.when(step == pick_tiles)
    def _():
        for copy in hand_over:
            copy.start()

    @pl.when((step >= pick_tiles) & (step < pick_tiles + row_tiles))
    def _():
        high = early_ref.shape[0]
        i = step - pick_tiles
        left = pl.ds(pl.multiple_of(i * high, high), high)
        early_ref[...] = gram_tile(yx_ref, yz_ref, left, pl.ds(rows, wide))
        front_ref[...] = early_ref[:, :front_ref.shape[1]]

        @pl.when(i == 0)
        def _():
            top_ref[:, :wide] = early_ref[:skipped, :]

    @pl.when(step == pick_tiles + row_tiles)
    def _():
        top_ref[:, wide:] = gram_tile(yx_ref, yz_ref, pl.ds(0, skipped), pl.ds(beyond, top_ref.shape[1] - wide))
        for copy in hand_over:
            copy.wait()


def gram_tile(yx_ref, yz_ref, left, right):
    left_x, left_z = yx_ref[:, left, :], yz_ref[:, left, :]
    _, high, width = left_x.shape
    left_x, left_z = left_x.reshape(RANK * high, width), left_z.reshape(RANK * high, width)
    total = None
    for q in range(RANK):
        gx = dot_bf16(left_x, yx_ref[q, right, :], NT)
        gz = dot_bf16(left_z, yz_ref[q, right, :], NT)
        for r in range(RANK):
            term = gx[r * high:(r + 1) * high] * gz[r * high:(r + 1) * high]
            total = signed(total, term, q, r)
    return total


def signed(total, term, q, r):
    if total is None:
        return term
    return total + term if rank_signs[q] * rank_signs[r] > 0 else total - term


def assemble(place, slots, sources, x_factor, z_factor, rows, cols, lead_rows, lead_cols):
    _, parts, lanes = sources[0].shape
    slots_held = sum(source.shape[0] for source in sources)
    width = x_factor.shape[0]
    tile = 256
    high, wide = min(512, rows), cols // 2
    lead_tiles, pick_tiles = K // tile, slots.shape[0] // tile
    row_tiles = rows // high
    whole = pl.BlockSpec((width, width), lambda s: (0, 0), pipeline_mode=pl.Buffered(1))
    lead = pl.BlockSpec((RANK, tile, width), lambda s: (0, jnp.minimum(s, lead_tiles - 1), 0))
    tile_of = lambda s: (jnp.clip(s - pick_tiles, 0, row_tiles - 1), 0)
    handed = jax.ShapeDtypeStruct((RANK, rows - lead_rows + cols - wide, width), jnp.bfloat16)
    bf16 = jnp.bfloat16
    any_space = pl.BlockSpec(memory_space=pl.ANY)
    body = functools.partial(assemble_kernel, sources=len(sources), lead_tiles=lead_tiles, pick_tiles=pick_tiles, row_tiles=row_tiles, rows=rows, prow=K // lead_rows, pcol=K // lead_cols)
    return pl.pallas_call(
        body,
        grid=(pick_tiles + row_tiles + 1,),
        out_shape=(jax.ShapeDtypeStruct((RANK, K, width), bf16),) * 2 + (
            jax.ShapeDtypeStruct((rows, wide), jnp.float32),
            jax.ShapeDtypeStruct((rows, lead_cols), jnp.float32),
            jax.ShapeDtypeStruct((lead_rows, cols), jnp.float32), handed, handed),
        in_specs=[SMEM, SMEM, whole, whole] + [any_space] * len(sources),
        out_specs=(lead, lead,
                   pl.BlockSpec((high, wide), tile_of),
                   pl.BlockSpec((high, lead_cols), tile_of),
                   pl.BlockSpec((lead_rows, cols), lambda s: (0, 0)), any_space, any_space),
        scratch_shapes=[pltpu.VMEM((slots_held, parts, lanes), bf16), pltpu.VMEM((tile, parts, lanes), bf16)]
        + [pltpu.VMEM((RANK, rows + cols, width), bf16)] * 2 + [pltpu.SemaphoreType.DMA((len(sources) + 4,))],
        compiler_params=pltpu.CompilerParams(vmem_limit_bytes=58 * MIB),
        cost_estimate=pl.CostEstimate(flops=28 * 10**9, bytes_accessed=30 * MIB, transcendentals=0),
    )(place, slots, x_factor, z_factor, *sources)


def factor_block(block, u_ref, v_ref, beside):
    count = BLK // SUB
    sub_iota = lax.broadcasted_iota(jnp.int32, (SUB, BLK), 0)
    lane_iota = lax.broadcasted_iota(jnp.int32, (SUB, BLK), 1)
    rows_a = [block[SUB * i:SUB * (i + 1), :] for i in range(count)]
    rows_v = [(lane_iota == sub_iota + SUB * i).astype(jnp.float32) for i in range(count)]

    def spread_lane(x, lane):
        return jnp.broadcast_to(x[:, lane:lane + 1], (SUB, BLK))

    def spread_row(x, row):
        return jnp.broadcast_to(x[row:row + 1, :], (SUB, BLK))

    for m in range(count):
        beside(m)
        head_a, head_v = rows_a[m], rows_v[m]
        cols = [spread_lane(head_a, SUB * m + k) for k in range(SUB)]
        below = [[spread_lane(rows_a[i], SUB * m + k) for k in range(SUB)] for i in range(m + 1, count)]
        scale = jnp.zeros((SUB, BLK), jnp.float32)
        for j in range(SUB):
            pivot = spread_row(cols[j], j)
            root = lax.rsqrt(pivot)
            scale = jnp.where(sub_iota == j, root, scale)
            mult = jnp.where(sub_iota > j, cols[j], 0.0) * root
            row_a = spread_row(head_a, j) * root
            row_v = spread_row(head_v, j) * root
            lead = [spread_row(cols[k], j) * root if k > j else None for k in range(SUB)]
            if j + 1 < SUB:
                head_a = head_a - mult * row_a
                head_v = head_v - mult * row_v
                for k in range(j + 1, SUB):
                    cols[k] = cols[k] - mult * lead[k]
            for n, i in enumerate(range(m + 1, count)):
                mult_i = below[n][j] * root
                rows_a[i] = rows_a[i] - mult_i * row_a
                rows_v[i] = rows_v[i] - mult_i * row_v
                for k in range(j + 1, SUB):
                    below[n][k] = below[n][k] - mult_i * lead[k]
        u = jnp.where(lane_iota >= sub_iota + SUB * m, head_a * scale, 0.0)
        v = jnp.where(lane_iota <= sub_iota + SUB * m, head_v * scale, 0.0)
        u_ref[SUB * m:SUB * (m + 1), :] = u
        v_ref[SUB * m:SUB * (m + 1), :] = v


def factor_kernel(yx_ref, yz_ref, rest_x_any, rest_z_any, lh_ref, ll_ref, d_ref, rest_ref, w_ref, g_ref, u_ref, v_ref, rest_x, rest_z, sem_ref):
    order = lh_ref.shape[0]
    steps = order // BLK
    tile = 2 * BLK
    rest_rows, rest_cols = rest_ref.shape
    fetched = [pltpu.make_async_copy(here, there, sem_ref.at[n]) for n, (here, there) in enumerate(((rest_x_any, rest_x), (rest_z_any, rest_z)))]
    for copy in fetched:
        copy.start()
    lh_ref[...] = jnp.zeros_like(lh_ref)
    ll_ref[...] = jnp.zeros_like(ll_ref)
    w_ref[:, tile:] = jnp.zeros((order, order - tile), jnp.float32)

    def rows_of(i, carry):
        left = pl.ds(pl.multiple_of(i * 2 * tile, 2 * tile), 2 * tile)
        w_ref[left, :tile] = gram_tile(yx_ref, yz_ref, left, pl.ds(0, tile))
        return carry
    lax.fori_loop(0, order // (2 * tile), rows_of, 0)

    def step(b, window, share):
        at = pl.ds(pl.multiple_of(b * BLK, BLK), BLK)
        after = jnp.minimum(b // 2 + 1, order // tile - 1)
        left = pl.ds(pl.multiple_of(jnp.minimum(after * tile + (b % 2) * window, order - window), BLK), window)
        right = pl.ds(pl.multiple_of(after * tile, tile), tile)
        if share > 0:
            part = pl.ds(pl.multiple_of((b - 2) * share, share), share)

        def pair(x_ref, z_ref, lhs, rhs, q, r):
            return dot_bf16(x_ref[r, lhs, :], x_ref[q, rhs, :], NT) * dot_bf16(z_ref[r, lhs, :], z_ref[q, rhs, :], NT)

        def beside(m):
            q, r = m // RANK, m % RANK
            g_ref[left, :] = signed(g_ref[left, :] if m > 0 else None, pair(yx_ref, yz_ref, left, right, q, r), q, r)
            if share > 0:
                term = pair(rest_x, rest_z, part, pl.ds(rest_rows, rest_cols), q, r)
                rest_ref[part, :] = signed(rest_ref[part, :] if m > 0 else None, term, q, r)

        factor_block(w_ref[at, at], u_ref, v_ref, beside)
        lh_ref[at, at], ll_ref[at, at] = split(u_ref[...].T)
        d_ref[at, :] = v_ref[...]
        for k in range(steps - 1):
            @pl.when(b == k)
            def _():
                first = (k + 1) * BLK
                column = slice(k * BLK, first)
                lh_ref[first:, column], ll_ref[first:, column] = split(dot3(split(w_ref[first:, column]), split(v_ref[...]), NT))
                for top in range(first, order, tile):
                    bottom = min(top + tile, order)
                    left = (lh_ref[top:bottom, column], ll_ref[top:bottom, column])
                    right = (lh_ref[first:bottom, column], ll_ref[first:bottom, column])
                    w_ref[top:bottom, first:bottom] = w_ref[top:bottom, first:bottom] - dot3(left, right, NT)
                if k % 2 == 1:
                    w_ref[first:, first:first + tile] = w_ref[first:, first:first + tile] + g_ref[first:, :]

    def first_step(b, carry):
        step(b, 3 * BLK, 0)
        return carry

    def later_step(b, carry):
        step(b, 2 * BLK, rest_rows // (steps - 2))
        return carry

    lax.fori_loop(0, 2, first_step, 0)
    for copy in fetched:
        copy.wait()
    lax.fori_loop(2, steps, later_step, 0)


def factor(yx, yz, rest_x, rest_z, rest_rows):
    tile = 2 * BLK
    f32 = jnp.float32
    any_space = pl.BlockSpec(memory_space=pl.ANY)
    rest_cols = rest_x.shape[1] - rest_rows
    return pl.pallas_call(
        factor_kernel,
        out_shape=(jax.ShapeDtypeStruct((K, K), jnp.bfloat16),) * 2 + (jax.ShapeDtypeStruct((K, BLK), f32), jax.ShapeDtypeStruct((rest_rows, rest_cols), f32)),
        in_specs=[VMEM] * 2 + [any_space] * 2,
        out_specs=(VMEM,) * 4,
        scratch_shapes=[pltpu.VMEM((K, K), f32), pltpu.VMEM((K, tile), f32), pltpu.VMEM((BLK, BLK), f32), pltpu.VMEM((BLK, BLK), f32)]
        + [pltpu.VMEM(rest_x.shape, jnp.bfloat16)] * 2 + [pltpu.SemaphoreType.DMA((2,))],
        compiler_params=pltpu.CompilerParams(vmem_limit_bytes=58 * MIB),
        cost_estimate=pl.CostEstimate(flops=40 * 10**9, bytes_accessed=12 * MIB, transcendentals=0),
    )(yx, yz, rest_x, rest_z)


def solve_kernel(place_ref, lh_any, ll_any, d_any, pieces_any, early_any, last_any, *refs, prow):
    top_refs, refs = refs[:prow], refs[prow:]
    rest_ref, panel_ref, lh, ll, d_ref, pieces_ref, tops_ref, schur_ref, xh, xl, zh, zl, sem_ref = refs
    pcol = pieces_ref.shape[0]
    row, column = place_ref[0], place_ref[1]
    pairs = [(d_any, d_ref), (lh_any, lh), (ll_any, ll)]
    pairs += [(ref, tops_ref.at[turn ^ row]) for turn, ref in enumerate(top_refs)]
    skipped, halfway = tops_ref.shape[1], early_any.shape[1]
    left, right = pl.ds(0, halfway), pl.ds(halfway, schur_ref.shape[1] - halfway)
    pairs += [(pieces_any, pieces_ref), (early_any, schur_ref.at[:, left]), (top_refs[0].at[:, right], schur_ref.at[pl.ds(0, skipped), right]),
              (last_any, schur_ref.at[pl.ds(skipped, schur_ref.shape[0] - skipped), right])]
    copies = [pltpu.make_async_copy(here, there, sem_ref.at[n]) for n, (here, there) in enumerate(pairs)]
    for copy in copies:
        copy.start()
    for copy in copies[:3]:
        copy.wait()
    wide = 2 * BLK
    inverses = []
    for b in range(K // wide):
        upper, lower = slice(b * wide, b * wide + BLK), slice(b * wide + BLK, (b + 1) * wide)
        first, second = split(d_ref[upper, :]), split(d_ref[lower, :])
        between = dot3((lh[lower, upper], ll[lower, upper]), first, NN)
        corner = -dot3(second, split(between), NN)
        inverses.append(split(jnp.concatenate([
            jnp.concatenate([d_ref[upper, :], jnp.zeros((BLK, BLK), jnp.float32)], axis=1),
            jnp.concatenate([corner, d_ref[lower, :]], axis=1)], axis=0)))
    for copy in copies[3:-3]:
        copy.wait()
    for b in range(K // wide):
        at, done = slice(b * wide, (b + 1) * wide), slice(0, b * wide)
        blocks = range(wide // NB * b, wide // NB * (b + 1))
        value = jnp.concatenate([pieces_ref[n % pcol, :, n // pcol * NB:(n // pcol + 1) * NB] for n in blocks], axis=1)
        top = jnp.concatenate([tops_ref[n % prow, n // prow * NB:(n // prow + 1) * NB, :] for n in blocks], axis=0)
        if b > 0:
            left = (lh[at, done], ll[at, done])
            value = value - dot3((xh[:, done], xl[:, done]), left, NT)
            top = top - dot3(left, (zh[done, :], zl[done, :]), NN)
        value = dot3(split(value), inverses[b], NT)
        top = dot3(inverses[b], split(top), NN)
        xh[:, at], xl[:, at] = split(value)
        zh[at, :], zl[at, :] = split(top)
        for place, block in enumerate(blocks):
            @pl.when(column == block % pcol)
            def _():
                panel_ref[:, block // pcol * NB:(block // pcol + 1) * NB] = value[:, place * NB:(place + 1) * NB]
    for copy in copies[-3:]:
        copy.wait()
    rest_ref[...] = schur_ref[...] - dot3((xh[...], xl[...]), (zh[...], zl[...]), NN)


def solve(place, high, low, inverses, pieces, early, last, tops):
    rows, cols = early.shape[0], tops[0].shape[1]
    lead = K // pieces.shape[0]
    bf16, f32 = jnp.bfloat16, jnp.float32
    any_space = pl.BlockSpec(memory_space=pl.ANY)
    return pl.pallas_call(
        functools.partial(solve_kernel, prow=len(tops)),
        out_shape=(jax.ShapeDtypeStruct((rows, cols), f32), jax.ShapeDtypeStruct((rows, lead), f32)),
        in_specs=[SMEM] + [any_space] * (6 + len(tops)),
        out_specs=(VMEM, VMEM),
        scratch_shapes=[pltpu.VMEM((K, K), bf16)] * 2 + [pltpu.VMEM((K, BLK), f32), pltpu.VMEM(pieces.shape, f32)]
        + [pltpu.VMEM((len(tops),) + tops[0].shape, f32), pltpu.VMEM((rows, cols), f32)]
        + [pltpu.VMEM((rows, K), bf16)] * 2 + [pltpu.VMEM((K, cols), bf16)] * 2 + [pltpu.SemaphoreType.DMA((len(tops) + 7,))],
        compiler_params=pltpu.CompilerParams(vmem_limit_bytes=58 * MIB),
        cost_estimate=pl.CostEstimate(flops=12 * 10**9, bytes_accessed=24 * MIB, transcendentals=0),
    )(place, high, low, inverses, pieces, early, last, *tops)


def gather_factors(mine, prow_count, pcol_count):
    own = mine.shape[0]
    half = own // 2

    def swap(axis, count, turn, value):
        return lax.ppermute(value, axis, [(n, n ^ turn) for n in range(count)])

    span = pcol_count // 2
    level_of = {j: bin(j).count("1") for j in range(1, span)}
    levels = max(level_of.values(), default=0)
    order = [0] + list(range(1, prow_count, 2)) + list(range(2, prow_count, 2))
    items = {0: mine}
    held = {turn: {} for turn in order}
    parts = []

    def spread(turn, j):
        low, high = j & -j, 1 << (j.bit_length() - 1)
        if low == high:
            return [swap("pcol", pcol_count, 2 * j, held[turn][0])]
        return [swap("pcol", pcol_count, 2 * high, held[turn][j ^ high][:half]), swap("pcol", pcol_count, 2 * low, held[turn][j ^ low][half:])]

    def take(turn, which):
        whole = jnp.concatenate([held[turn][j] for j in which]) if len(which) > 1 else held[turn][which[0]]
        parts.append((turn, which, whole, swap("pcol", pcol_count, 1, whole)))

    for phase in range(len(order) + levels - 1):
        moved = {}
        if phase < len(order):
            turn = order[phase]
            held[turn][0] = items[turn]
            if turn % 2 == 1 and turn > 1:
                moved["z", turn - 1] = [swap("prow", prow_count, 1, items[turn])]
        for level in range(1, levels + 1):
            if 0 <= phase - level + 1 < len(order):
                turn = order[phase - level + 1]
                for j in range(1, span):
                    if level_of[j] == level:
                        moved[turn, j] = spread(turn, j)
        if phase + 1 < len(order):
            turn = order[phase + 1]
            if turn % 2 == 1:
                moved["z", turn] = [swap("prow", prow_count, turn, mine)]
            elif turn in items:
                moved["z", turn] = [items[turn]]
        mine, *results = lax.optimization_barrier([mine] + [value for values in moved.values() for value in values])
        results = iter(results)
        for (turn, j), values in moved.items():
            arrived = [next(results) for _ in values]
            if turn == "z":
                items[j] = arrived[0]
            else:
                held[turn][j] = arrived[0] if len(arrived) == 1 else jnp.concatenate(arrived)
        if 0 <= phase - levels + 1 < len(order) - 1:
            take(order[phase - levels + 1], list(held[order[phase - levels + 1]]))
        if phase == len(order) + levels - 3:
            early = [j for j in held[order[-1]] if j == 0 or level_of[j] < levels]
            if len(early) == span or levels < 2:
                early = []
            else:
                take(order[-1], early)
    take(order[-1], [j for j in range(span) if j not in early])
    near = [whole for _, _, whole, _ in parts]
    far = [swapped for _, _, _, swapped in parts]
    places = [(turn, 2 * j) for turn, which, _, _ in parts for j in which]
    return near + far, places + [(turn, col + 1) for turn, col in places]


def places_of(placement, order, prow_id, pcol_id, pcol_count):
    total = placement.shape[0]
    own = total // len(order)
    unit_of = [0] * len(order)
    for unit, (row_turn, col_turn) in enumerate(order):
        unit_of[row_turn * pcol_count + col_turn] = unit
    holder = jnp.arange(len(order))
    turn = ((holder // pcol_count) ^ prow_id) * pcol_count + ((holder % pcol_count) ^ pcol_id)
    units = jnp.sum(jnp.where(turn[:, None] == jnp.arange(len(order))[None, :], jnp.array(unit_of)[None, :], 0), axis=1)
    place = (units[:, None] * own + jnp.arange(own)[None, :]).reshape(1, total)
    blocks = total // NB
    in_block = jnp.arange(blocks)[:, None] == placement[None, :] // NB
    digits = jnp.concatenate([jnp.where(in_block, place // NB, 0), jnp.where(in_block, place % NB, 0)]).astype(jnp.bfloat16)
    at_row = (jnp.arange(NB)[:, None] == placement[None, :] % NB).astype(jnp.bfloat16)
    found = dot_bf16(digits, at_row, NT).astype(jnp.int32)
    return found[:blocks] * NB + found[blocks:]


def per_device(factors, x_factor, zinv_factor, placement):
    prow_count = lax.axis_size("prow")
    pcol_count = lax.axis_size("pcol")
    total_rows = placement.shape[0]
    local_rows = total_rows // prow_count
    local_cols = total_rows // pcol_count
    prow_id = lax.axis_index("prow")
    pcol_id = lax.axis_index("pcol")
    _, own, width = factors.shape
    count = prow_count * pcol_count
    lanes = BLK
    mine = factors.transpose(1, 0, 2).reshape(own, RANK * width // lanes, lanes)
    sources, order = gather_factors(mine, prow_count, pcol_count)
    found = places_of(placement, order, prow_id, pcol_id, pcol_count)
    by_row = lax.dynamic_index_in_dim(found.reshape(local_rows // NB, prow_count, NB), prow_id, 1, keepdims=False)
    by_col = lax.dynamic_index_in_dim(found.reshape(local_cols // NB, pcol_count, NB), pcol_id, 1, keepdims=False)
    lead_rows, lead_cols = K // prow_count, K // pcol_count
    places = jnp.concatenate([found[:K // NB], by_row[lead_rows // NB:], by_col[lead_cols // NB:]])
    places = jnp.pad(places, ((0, -places.shape[0] % (256 // NB)), (0, 0))).reshape(-1)
    place = jnp.stack([prow_id, pcol_id]).astype(jnp.int32)
    lead_x, lead_z, early, front, top, rest_x, rest_z = assemble(
        place, places.astype(jnp.int32), sources, x_factor, zinv_factor, local_rows, local_cols, lead_rows, lead_cols)
    pieces = lax.all_gather(front, "pcol", axis=0, tiled=False)
    tops = [top] + [lax.ppermute(top, "prow", [(n, n ^ turn) for n in range(prow_count)]) for turn in range(1, prow_count)]
    high, low, inverses, last = factor(lead_x, lead_z, rest_x, rest_z, local_rows - lead_rows)
    return solve(place, high, low, inverses, pieces, early, last, tops)


def solution(mesh):
    in_specs = (P(None, ("prow", "pcol"), None), P(), P(), P())
    out_specs = (P("prow", "pcol"), P("prow", "pcol"))
    return jax.shard_map(
        per_device, mesh=mesh, in_specs=in_specs, out_specs=out_specs, check_vma=False
    )
```

```python
import functools

import jax
import jax.numpy as jnp
from jax import lax
from jax.experimental import pallas as pl
from jax.experimental.pallas import tpu as pltpu
from jax.sharding import PartitionSpec as P

RANK = 4
NB = 64
K = 1024
SUB = 8
BLK = 128
MIB = 2**20

rank_signs = (1.0, 1.0, -1.0, -1.0)
NT = ((1,), (1,))
NN = ((1,), (0,))
VMEM = pl.BlockSpec(memory_space=pltpu.VMEM)
SMEM = pl.BlockSpec(memory_space=pltpu.SMEM)


def split(x):
    hi = x.astype(jnp.bfloat16)
    lo = (x - hi.astype(jnp.float32)).astype(jnp.bfloat16)
    return hi, lo


def dot_bf16(a, b, dims):
    return lax.dot_general(a, b, (dims, ((), ())), preferred_element_type=jnp.float32)


def dot3(a, b, dims):
    return dot_bf16(a[0], b[0], dims) + (dot_bf16(a[0], b[1], dims) + dot_bf16(a[1], b[0], dims))


def assemble_kernel(place_ref, slots_ref, x_ref, z_ref, *refs, sources, lead_tiles, pick_tiles, col_tiles, rows, prow, pcol):
    source_refs, refs = refs[:sources], refs[sources:]
    lead_x_ref, lead_z_ref, schur_ref, front_ref, top_ref, every_ref, picked_ref, yx_ref, yz_ref, sem_ref = refs
    step = pl.program_id(0)
    tile, parts, lanes = picked_ref.shape
    width = x_ref.shape[0]
    per_rank = width // lanes

    @pl.when(step == 0)
    def _():
        copies, first = [], 0
        for n, ref in enumerate(source_refs):
            copies.append(pltpu.make_async_copy(ref, every_ref.at[pl.ds(first, ref.shape[0])], sem_ref.at[n]))
            first += ref.shape[0]
        for copy in copies:
            copy.start()
        for copy in copies:
            copy.wait()

    @pl.when(step < pick_tiles)
    def _():
        def pick(group, carry):
            for k in range(16):
                i = group * 16 + k
                picked_ref[i] = every_ref[slots_ref[step * tile + i]]
            return carry
        lax.fori_loop(0, tile // 16, pick, 0)
        by_part = jnp.swapaxes(picked_ref[...], 0, 1)
        mine = jnp.concatenate([
            jnp.concatenate([by_part[r * per_rank + k] for k in range(per_rank)], axis=1) for r in range(RANK)], axis=0)
        images_x = dot_bf16(mine, x_ref[...], NN).astype(jnp.bfloat16).reshape(RANK, tile, width)
        images_z = dot_bf16(mine, z_ref[...], NN).astype(jnp.bfloat16).reshape(RANK, tile, width)

        def keep(block, s):
            at = pl.ds(pl.multiple_of(block * NB, NB), NB)
            yx_ref[:, at, :] = images_x[:, s * NB:(s + 1) * NB, :]
            yz_ref[:, at, :] = images_z[:, s * NB:(s + 1) * NB, :]

        @pl.when(step < lead_tiles)
        def _():
            lead_x_ref[...], lead_z_ref[...] = images_x, images_z
            for s in range(tile // NB):
                block = step * (tile // NB) + s

                @pl.when(block % prow == place_ref[0])
                def _():
                    keep(block // prow, s)

                @pl.when(block % pcol == place_ref[1])
                def _():
                    keep(rows // NB + block // pcol, s)

        @pl.when(step >= lead_tiles)
        def _():
            lead = K // NB
            row_rest, col_rest = rows // NB - lead // prow, (yx_ref.shape[1] - rows) // NB - lead // pcol
            for s in range(tile // NB):
                block = (step - lead_tiles) * (tile // NB) + s

                @pl.when(block < row_rest + col_rest)
                def _():
                    keep(jnp.where(block < row_rest, lead // prow + block, rows // NB + lead // pcol + block - row_rest), s)

    @pl.when(step >= pick_tiles)
    def _():
        high, wide = schur_ref.shape
        i, j = (step - pick_tiles) // col_tiles, (step - pick_tiles) % col_tiles
        left = pl.ds(pl.multiple_of(i * high, high), high)
        right = pl.ds(pl.multiple_of(rows + j * wide, wide), wide)
        schur_ref[...] = gram_tile(yx_ref, yz_ref, left, right)

        @pl.when(j == 0)
        def _():
            front_ref[...] = schur_ref[:, :front_ref.shape[1]]

        @pl.when(i == 0)
        def _():
            top_ref[...] = schur_ref[:top_ref.shape[0], :]


def gram_tile(yx_ref, yz_ref, left, right):
    left_x, left_z = yx_ref[:, left, :], yz_ref[:, left, :]
    _, high, width = left_x.shape
    left_x, left_z = left_x.reshape(RANK * high, width), left_z.reshape(RANK * high, width)
    total = None
    for q in range(RANK):
        gx = dot_bf16(left_x, yx_ref[q, right, :], NT)
        gz = dot_bf16(left_z, yz_ref[q, right, :], NT)
        for r in range(RANK):
            term = gx[r * high:(r + 1) * high] * gz[r * high:(r + 1) * high]
            total = signed(total, term, q, r)
    return total


def signed(total, term, q, r):
    if total is None:
        return term
    return total + term if rank_signs[q] * rank_signs[r] > 0 else total - term


def assemble(place, slots, sources, x_factor, z_factor, rows, cols, lead_rows, lead_cols):
    _, parts, lanes = sources[0].shape
    slots_held = sum(source.shape[0] for source in sources)
    width = x_factor.shape[0]
    tile = 256
    high, wide = min(512, rows), min(256, cols)
    lead_tiles, pick_tiles = K // tile, slots.shape[0] // tile
    row_tiles, col_tiles = rows // high, cols // wide
    whole = pl.BlockSpec((width, width), lambda s: (0, 0), pipeline_mode=pl.Buffered(1))
    lead = pl.BlockSpec((RANK, tile, width), lambda s: (0, jnp.minimum(s, lead_tiles - 1), 0))
    after = lambda s: jnp.maximum(s - pick_tiles, 0)
    bf16 = jnp.bfloat16
    any_space = pl.BlockSpec(memory_space=pl.ANY)
    body = functools.partial(assemble_kernel, sources=len(sources), lead_tiles=lead_tiles, pick_tiles=pick_tiles, col_tiles=col_tiles, rows=rows, prow=K // lead_rows, pcol=K // lead_cols)
    return pl.pallas_call(
        body,
        grid=(pick_tiles + row_tiles * col_tiles,),
        out_shape=(jax.ShapeDtypeStruct((RANK, K, width), bf16),) * 2 + (
            jax.ShapeDtypeStruct((rows, cols), jnp.float32),
            jax.ShapeDtypeStruct((rows, lead_cols), jnp.float32),
            jax.ShapeDtypeStruct((lead_rows, cols), jnp.float32)),
        in_specs=[SMEM, SMEM, whole, whole] + [any_space] * len(sources),
        out_specs=(lead, lead,
                   pl.BlockSpec((high, wide), lambda s: (after(s) // col_tiles, after(s) % col_tiles)),
                   pl.BlockSpec((high, lead_cols), lambda s: (after(s) // col_tiles, 0)),
                   pl.BlockSpec((lead_rows, wide), lambda s: (0, jnp.minimum(after(s), col_tiles - 1)))),
        scratch_shapes=[pltpu.VMEM((slots_held, parts, lanes), bf16), pltpu.VMEM((tile, parts, lanes), bf16)]
        + [pltpu.VMEM((RANK, rows + cols, width), bf16)] * 2 + [pltpu.SemaphoreType.DMA((len(sources),))],
        compiler_params=pltpu.CompilerParams(vmem_limit_bytes=58 * MIB),
        cost_estimate=pl.CostEstimate(flops=28 * 10**9, bytes_accessed=30 * MIB, transcendentals=0),
    )(place, slots, x_factor, z_factor, *sources)


def factor_block(block, u_ref, v_ref, beside):
    count = BLK // SUB
    sub_iota = lax.broadcasted_iota(jnp.int32, (SUB, BLK), 0)
    lane_iota = lax.broadcasted_iota(jnp.int32, (SUB, BLK), 1)
    rows_a = [block[SUB * i:SUB * (i + 1), :] for i in range(count)]
    rows_v = [(lane_iota == sub_iota + SUB * i).astype(jnp.float32) for i in range(count)]

    def spread_lane(x, lane):
        return jnp.broadcast_to(x[:, lane:lane + 1], (SUB, BLK))

    def spread_row(x, row):
        return jnp.broadcast_to(x[row:row + 1, :], (SUB, BLK))

    for m in range(count):
        beside(m)
        head_a, head_v = rows_a[m], rows_v[m]
        cols = [spread_lane(head_a, SUB * m + k) for k in range(SUB)]
        below = [[spread_lane(rows_a[i], SUB * m + k) for k in range(SUB)] for i in range(m + 1, count)]
        scale = jnp.zeros((SUB, BLK), jnp.float32)
        for j in range(SUB):
            pivot = spread_row(cols[j], j)
            root = lax.rsqrt(pivot)
            scale = jnp.where(sub_iota == j, root, scale)
            mult = jnp.where(sub_iota > j, cols[j], 0.0) * root
            row_a = spread_row(head_a, j) * root
            row_v = spread_row(head_v, j) * root
            lead = [spread_row(cols[k], j) * root if k > j else None for k in range(SUB)]
            if j + 1 < SUB:
                head_a = head_a - mult * row_a
                head_v = head_v - mult * row_v
                for k in range(j + 1, SUB):
                    cols[k] = cols[k] - mult * lead[k]
            for n, i in enumerate(range(m + 1, count)):
                mult_i = below[n][j] * root
                rows_a[i] = rows_a[i] - mult_i * row_a
                rows_v[i] = rows_v[i] - mult_i * row_v
                for k in range(j + 1, SUB):
                    below[n][k] = below[n][k] - mult_i * lead[k]
        u = jnp.where(lane_iota >= sub_iota + SUB * m, head_a * scale, 0.0)
        v = jnp.where(lane_iota <= sub_iota + SUB * m, head_v * scale, 0.0)
        u_ref[SUB * m:SUB * (m + 1), :] = u
        v_ref[SUB * m:SUB * (m + 1), :] = v


def factor_kernel(yx_ref, yz_ref, lh_ref, ll_ref, d_ref, w_ref, g_ref, u_ref, v_ref):
    order = lh_ref.shape[0]
    steps = order // BLK
    tile = 2 * BLK
    lh_ref[...] = jnp.zeros_like(lh_ref)
    ll_ref[...] = jnp.zeros_like(ll_ref)
    w_ref[:, tile:] = jnp.zeros((order, order - tile), jnp.float32)

    def rows_of(i, carry):
        left = pl.ds(pl.multiple_of(i * 2 * tile, 2 * tile), 2 * tile)
        w_ref[left, :tile] = gram_tile(yx_ref, yz_ref, left, pl.ds(0, tile))
        return carry
    lax.fori_loop(0, order // (2 * tile), rows_of, 0)

    def step(b, ahead, window):
        at = pl.ds(pl.multiple_of(b * BLK, BLK), BLK)
        left = pl.ds(pl.multiple_of(ahead * tile + (b % 2) * window, BLK), window)
        right = slice(ahead * tile, (ahead + 1) * tile)

        def beside(m):
            if window > 0:
                q, r = m // RANK, m % RANK
                term = dot_bf16(yx_ref[r, left, :], yx_ref[q, right, :], NT) * dot_bf16(yz_ref[r, left, :], yz_ref[q, right, :], NT)
                g_ref[left, :] = signed(g_ref[left, :] if m > 0 else None, term, q, r)

        factor_block(w_ref[at, at], u_ref, v_ref, beside)
        lh_ref[at, at], ll_ref[at, at] = split(u_ref[...].T)
        d_ref[at, :] = v_ref[...]
        for k in range(2 * ahead - 2, min(2 * ahead, steps - 1)):
            @pl.when(b == k)
            def _():
                first = (k + 1) * BLK
                column = slice(k * BLK, first)
                lh_ref[first:, column], ll_ref[first:, column] = split(dot3(split(w_ref[first:, column]), split(v_ref[...]), NT))
                for top in range(first, order, tile):
                    bottom = min(top + tile, order)
                    left = (lh_ref[top:bottom, column], ll_ref[top:bottom, column])
                    right = (lh_ref[first:bottom, column], ll_ref[first:bottom, column])
                    w_ref[top:bottom, first:bottom] = w_ref[top:bottom, first:bottom] - dot3(left, right, NT)
                if k % 2 == 1:
                    w_ref[first:, first:first + tile] = w_ref[first:, first:first + tile] + g_ref[first:, :]

    for ahead in range(1, order // tile + 1):
        def two_steps(b, carry, ahead=ahead):
            step(b, ahead, (order - ahead * tile) // 2)
            return carry
        lax.fori_loop(2 * ahead - 2, 2 * ahead, two_steps, 0)


def factor(yx, yz):
    tile = 2 * BLK
    f32 = jnp.float32
    return pl.pallas_call(
        factor_kernel,
        out_shape=(jax.ShapeDtypeStruct((K, K), jnp.bfloat16),) * 2 + (jax.ShapeDtypeStruct((K, BLK), f32),),
        in_specs=[VMEM] * 2,
        out_specs=(VMEM,) * 3,
        scratch_shapes=[pltpu.VMEM((K, K), f32), pltpu.VMEM((K, tile), f32), pltpu.VMEM((BLK, BLK), f32), pltpu.VMEM((BLK, BLK), f32)],
        compiler_params=pltpu.CompilerParams(vmem_limit_bytes=58 * MIB),
        cost_estimate=pl.CostEstimate(flops=40 * 10**9, bytes_accessed=12 * MIB, transcendentals=0),
    )(yx, yz)


def solve_kernel(place_ref, lh_any, ll_any, d_any, pieces_any, schur_any, *refs, prow):
    top_refs, refs = refs[:prow], refs[prow:]
    rest_ref, panel_ref, lh, ll, d_ref, pieces_ref, tops_ref, schur_ref, xh, xl, zh, zl, sem_ref = refs
    pcol = pieces_ref.shape[0]
    row, column = place_ref[0], place_ref[1]
    pairs = [(d_any, d_ref), (lh_any, lh), (ll_any, ll)]
    pairs += [(ref, tops_ref.at[turn ^ row]) for turn, ref in enumerate(top_refs)]
    pairs += [(pieces_any, pieces_ref), (schur_any, schur_ref)]
    copies = [pltpu.make_async_copy(here, there, sem_ref.at[n]) for n, (here, there) in enumerate(pairs)]
    for copy in copies:
        copy.start()
    for copy in copies[:3]:
        copy.wait()
    wide = 2 * BLK
    inverses = []
    for b in range(K // wide):
        upper, lower = slice(b * wide, b * wide + BLK), slice(b * wide + BLK, (b + 1) * wide)
        first, second = split(d_ref[upper, :]), split(d_ref[lower, :])
        between = dot3((lh[lower, upper], ll[lower, upper]), first, NN)
        corner = -dot3(second, split(between), NN)
        inverses.append(split(jnp.concatenate([
            jnp.concatenate([d_ref[upper, :], jnp.zeros((BLK, BLK), jnp.float32)], axis=1),
            jnp.concatenate([corner, d_ref[lower, :]], axis=1)], axis=0)))
    for copy in copies[3:-1]:
        copy.wait()
    for b in range(K // wide):
        at, done = slice(b * wide, (b + 1) * wide), slice(0, b * wide)
        blocks = range(wide // NB * b, wide // NB * (b + 1))
        value = jnp.concatenate([pieces_ref[n % pcol, :, n // pcol * NB:(n // pcol + 1) * NB] for n in blocks], axis=1)
        top = jnp.concatenate([tops_ref[n % prow, n // prow * NB:(n // prow + 1) * NB, :] for n in blocks], axis=0)
        if b > 0:
            left = (lh[at, done], ll[at, done])
            value = value - dot3((xh[:, done], xl[:, done]), left, NT)
            top = top - dot3(left, (zh[done, :], zl[done, :]), NN)
        value = dot3(split(value), inverses[b], NT)
        top = dot3(inverses[b], split(top), NN)
        xh[:, at], xl[:, at] = split(value)
        zh[at, :], zl[at, :] = split(top)
        for place, block in enumerate(blocks):
            @pl.when(column == block % pcol)
            def _():
                panel_ref[:, block // pcol * NB:(block // pcol + 1) * NB] = value[:, place * NB:(place + 1) * NB]
    copies[-1].wait()
    rest_ref[...] = schur_ref[...] - dot3((xh[...], xl[...]), (zh[...], zl[...]), NN)


def solve(place, high, low, inverses, pieces, schur, tops):
    rows, cols = schur.shape
    lead = K // pieces.shape[0]
    bf16, f32 = jnp.bfloat16, jnp.float32
    any_space = pl.BlockSpec(memory_space=pl.ANY)
    return pl.pallas_call(
        functools.partial(solve_kernel, prow=len(tops)),
        out_shape=(jax.ShapeDtypeStruct((rows, cols), f32), jax.ShapeDtypeStruct((rows, lead), f32)),
        in_specs=[SMEM] + [any_space] * (5 + len(tops)),
        out_specs=(VMEM, VMEM),
        scratch_shapes=[pltpu.VMEM((K, K), bf16)] * 2 + [pltpu.VMEM((K, BLK), f32), pltpu.VMEM(pieces.shape, f32)]
        + [pltpu.VMEM((len(tops),) + tops[0].shape, f32), pltpu.VMEM(schur.shape, f32)]
        + [pltpu.VMEM((rows, K), bf16)] * 2 + [pltpu.VMEM((K, cols), bf16)] * 2 + [pltpu.SemaphoreType.DMA((len(tops) + 5,))],
        compiler_params=pltpu.CompilerParams(vmem_limit_bytes=58 * MIB),
        cost_estimate=pl.CostEstimate(flops=12 * 10**9, bytes_accessed=24 * MIB, transcendentals=0),
    )(place, high, low, inverses, pieces, schur, *tops)


def gather_factors(mine, prow_count, pcol_count, prow_id):
    own = mine.shape[0]
    half = own // 2

    def swap(axis, count, turn, value, chosen=lambda n: True):
        return lax.ppermute(value, axis, [(n, n ^ turn) for n in range(count) if chosen(n)])

    def close(n):
        return abs(n - (n ^ 3)) == 1

    span = pcol_count // 2
    level_of = {j: bin(j).count("1") for j in range(1, span)}
    levels = max(level_of.values(), default=0)
    order = [0] + list(range(1, prow_count, 2)) + list(range(2, prow_count, 2))
    items = {0: mine}
    held = {turn: {} for turn in order}
    split_turn = 3 if prow_count == 4 else None
    if split_turn:
        middle = swap("prow", prow_count, split_turn, mine, close)
    parts = []

    def spread(turn, j):
        low, high = j & -j, 1 << (j.bit_length() - 1)
        if low == high:
            return [swap("pcol", pcol_count, 2 * j, held[turn][0])]
        return [swap("pcol", pcol_count, 2 * high, held[turn][j ^ high][:half]), swap("pcol", pcol_count, 2 * low, held[turn][j ^ low][half:])]

    def take(turn, which):
        whole = jnp.concatenate([held[turn][j] for j in which]) if len(which) > 1 else held[turn][which[0]]
        parts.append((turn, which, whole, swap("pcol", pcol_count, 1, whole)))

    for phase in range(len(order) + levels - 1):
        moved = {}
        if phase < len(order):
            turn = order[phase]
            held[turn][0] = items[turn]
            if turn % 2 == 1 and turn > 1:
                moved["z", turn - 1] = [swap("prow", prow_count, 1, items[turn])]
        for level in range(1, levels + 1):
            if 0 <= phase - level + 1 < len(order):
                turn = order[phase - level + 1]
                for j in range(1, span):
                    if level_of[j] == level:
                        moved[turn, j] = spread(turn, j)
        if phase + 1 < len(order):
            turn = order[phase + 1]
            if turn % 2 == 1:
                if turn == split_turn:
                    moved["z", turn] = [swap("prow", prow_count, turn, mine, lambda n: not close(n))]
                else:
                    moved["z", turn] = [swap("prow", prow_count, turn, mine)]
            elif turn in items:
                moved["z", turn] = [items[turn]]
        if phase == 0 and split_turn:
            moved["middle", split_turn] = [middle]
        mine, *results = lax.optimization_barrier([mine] + [value for values in moved.values() for value in values])
        results = iter(results)
        for (turn, j), values in moved.items():
            arrived = [next(results) for _ in values]
            if turn == "middle":
                middle = arrived[0]
            elif turn == "z" and j == split_turn:
                items[j] = jnp.where(close(prow_id), middle, arrived[0])
            elif turn == "z":
                items[j] = arrived[0]
            else:
                held[turn][j] = arrived[0] if len(arrived) == 1 else jnp.concatenate(arrived)
        if 0 <= phase - levels + 1 < len(order) - 1:
            take(order[phase - levels + 1], list(held[order[phase - levels + 1]]))
        if phase == len(order) + levels - 3:
            early = [j for j in held[order[-1]] if j == 0 or level_of[j] < levels]
            if len(early) == span or levels < 2:
                early = []
            else:
                take(order[-1], early)
    take(order[-1], [j for j in range(span) if j not in early])
    near = [whole for _, _, whole, _ in parts]
    far = [swapped for _, _, _, swapped in parts]
    places = [(turn, 2 * j) for turn, which, _, _ in parts for j in which]
    return near + far, places + [(turn, col + 1) for turn, col in places]


def places_of(placement, order, prow_id, pcol_id, pcol_count):
    total = placement.shape[0]
    own = total // len(order)
    unit_of = [0] * len(order)
    for unit, (row_turn, col_turn) in enumerate(order):
        unit_of[row_turn * pcol_count + col_turn] = unit
    holder = jnp.arange(len(order))
    turn = ((holder // pcol_count) ^ prow_id) * pcol_count + ((holder % pcol_count) ^ pcol_id)
    units = jnp.sum(jnp.where(turn[:, None] == jnp.arange(len(order))[None, :], jnp.array(unit_of)[None, :], 0), axis=1)
    place = (units[:, None] * own + jnp.arange(own)[None, :]).reshape(1, total)
    blocks = total // NB
    in_block = jnp.arange(blocks)[:, None] == placement[None, :] // NB
    digits = jnp.concatenate([jnp.where(in_block, place // NB, 0), jnp.where(in_block, place % NB, 0)]).astype(jnp.bfloat16)
    at_row = (jnp.arange(NB)[:, None] == placement[None, :] % NB).astype(jnp.bfloat16)
    found = dot_bf16(digits, at_row, NT).astype(jnp.int32)
    return found[:blocks] * NB + found[blocks:]


def per_device(factors, x_factor, zinv_factor, placement):
    prow_count = lax.axis_size("prow")
    pcol_count = lax.axis_size("pcol")
    total_rows = placement.shape[0]
    local_rows = total_rows // prow_count
    local_cols = total_rows // pcol_count
    prow_id = lax.axis_index("prow")
    pcol_id = lax.axis_index("pcol")
    _, own, width = factors.shape
    count = prow_count * pcol_count
    lanes = BLK
    mine = factors.transpose(1, 0, 2).reshape(own, RANK * width // lanes, lanes)
    sources, order = gather_factors(mine, prow_count, pcol_count, prow_id)
    found = places_of(placement, order, prow_id, pcol_id, pcol_count)
    by_row = lax.dynamic_index_in_dim(found.reshape(local_rows // NB, prow_count, NB), prow_id, 1, keepdims=False)
    by_col = lax.dynamic_index_in_dim(found.reshape(local_cols // NB, pcol_count, NB), pcol_id, 1, keepdims=False)
    lead_rows, lead_cols = K // prow_count, K // pcol_count
    places = jnp.concatenate([found[:K // NB], by_row[lead_rows // NB:], by_col[lead_cols // NB:]])
    places = jnp.pad(places, ((0, -places.shape[0] % (256 // NB)), (0, 0))).reshape(-1)
    place = jnp.stack([prow_id, pcol_id]).astype(jnp.int32)
    lead_x, lead_z, schur_local, front, top = assemble(
        place, places.astype(jnp.int32), sources, x_factor, zinv_factor, local_rows, local_cols, lead_rows, lead_cols)
    pieces = lax.all_gather(front, "pcol", axis=0, tiled=False)
    tops = [top] + [lax.ppermute(top, "prow", [(n, n ^ turn) for n in range(prow_count)]) for turn in range(1, prow_count)]
    high, low, inverses = factor(lead_x, lead_z)
    return solve(place, high, low, inverses, pieces, schur_local, tops)


def solution(mesh):
    in_specs = (P(None, ("prow", "pcol"), None), P(), P(), P())
    out_specs = (P("prow", "pcol"), P("prow", "pcol"))
    return jax.shard_map(
        per_device, mesh=mesh, in_specs=in_specs, out_specs=out_specs, check_vma=False
    )
```

```python
import functools

import jax
import jax.numpy as jnp
from jax import lax
from jax.experimental import pallas as pl
from jax.experimental.pallas import tpu as pltpu
from jax.sharding import PartitionSpec as P

RANK = 4
NB = 64
K = 1024
SUB = 8
BLK = 128
MIB = 2**20

rank_signs = (1.0, 1.0, -1.0, -1.0)
NT = ((1,), (1,))
NN = ((1,), (0,))
VMEM = pl.BlockSpec(memory_space=pltpu.VMEM)
SMEM = pl.BlockSpec(memory_space=pltpu.SMEM)


def split(x):
    hi = x.astype(jnp.bfloat16)
    lo = (x - hi.astype(jnp.float32)).astype(jnp.bfloat16)
    return hi, lo


def dot_bf16(a, b, dims):
    return lax.dot_general(a, b, (dims, ((), ())), preferred_element_type=jnp.float32)


def dot3(a, b, dims):
    return dot_bf16(a[0], b[0], dims) + (dot_bf16(a[0], b[1], dims) + dot_bf16(a[1], b[0], dims))


def assemble_kernel(place_ref, slots_ref, x_ref, z_ref, *refs, sources, lead_tiles, pick_tiles, col_tiles, rows, prow, pcol):
    source_refs, refs = refs[:sources], refs[sources:]
    lead_x_ref, lead_z_ref, schur_ref, front_ref, top_ref, every_ref, picked_ref, yx_ref, yz_ref, sem_ref = refs
    step = pl.program_id(0)
    tile, parts, lanes = picked_ref.shape
    width = x_ref.shape[0]
    per_rank = width // lanes

    @pl.when(step == 0)
    def _():
        copies, first = [], 0
        for n, ref in enumerate(source_refs):
            copies.append(pltpu.make_async_copy(ref, every_ref.at[pl.ds(first, ref.shape[0])], sem_ref.at[n]))
            first += ref.shape[0]
        for copy in copies:
            copy.start()
        for copy in copies:
            copy.wait()

    @pl.when(step < pick_tiles)
    def _():
        def pick(group, carry):
            for k in range(16):
                i = group * 16 + k
                picked_ref[i] = every_ref[slots_ref[step * tile + i]]
            return carry
        lax.fori_loop(0, tile // 16, pick, 0)
        by_part = jnp.swapaxes(picked_ref[...], 0, 1)
        mine = jnp.concatenate([
            jnp.concatenate([by_part[r * per_rank + k] for k in range(per_rank)], axis=1) for r in range(RANK)], axis=0)
        images_x = dot_bf16(mine, x_ref[...], NN).astype(jnp.bfloat16).reshape(RANK, tile, width)
        images_z = dot_bf16(mine, z_ref[...], NN).astype(jnp.bfloat16).reshape(RANK, tile, width)

        def keep(block, s):
            at = pl.ds(pl.multiple_of(block * NB, NB), NB)
            yx_ref[:, at, :] = images_x[:, s * NB:(s + 1) * NB, :]
            yz_ref[:, at, :] = images_z[:, s * NB:(s + 1) * NB, :]

        @pl.when(step < lead_tiles)
        def _():
            lead_x_ref[...], lead_z_ref[...] = images_x, images_z
            for s in range(tile // NB):
                block = step * (tile // NB) + s

                @pl.when(block % prow == place_ref[0])
                def _():
                    keep(block // prow, s)

                @pl.when(block % pcol == place_ref[1])
                def _():
                    keep(rows // NB + block // pcol, s)

        @pl.when(step >= lead_tiles)
        def _():
            lead = K // NB
            row_rest, col_rest = rows // NB - lead // prow, (yx_ref.shape[1] - rows) // NB - lead // pcol
            for s in range(tile // NB):
                block = (step - lead_tiles) * (tile // NB) + s

                @pl.when(block < row_rest + col_rest)
                def _():
                    keep(jnp.where(block < row_rest, lead // prow + block, rows // NB + lead // pcol + block - row_rest), s)

    @pl.when(step >= pick_tiles)
    def _():
        high, wide = schur_ref.shape
        i, j = (step - pick_tiles) // col_tiles, (step - pick_tiles) % col_tiles
        left = pl.ds(pl.multiple_of(i * high, high), high)
        right = pl.ds(pl.multiple_of(rows + j * wide, wide), wide)
        schur_ref[...] = gram_tile(yx_ref, yz_ref, left, right)

        @pl.when(j == 0)
        def _():
            front_ref[...] = schur_ref[:, :front_ref.shape[1]]

        @pl.when(i == 0)
        def _():
            top_ref[...] = schur_ref[:top_ref.shape[0], :]


def gram_tile(yx_ref, yz_ref, left, right):
    left_x, left_z = yx_ref[:, left, :], yz_ref[:, left, :]
    _, high, width = left_x.shape
    left_x, left_z = left_x.reshape(RANK * high, width), left_z.reshape(RANK * high, width)
    total = None
    for q in range(RANK):
        gx = dot_bf16(left_x, yx_ref[q, right, :], NT)
        gz = dot_bf16(left_z, yz_ref[q, right, :], NT)
        for r in range(RANK):
            term = gx[r * high:(r + 1) * high] * gz[r * high:(r + 1) * high]
            total = signed(total, term, q, r)
    return total


def signed(total, term, q, r):
    if total is None:
        return term
    return total + term if rank_signs[q] * rank_signs[r] > 0 else total - term


def assemble(place, slots, sources, x_factor, z_factor, rows, cols, lead_rows, lead_cols):
    _, parts, lanes = sources[0].shape
    slots_held = sum(source.shape[0] for source in sources)
    width = x_factor.shape[0]
    tile = 256
    high, wide = min(512, rows), min(256, cols)
    lead_tiles, pick_tiles = K // tile, slots.shape[0] // tile
    row_tiles, col_tiles = rows // high, cols // wide
    whole = pl.BlockSpec((width, width), lambda s: (0, 0), pipeline_mode=pl.Buffered(1))
    lead = pl.BlockSpec((RANK, tile, width), lambda s: (0, jnp.minimum(s, lead_tiles - 1), 0))
    after = lambda s: jnp.maximum(s - pick_tiles, 0)
    bf16 = jnp.bfloat16
    any_space = pl.BlockSpec(memory_space=pl.ANY)
    body = functools.partial(assemble_kernel, sources=len(sources), lead_tiles=lead_tiles, pick_tiles=pick_tiles, col_tiles=col_tiles, rows=rows, prow=K // lead_rows, pcol=K // lead_cols)
    return pl.pallas_call(
        body,
        grid=(pick_tiles + row_tiles * col_tiles,),
        out_shape=(jax.ShapeDtypeStruct((RANK, K, width), bf16),) * 2 + (
            jax.ShapeDtypeStruct((rows, cols), jnp.float32),
            jax.ShapeDtypeStruct((rows, lead_cols), jnp.float32),
            jax.ShapeDtypeStruct((lead_rows, cols), jnp.float32)),
        in_specs=[SMEM, SMEM, whole, whole] + [any_space] * len(sources),
        out_specs=(lead, lead,
                   pl.BlockSpec((high, wide), lambda s: (after(s) // col_tiles, after(s) % col_tiles)),
                   pl.BlockSpec((high, lead_cols), lambda s: (after(s) // col_tiles, 0)),
                   pl.BlockSpec((lead_rows, wide), lambda s: (0, jnp.minimum(after(s), col_tiles - 1)))),
        scratch_shapes=[pltpu.VMEM((slots_held, parts, lanes), bf16), pltpu.VMEM((tile, parts, lanes), bf16)]
        + [pltpu.VMEM((RANK, rows + cols, width), bf16)] * 2 + [pltpu.SemaphoreType.DMA((len(sources),))],
        compiler_params=pltpu.CompilerParams(vmem_limit_bytes=58 * MIB),
        cost_estimate=pl.CostEstimate(flops=28 * 10**9, bytes_accessed=30 * MIB, transcendentals=0),
    )(place, slots, x_factor, z_factor, *sources)


def factor_block(block, u_ref, v_ref, beside):
    count = BLK // SUB
    sub_iota = lax.broadcasted_iota(jnp.int32, (SUB, BLK), 0)
    lane_iota = lax.broadcasted_iota(jnp.int32, (SUB, BLK), 1)
    rows_a = [block[SUB * i:SUB * (i + 1), :] for i in range(count)]
    rows_v = [(lane_iota == sub_iota + SUB * i).astype(jnp.float32) for i in range(count)]

    def spread_lane(x, lane):
        return jnp.broadcast_to(x[:, lane:lane + 1], (SUB, BLK))

    def spread_row(x, row):
        return jnp.broadcast_to(x[row:row + 1, :], (SUB, BLK))

    for m in range(count):
        beside(m)
        head_a, head_v = rows_a[m], rows_v[m]
        cols = [spread_lane(head_a, SUB * m + k) for k in range(SUB)]
        below = [[spread_lane(rows_a[i], SUB * m + k) for k in range(SUB)] for i in range(m + 1, count)]
        scale = jnp.zeros((SUB, BLK), jnp.float32)
        for j in range(SUB):
            pivot = spread_row(cols[j], j)
            root = lax.rsqrt(pivot)
            scale = jnp.where(sub_iota == j, root, scale)
            mult = jnp.where(sub_iota > j, cols[j], 0.0) * root
            row_a = spread_row(head_a, j) * root
            row_v = spread_row(head_v, j) * root
            lead = [spread_row(cols[k], j) * root if k > j else None for k in range(SUB)]
            if j + 1 < SUB:
                head_a = head_a - mult * row_a
                head_v = head_v - mult * row_v
                for k in range(j + 1, SUB):
                    cols[k] = cols[k] - mult * lead[k]
            for n, i in enumerate(range(m + 1, count)):
                mult_i = below[n][j] * root
                rows_a[i] = rows_a[i] - mult_i * row_a
                rows_v[i] = rows_v[i] - mult_i * row_v
                for k in range(j + 1, SUB):
                    below[n][k] = below[n][k] - mult_i * lead[k]
        u = jnp.where(lane_iota >= sub_iota + SUB * m, head_a * scale, 0.0)
        v = jnp.where(lane_iota <= sub_iota + SUB * m, head_v * scale, 0.0)
        u_ref[SUB * m:SUB * (m + 1), :] = u
        v_ref[SUB * m:SUB * (m + 1), :] = v


def factor_kernel(yx_ref, yz_ref, lh_ref, ll_ref, d_ref, w_ref, g_ref, u_ref, v_ref):
    order = lh_ref.shape[0]
    steps = order // BLK
    tile = 2 * BLK
    window = 3 * BLK
    lh_ref[...] = jnp.zeros_like(lh_ref)
    ll_ref[...] = jnp.zeros_like(ll_ref)
    w_ref[:, tile:] = jnp.zeros((order, order - tile), jnp.float32)

    def rows_of(i, carry):
        left = pl.ds(pl.multiple_of(i * tile, tile), tile)
        w_ref[left, :tile] = gram_tile(yx_ref, yz_ref, left, pl.ds(0, tile))
        return carry
    lax.fori_loop(0, order // tile, rows_of, 0)

    def step(b, carry):
        at = pl.ds(pl.multiple_of(b * BLK, BLK), BLK)
        after = jnp.minimum(b // 2 + 1, order // tile - 1)
        top = pl.multiple_of(jnp.minimum(after * tile + (b % 2) * window, order - window), BLK)
        left = pl.ds(top, window)
        right = pl.ds(pl.multiple_of(after * tile, tile), tile)

        def beside(m):
            q, r = m // RANK, m % RANK
            term = dot_bf16(yx_ref[r, left, :], yx_ref[q, right, :], NT) * dot_bf16(yz_ref[r, left, :], yz_ref[q, right, :], NT)
            g_ref[left, :] = signed(g_ref[left, :] if m > 0 else None, term, q, r)

        factor_block(w_ref[at, at], u_ref, v_ref, beside)
        lh_ref[at, at], ll_ref[at, at] = split(u_ref[...].T)
        d_ref[at, :] = v_ref[...]
        for k in range(steps - 1):
            @pl.when(b == k)
            def _():
                first = (k + 1) * BLK
                column = slice(k * BLK, first)
                lh_ref[first:, column], ll_ref[first:, column] = split(dot3(split(w_ref[first:, column]), split(v_ref[...]), NT))
                for top in range(first, order, tile):
                    bottom = min(top + tile, order)
                    left = (lh_ref[top:bottom, column], ll_ref[top:bottom, column])
                    right = (lh_ref[first:bottom, column], ll_ref[first:bottom, column])
                    w_ref[top:bottom, first:bottom] = w_ref[top:bottom, first:bottom] - dot3(left, right, NT)
                if k % 2 == 1:
                    w_ref[first:, first:first + tile] = w_ref[first:, first:first + tile] + g_ref[first:, :]
        return carry
    lax.fori_loop(0, steps, step, 0)


def factor(yx, yz):
    tile = 2 * BLK
    f32 = jnp.float32
    return pl.pallas_call(
        factor_kernel,
        out_shape=(jax.ShapeDtypeStruct((K, K), jnp.bfloat16),) * 2 + (jax.ShapeDtypeStruct((K, BLK), f32),),
        in_specs=[VMEM] * 2,
        out_specs=(VMEM,) * 3,
        scratch_shapes=[pltpu.VMEM((K, K), f32), pltpu.VMEM((K, tile), f32), pltpu.VMEM((BLK, BLK), f32), pltpu.VMEM((BLK, BLK), f32)],
        compiler_params=pltpu.CompilerParams(vmem_limit_bytes=58 * MIB),
        cost_estimate=pl.CostEstimate(flops=40 * 10**9, bytes_accessed=12 * MIB, transcendentals=0),
    )(yx, yz)


def solve_kernel(place_ref, lh_any, ll_any, d_any, pieces_any, schur_any, *refs, prow):
    top_refs, refs = refs[:prow], refs[prow:]
    rest_ref, panel_ref, lh, ll, d_ref, pieces_ref, tops_ref, schur_ref, xh, xl, zh, zl, sem_ref = refs
    pcol = pieces_ref.shape[0]
    row, column = place_ref[0], place_ref[1]
    pairs = [(d_any, d_ref), (lh_any, lh), (ll_any, ll)]
    pairs += [(ref, tops_ref.at[turn ^ row]) for turn, ref in enumerate(top_refs)]
    pairs += [(pieces_any, pieces_ref), (schur_any, schur_ref)]
    copies = [pltpu.make_async_copy(here, there, sem_ref.at[n]) for n, (here, there) in enumerate(pairs)]
    for copy in copies:
        copy.start()
    for copy in copies[:3]:
        copy.wait()
    wide = 2 * BLK
    inverses = []
    for b in range(K // wide):
        upper, lower = slice(b * wide, b * wide + BLK), slice(b * wide + BLK, (b + 1) * wide)
        first, second = split(d_ref[upper, :]), split(d_ref[lower, :])
        between = dot3((lh[lower, upper], ll[lower, upper]), first, NN)
        corner = -dot3(second, split(between), NN)
        inverses.append(split(jnp.concatenate([
            jnp.concatenate([d_ref[upper, :], jnp.zeros((BLK, BLK), jnp.float32)], axis=1),
            jnp.concatenate([corner, d_ref[lower, :]], axis=1)], axis=0)))
    for copy in copies[3:-1]:
        copy.wait()
    for b in range(K // wide):
        at, done = slice(b * wide, (b + 1) * wide), slice(0, b * wide)
        blocks = range(wide // NB * b, wide // NB * (b + 1))
        value = jnp.concatenate([pieces_ref[n % pcol, :, n // pcol * NB:(n // pcol + 1) * NB] for n in blocks], axis=1)
        top = jnp.concatenate([tops_ref[n % prow, n // prow * NB:(n // prow + 1) * NB, :] for n in blocks], axis=0)
        if b > 0:
            left = (lh[at, done], ll[at, done])
            value = value - dot3((xh[:, done], xl[:, done]), left, NT)
            top = top - dot3(left, (zh[done, :], zl[done, :]), NN)
        value = dot3(split(value), inverses[b], NT)
        top = dot3(inverses[b], split(top), NN)
        xh[:, at], xl[:, at] = split(value)
        zh[at, :], zl[at, :] = split(top)
        for place, block in enumerate(blocks):
            @pl.when(column == block % pcol)
            def _():
                panel_ref[:, block // pcol * NB:(block // pcol + 1) * NB] = value[:, place * NB:(place + 1) * NB]
    copies[-1].wait()
    rest_ref[...] = schur_ref[...] - dot3((xh[...], xl[...]), (zh[...], zl[...]), NN)


def solve(place, high, low, inverses, pieces, schur, tops):
    rows, cols = schur.shape
    lead = K // pieces.shape[0]
    bf16, f32 = jnp.bfloat16, jnp.float32
    any_space = pl.BlockSpec(memory_space=pl.ANY)
    return pl.pallas_call(
        functools.partial(solve_kernel, prow=len(tops)),
        out_shape=(jax.ShapeDtypeStruct((rows, cols), f32), jax.ShapeDtypeStruct((rows, lead), f32)),
        in_specs=[SMEM] + [any_space] * (5 + len(tops)),
        out_specs=(VMEM, VMEM),
        scratch_shapes=[pltpu.VMEM((K, K), bf16)] * 2 + [pltpu.VMEM((K, BLK), f32), pltpu.VMEM(pieces.shape, f32)]
        + [pltpu.VMEM((len(tops),) + tops[0].shape, f32), pltpu.VMEM(schur.shape, f32)]
        + [pltpu.VMEM((rows, K), bf16)] * 2 + [pltpu.VMEM((K, cols), bf16)] * 2 + [pltpu.SemaphoreType.DMA((len(tops) + 5,))],
        compiler_params=pltpu.CompilerParams(vmem_limit_bytes=58 * MIB),
        cost_estimate=pl.CostEstimate(flops=12 * 10**9, bytes_accessed=24 * MIB, transcendentals=0),
    )(place, high, low, inverses, pieces, schur, *tops)


def gather_factors(mine, prow_count, pcol_count, prow_id):
    own = mine.shape[0]
    half = own // 2

    def swap(axis, count, turn, value, chosen=lambda n: True):
        return lax.ppermute(value, axis, [(n, n ^ turn) for n in range(count) if chosen(n)])

    def close(n):
        return abs(n - (n ^ 3)) == 1

    span = pcol_count // 2
    level_of = {j: bin(j).count("1") for j in range(1, span)}
    levels = max(level_of.values(), default=0)
    order = [0] + list(range(1, prow_count, 2)) + list(range(2, prow_count, 2))
    items = {0: mine}
    held = {turn: {} for turn in order}
    split_turn = 3 if prow_count == 4 else None
    if split_turn:
        middle = swap("prow", prow_count, split_turn, mine, close)
    parts = []

    def spread(turn, j):
        low, high = j & -j, 1 << (j.bit_length() - 1)
        if low == high:
            return [swap("pcol", pcol_count, 2 * j, held[turn][0])]
        return [swap("pcol", pcol_count, 2 * high, held[turn][j ^ high][:half]), swap("pcol", pcol_count, 2 * low, held[turn][j ^ low][half:])]

    def take(turn, which):
        whole = jnp.concatenate([held[turn][j] for j in which]) if len(which) > 1 else held[turn][which[0]]
        parts.append((turn, which, whole, swap("pcol", pcol_count, 1, whole)))

    for phase in range(len(order) + levels - 1):
        moved = {}
        if phase < len(order):
            turn = order[phase]
            held[turn][0] = items[turn]
            if turn % 2 == 1 and turn > 1:
                moved["z", turn - 1] = [swap("prow", prow_count, 1, items[turn])]
        for level in range(1, levels + 1):
            if 0 <= phase - level + 1 < len(order):
                turn = order[phase - level + 1]
                for j in range(1, span):
                    if level_of[j] == level:
                        moved[turn, j] = spread(turn, j)
        if phase + 1 < len(order):
            turn = order[phase + 1]
            if turn % 2 == 1:
                if turn == split_turn:
                    moved["z", turn] = [swap("prow", prow_count, turn, mine, lambda n: not close(n))]
                else:
                    moved["z", turn] = [swap("prow", prow_count, turn, mine)]
            elif turn in items:
                moved["z", turn] = [items[turn]]
        if phase == 0 and split_turn:
            moved["middle", split_turn] = [middle]
        mine, *results = lax.optimization_barrier([mine] + [value for values in moved.values() for value in values])
        results = iter(results)
        for (turn, j), values in moved.items():
            arrived = [next(results) for _ in values]
            if turn == "middle":
                middle = arrived[0]
            elif turn == "z" and j == split_turn:
                items[j] = jnp.where(close(prow_id), middle, arrived[0])
            elif turn == "z":
                items[j] = arrived[0]
            else:
                held[turn][j] = arrived[0] if len(arrived) == 1 else jnp.concatenate(arrived)
        if 0 <= phase - levels + 1 < len(order) - 1:
            take(order[phase - levels + 1], list(held[order[phase - levels + 1]]))
        if phase == len(order) + levels - 3:
            early = [j for j in held[order[-1]] if j == 0 or level_of[j] < levels]
            if len(early) == span or levels < 2:
                early = []
            else:
                take(order[-1], early)
    take(order[-1], [j for j in range(span) if j not in early])
    near = [whole for _, _, whole, _ in parts]
    far = [swapped for _, _, _, swapped in parts]
    places = [(turn, 2 * j) for turn, which, _, _ in parts for j in which]
    return near + far, places + [(turn, col + 1) for turn, col in places]


def places_of(placement, order, prow_id, pcol_id, pcol_count):
    total = placement.shape[0]
    own = total // len(order)
    unit_of = [0] * len(order)
    for unit, (row_turn, col_turn) in enumerate(order):
        unit_of[row_turn * pcol_count + col_turn] = unit
    holder = jnp.arange(len(order))
    turn = ((holder // pcol_count) ^ prow_id) * pcol_count + ((holder % pcol_count) ^ pcol_id)
    units = jnp.sum(jnp.where(turn[:, None] == jnp.arange(len(order))[None, :], jnp.array(unit_of)[None, :], 0), axis=1)
    place = (units[:, None] * own + jnp.arange(own)[None, :]).reshape(1, total)
    blocks = total // NB
    in_block = jnp.arange(blocks)[:, None] == placement[None, :] // NB
    digits = jnp.concatenate([jnp.where(in_block, place // NB, 0), jnp.where(in_block, place % NB, 0)]).astype(jnp.bfloat16)
    at_row = (jnp.arange(NB)[:, None] == placement[None, :] % NB).astype(jnp.bfloat16)
    found = dot_bf16(digits, at_row, NT).astype(jnp.int32)
    return found[:blocks] * NB + found[blocks:]


def per_device(factors, x_factor, zinv_factor, placement):
    prow_count = lax.axis_size("prow")
    pcol_count = lax.axis_size("pcol")
    total_rows = placement.shape[0]
    local_rows = total_rows // prow_count
    local_cols = total_rows // pcol_count
    prow_id = lax.axis_index("prow")
    pcol_id = lax.axis_index("pcol")
    _, own, width = factors.shape
    count = prow_count * pcol_count
    lanes = BLK
    mine = factors.transpose(1, 0, 2).reshape(own, RANK * width // lanes, lanes)
    sources, order = gather_factors(mine, prow_count, pcol_count, prow_id)
    found = places_of(placement, order, prow_id, pcol_id, pcol_count)
    by_row = lax.dynamic_index_in_dim(found.reshape(local_rows // NB, prow_count, NB), prow_id, 1, keepdims=False)
    by_col = lax.dynamic_index_in_dim(found.reshape(local_cols // NB, pcol_count, NB), pcol_id, 1, keepdims=False)
    lead_rows, lead_cols = K // prow_count, K // pcol_count
    places = jnp.concatenate([found[:K // NB], by_row[lead_rows // NB:], by_col[lead_cols // NB:]])
    places = jnp.pad(places, ((0, -places.shape[0] % (256 // NB)), (0, 0))).reshape(-1)
    place = jnp.stack([prow_id, pcol_id]).astype(jnp.int32)
    lead_x, lead_z, schur_local, front, top = assemble(
        place, places.astype(jnp.int32), sources, x_factor, zinv_factor, local_rows, local_cols, lead_rows, lead_cols)
    pieces = lax.all_gather(front, "pcol", axis=0, tiled=False)
    tops = [top] + [lax.ppermute(top, "prow", [(n, n ^ turn) for n in range(prow_count)]) for turn in range(1, prow_count)]
    high, low, inverses = factor(lead_x, lead_z)
    return solve(place, high, low, inverses, pieces, schur_local, tops)


def solution(mesh):
    in_specs = (P(None, ("prow", "pcol"), None), P(), P(), P())
    out_specs = (P("prow", "pcol"), P("prow", "pcol"))
    return jax.shard_map(
        per_device, mesh=mesh, in_specs=in_specs, out_specs=out_specs, check_vma=False
    )
```

```python
import functools

import jax
import jax.numpy as jnp
from jax import lax
from jax.experimental import pallas as pl
from jax.experimental.pallas import tpu as pltpu
from jax.sharding import PartitionSpec as P

RANK = 4
NB = 64
K = 1024
SUB = 8
BLK = 128
MIB = 2**20

rank_signs = (1.0, 1.0, -1.0, -1.0)
NT = ((1,), (1,))
NN = ((1,), (0,))
VMEM = pl.BlockSpec(memory_space=pltpu.VMEM)
SMEM = pl.BlockSpec(memory_space=pltpu.SMEM)


def split(x):
    hi = x.astype(jnp.bfloat16)
    lo = (x - hi.astype(jnp.float32)).astype(jnp.bfloat16)
    return hi, lo


def dot_bf16(a, b, dims):
    return lax.dot_general(a, b, (dims, ((), ())), preferred_element_type=jnp.float32)


def dot3(a, b, dims):
    return dot_bf16(a[0], b[0], dims) + (dot_bf16(a[0], b[1], dims) + dot_bf16(a[1], b[0], dims))


def assemble_kernel(place_ref, slots_ref, x_ref, z_ref, *refs, sources, lead_tiles, pick_tiles, col_tiles, rows, prow, pcol):
    source_refs, refs = refs[:sources], refs[sources:]
    lead_x_ref, lead_z_ref, schur_ref, front_ref, top_ref, every_ref, picked_ref, yx_ref, yz_ref, sem_ref = refs
    step = pl.program_id(0)
    tile, parts, lanes = picked_ref.shape
    width = x_ref.shape[0]
    per_rank = width // lanes

    @pl.when(step == 0)
    def _():
        copies, first = [], 0
        for n, ref in enumerate(source_refs):
            copies.append(pltpu.make_async_copy(ref, every_ref.at[pl.ds(first, ref.shape[0])], sem_ref.at[n]))
            first += ref.shape[0]
        for copy in copies:
            copy.start()
        for copy in copies:
            copy.wait()

    @pl.when(step < pick_tiles)
    def _():
        def pick(group, carry):
            for k in range(16):
                i = group * 16 + k
                picked_ref[i] = every_ref[slots_ref[step * tile + i]]
            return carry
        lax.fori_loop(0, tile // 16, pick, 0)
        by_part = jnp.swapaxes(picked_ref[...], 0, 1)
        mine = jnp.concatenate([
            jnp.concatenate([by_part[r * per_rank + k] for k in range(per_rank)], axis=1) for r in range(RANK)], axis=0)
        images_x = dot_bf16(mine, x_ref[...], NN).astype(jnp.bfloat16).reshape(RANK, tile, width)
        images_z = dot_bf16(mine, z_ref[...], NN).astype(jnp.bfloat16).reshape(RANK, tile, width)

        def keep(block, s):
            at = pl.ds(pl.multiple_of(block * NB, NB), NB)
            yx_ref[:, at, :] = images_x[:, s * NB:(s + 1) * NB, :]
            yz_ref[:, at, :] = images_z[:, s * NB:(s + 1) * NB, :]

        @pl.when(step < lead_tiles)
        def _():
            lead_x_ref[...], lead_z_ref[...] = images_x, images_z
            for s in range(tile // NB):
                block = step * (tile // NB) + s

                @pl.when(block % prow == place_ref[0])
                def _():
                    keep(block // prow, s)

                @pl.when(block % pcol == place_ref[1])
                def _():
                    keep(rows // NB + block // pcol, s)

        @pl.when(step >= lead_tiles)
        def _():
            lead = K // NB
            row_rest, col_rest = rows // NB - lead // prow, (yx_ref.shape[1] - rows) // NB - lead // pcol
            for s in range(tile // NB):
                block = (step - lead_tiles) * (tile // NB) + s

                @pl.when(block < row_rest + col_rest)
                def _():
                    keep(jnp.where(block < row_rest, lead // prow + block, rows // NB + lead // pcol + block - row_rest), s)

    @pl.when(step >= pick_tiles)
    def _():
        high, wide = schur_ref.shape
        i, j = (step - pick_tiles) // col_tiles, (step - pick_tiles) % col_tiles
        left = pl.ds(pl.multiple_of(i * high, high), high)
        right = pl.ds(pl.multiple_of(rows + j * wide, wide), wide)
        schur_ref[...] = gram_tile(yx_ref, yz_ref, left, right)

        @pl.when(j == 0)
        def _():
            front_ref[...] = schur_ref[:, :front_ref.shape[1]]

        @pl.when(i == 0)
        def _():
            top_ref[...] = schur_ref[:top_ref.shape[0], :]


def gram_tile(yx_ref, yz_ref, left, right):
    left_x, left_z = yx_ref[:, left, :], yz_ref[:, left, :]
    _, high, width = left_x.shape
    left_x, left_z = left_x.reshape(RANK * high, width), left_z.reshape(RANK * high, width)
    total = None
    for q in range(RANK):
        gx = dot_bf16(left_x, yx_ref[q, right, :], NT)
        gz = dot_bf16(left_z, yz_ref[q, right, :], NT)
        for r in range(RANK):
            term = gx[r * high:(r + 1) * high] * gz[r * high:(r + 1) * high]
            total = signed(total, term, q, r)
    return total


def signed(total, term, q, r):
    if total is None:
        return term
    return total + term if rank_signs[q] * rank_signs[r] > 0 else total - term


def assemble(place, slots, sources, x_factor, z_factor, rows, cols, lead_rows, lead_cols):
    _, parts, lanes = sources[0].shape
    slots_held = sum(source.shape[0] for source in sources)
    width = x_factor.shape[0]
    tile = 256
    high, wide = min(512, rows), min(256, cols)
    lead_tiles, pick_tiles = K // tile, slots.shape[0] // tile
    row_tiles, col_tiles = rows // high, cols // wide
    whole = pl.BlockSpec((width, width), lambda s: (0, 0), pipeline_mode=pl.Buffered(1))
    lead = pl.BlockSpec((RANK, tile, width), lambda s: (0, jnp.minimum(s, lead_tiles - 1), 0))
    after = lambda s: jnp.maximum(s - pick_tiles, 0)
    bf16 = jnp.bfloat16
    any_space = pl.BlockSpec(memory_space=pl.ANY)
    body = functools.partial(assemble_kernel, sources=len(sources), lead_tiles=lead_tiles, pick_tiles=pick_tiles, col_tiles=col_tiles, rows=rows, prow=K // lead_rows, pcol=K // lead_cols)
    return pl.pallas_call(
        body,
        grid=(pick_tiles + row_tiles * col_tiles,),
        out_shape=(jax.ShapeDtypeStruct((RANK, K, width), bf16),) * 2 + (
            jax.ShapeDtypeStruct((rows, cols), jnp.float32),
            jax.ShapeDtypeStruct((rows, lead_cols), jnp.float32),
            jax.ShapeDtypeStruct((lead_rows, cols), jnp.float32)),
        in_specs=[SMEM, SMEM, whole, whole] + [any_space] * len(sources),
        out_specs=(lead, lead,
                   pl.BlockSpec((high, wide), lambda s: (after(s) // col_tiles, after(s) % col_tiles)),
                   pl.BlockSpec((high, lead_cols), lambda s: (after(s) // col_tiles, 0)),
                   pl.BlockSpec((lead_rows, wide), lambda s: (0, jnp.minimum(after(s), col_tiles - 1)))),
        scratch_shapes=[pltpu.VMEM((slots_held, parts, lanes), bf16), pltpu.VMEM((tile, parts, lanes), bf16)]
        + [pltpu.VMEM((RANK, rows + cols, width), bf16)] * 2 + [pltpu.SemaphoreType.DMA((len(sources),))],
        compiler_params=pltpu.CompilerParams(vmem_limit_bytes=58 * MIB),
        cost_estimate=pl.CostEstimate(flops=28 * 10**9, bytes_accessed=30 * MIB, transcendentals=0),
    )(place, slots, x_factor, z_factor, *sources)


def factor_block(block, u_ref, v_ref, beside):
    count = BLK // SUB
    sub_iota = lax.broadcasted_iota(jnp.int32, (SUB, BLK), 0)
    lane_iota = lax.broadcasted_iota(jnp.int32, (SUB, BLK), 1)
    rows_a = [block[SUB * i:SUB * (i + 1), :] for i in range(count)]
    rows_v = [(lane_iota == sub_iota + SUB * i).astype(jnp.float32) for i in range(count)]

    def spread_lane(x, lane):
        return jnp.broadcast_to(x[:, lane:lane + 1], (SUB, BLK))

    def spread_row(x, row):
        return jnp.broadcast_to(x[row:row + 1, :], (SUB, BLK))

    for m in range(count):
        beside(m)
        head_a, head_v = rows_a[m], rows_v[m]
        cols = [spread_lane(head_a, SUB * m + k) for k in range(SUB)]
        below = [[spread_lane(rows_a[i], SUB * m + k) for k in range(SUB if i == m + 1 else SUB // 2)] + [None] * (0 if i == m + 1 else SUB // 2)
                 for i in range(m + 1, count)]
        scale = jnp.zeros((SUB, BLK), jnp.float32)
        for j in range(SUB):
            pivot = spread_row(cols[j], j)
            root = lax.rsqrt(pivot)
            scale = jnp.where(sub_iota == j, root, scale)
            mult = jnp.where(sub_iota > j, cols[j], 0.0) * root
            row_a = spread_row(head_a, j) * root
            row_v = spread_row(head_v, j) * root
            lead = [spread_row(cols[k], j) * root if k > j else None for k in range(SUB)]
            if j + 1 < SUB:
                head_a = head_a - mult * row_a
                head_v = head_v - mult * row_v
                for k in range(j + 1, SUB):
                    cols[k] = cols[k] - mult * lead[k]
            for n, i in enumerate(range(m + 1, count)):
                mult_i = below[n][j] * root
                rows_a[i] = rows_a[i] - mult_i * row_a
                rows_v[i] = rows_v[i] - mult_i * row_v
                if n > 0 and j + 1 == SUB // 2:
                    below[n][j + 1:] = [spread_lane(rows_a[i], SUB * m + k) for k in range(j + 1, SUB)]
                for k in range(j + 1, SUB if n == 0 else max(SUB // 2, j // (SUB // 2) * SUB)):
                    below[n][k] = below[n][k] - mult_i * lead[k]
        u = jnp.where(lane_iota >= sub_iota + SUB * m, head_a * scale, 0.0)
        v = jnp.where(lane_iota <= sub_iota + SUB * m, head_v * scale, 0.0)
        u_ref[SUB * m:SUB * (m + 1), :] = u
        v_ref[SUB * m:SUB * (m + 1), :] = v


def factor_kernel(yx_ref, yz_ref, lh_ref, ll_ref, d_ref, w_ref, g_ref, u_ref, v_ref):
    order = lh_ref.shape[0]
    steps = order // BLK
    tile = 2 * BLK
    window = 3 * BLK
    lh_ref[...] = jnp.zeros_like(lh_ref)
    ll_ref[...] = jnp.zeros_like(ll_ref)
    w_ref[:, tile:] = jnp.zeros((order, order - tile), jnp.float32)

    def rows_of(i, carry):
        left = pl.ds(pl.multiple_of(i * tile, tile), tile)
        w_ref[left, :tile] = gram_tile(yx_ref, yz_ref, left, pl.ds(0, tile))
        return carry
    lax.fori_loop(0, order // tile, rows_of, 0)

    def step(b, carry):
        at = pl.ds(pl.multiple_of(b * BLK, BLK), BLK)
        after = jnp.minimum(b // 2 + 1, order // tile - 1)
        top = pl.multiple_of(jnp.minimum(after * tile + (b % 2) * window, order - window), BLK)
        left = pl.ds(top, window)
        right = pl.ds(pl.multiple_of(after * tile, tile), tile)

        def beside(m):
            q, r = m // RANK, m % RANK
            term = dot_bf16(yx_ref[r, left, :], yx_ref[q, right, :], NT) * dot_bf16(yz_ref[r, left, :], yz_ref[q, right, :], NT)
            g_ref[left, :] = signed(g_ref[left, :] if m > 0 else None, term, q, r)

        factor_block(w_ref[at, at], u_ref, v_ref, beside)
        lh_ref[at, at], ll_ref[at, at] = split(u_ref[...].T)
        d_ref[at, :] = v_ref[...]
        for k in range(steps - 1):
            @pl.when(b == k)
            def _():
                first = (k + 1) * BLK
                column = slice(k * BLK, first)
                lh_ref[first:, column], ll_ref[first:, column] = split(dot3(split(w_ref[first:, column]), split(v_ref[...]), NT))
                for top in range(first, order, tile):
                    bottom = min(top + tile, order)
                    left = (lh_ref[top:bottom, column], ll_ref[top:bottom, column])
                    right = (lh_ref[first:bottom, column], ll_ref[first:bottom, column])
                    w_ref[top:bottom, first:bottom] = w_ref[top:bottom, first:bottom] - dot3(left, right, NT)
                if k % 2 == 1:
                    w_ref[first:, first:first + tile] = w_ref[first:, first:first + tile] + g_ref[first:, :]
        return carry
    lax.fori_loop(0, steps, step, 0)


def factor(yx, yz):
    tile = 2 * BLK
    f32 = jnp.float32
    return pl.pallas_call(
        factor_kernel,
        out_shape=(jax.ShapeDtypeStruct((K, K), jnp.bfloat16),) * 2 + (jax.ShapeDtypeStruct((K, BLK), f32),),
        in_specs=[VMEM] * 2,
        out_specs=(VMEM,) * 3,
        scratch_shapes=[pltpu.VMEM((K, K), f32), pltpu.VMEM((K, tile), f32), pltpu.VMEM((BLK, BLK), f32), pltpu.VMEM((BLK, BLK), f32)],
        compiler_params=pltpu.CompilerParams(vmem_limit_bytes=58 * MIB),
        cost_estimate=pl.CostEstimate(flops=40 * 10**9, bytes_accessed=12 * MIB, transcendentals=0),
    )(yx, yz)


def solve_kernel(place_ref, lh_any, ll_any, d_any, pieces_any, schur_any, *refs, prow):
    top_refs, refs = refs[:prow], refs[prow:]
    rest_ref, panel_ref, lh, ll, d_ref, pieces_ref, tops_ref, schur_ref, xh, xl, zh, zl, sem_ref = refs
    pcol = pieces_ref.shape[0]
    row, column = place_ref[0], place_ref[1]
    pairs = [(d_any, d_ref), (lh_any, lh), (ll_any, ll)]
    pairs += [(ref, tops_ref.at[turn ^ row]) for turn, ref in enumerate(top_refs)]
    pairs += [(pieces_any, pieces_ref), (schur_any, schur_ref)]
    copies = [pltpu.make_async_copy(here, there, sem_ref.at[n]) for n, (here, there) in enumerate(pairs)]
    for copy in copies:
        copy.start()
    for copy in copies[:3]:
        copy.wait()
    wide = 2 * BLK
    inverses = []
    for b in range(K // wide):
        upper, lower = slice(b * wide, b * wide + BLK), slice(b * wide + BLK, (b + 1) * wide)
        first, second = split(d_ref[upper, :]), split(d_ref[lower, :])
        between = dot3((lh[lower, upper], ll[lower, upper]), first, NN)
        corner = -dot3(second, split(between), NN)
        inverses.append(split(jnp.concatenate([
            jnp.concatenate([d_ref[upper, :], jnp.zeros((BLK, BLK), jnp.float32)], axis=1),
            jnp.concatenate([corner, d_ref[lower, :]], axis=1)], axis=0)))
    for copy in copies[3:-1]:
        copy.wait()
    for b in range(K // wide):
        at, done = slice(b * wide, (b + 1) * wide), slice(0, b * wide)
        blocks = range(wide // NB * b, wide // NB * (b + 1))
        value = jnp.concatenate([pieces_ref[n % pcol, :, n // pcol * NB:(n // pcol + 1) * NB] for n in blocks], axis=1)
        top = jnp.concatenate([tops_ref[n % prow, n // prow * NB:(n // prow + 1) * NB, :] for n in blocks], axis=0)
        if b > 0:
            left = (lh[at, done], ll[at, done])
            value = value - dot3((xh[:, done], xl[:, done]), left, NT)
            top = top - dot3(left, (zh[done, :], zl[done, :]), NN)
        value = dot3(split(value), inverses[b], NT)
        top = dot3(inverses[b], split(top), NN)
        xh[:, at], xl[:, at] = split(value)
        zh[at, :], zl[at, :] = split(top)
        for place, block in enumerate(blocks):
            @pl.when(column == block % pcol)
            def _():
                panel_ref[:, block // pcol * NB:(block // pcol + 1) * NB] = value[:, place * NB:(place + 1) * NB]
    copies[-1].wait()
    rest_ref[...] = schur_ref[...] - dot3((xh[...], xl[...]), (zh[...], zl[...]), NN)


def solve(place, high, low, inverses, pieces, schur, tops):
    rows, cols = schur.shape
    lead = K // pieces.shape[0]
    bf16, f32 = jnp.bfloat16, jnp.float32
    any_space = pl.BlockSpec(memory_space=pl.ANY)
    return pl.pallas_call(
        functools.partial(solve_kernel, prow=len(tops)),
        out_shape=(jax.ShapeDtypeStruct((rows, cols), f32), jax.ShapeDtypeStruct((rows, lead), f32)),
        in_specs=[SMEM] + [any_space] * (5 + len(tops)),
        out_specs=(VMEM, VMEM),
        scratch_shapes=[pltpu.VMEM((K, K), bf16)] * 2 + [pltpu.VMEM((K, BLK), f32), pltpu.VMEM(pieces.shape, f32)]
        + [pltpu.VMEM((len(tops),) + tops[0].shape, f32), pltpu.VMEM(schur.shape, f32)]
        + [pltpu.VMEM((rows, K), bf16)] * 2 + [pltpu.VMEM((K, cols), bf16)] * 2 + [pltpu.SemaphoreType.DMA((len(tops) + 5,))],
        compiler_params=pltpu.CompilerParams(vmem_limit_bytes=58 * MIB),
        cost_estimate=pl.CostEstimate(flops=12 * 10**9, bytes_accessed=24 * MIB, transcendentals=0),
    )(place, high, low, inverses, pieces, schur, *tops)


def gather_factors(mine, prow_count, pcol_count, prow_id):
    own = mine.shape[0]
    half = own // 2

    def swap(axis, count, turn, value, chosen=lambda n: True):
        return lax.ppermute(value, axis, [(n, n ^ turn) for n in range(count) if chosen(n)])

    def close(n):
        return abs(n - (n ^ 3)) == 1

    span = pcol_count // 2
    level_of = {j: bin(j).count("1") for j in range(1, span)}
    levels = max(level_of.values(), default=0)
    order = [0] + list(range(1, prow_count, 2)) + list(range(2, prow_count, 2))
    items = {0: mine}
    held = {turn: {} for turn in order}
    split_turn = 3 if prow_count == 4 else None
    if split_turn:
        middle = swap("prow", prow_count, split_turn, mine, close)
    parts = []

    def spread(turn, j):
        low, high = j & -j, 1 << (j.bit_length() - 1)
        if low == high:
            return [swap("pcol", pcol_count, 2 * j, held[turn][0])]
        return [swap("pcol", pcol_count, 2 * high, held[turn][j ^ high][:half]), swap("pcol", pcol_count, 2 * low, held[turn][j ^ low][half:])]

    def take(turn, which):
        whole = jnp.concatenate([held[turn][j] for j in which]) if len(which) > 1 else held[turn][which[0]]
        parts.append((turn, which, whole, swap("pcol", pcol_count, 1, whole)))

    for phase in range(len(order) + levels - 1):
        moved = {}
        if phase < len(order):
            turn = order[phase]
            held[turn][0] = items[turn]
            if turn % 2 == 1 and turn > 1:
                moved["z", turn - 1] = [swap("prow", prow_count, 1, items[turn])]
        for level in range(1, levels + 1):
            if 0 <= phase - level + 1 < len(order):
                turn = order[phase - level + 1]
                for j in range(1, span):
                    if level_of[j] == level:
                        moved[turn, j] = spread(turn, j)
        if phase + 1 < len(order):
            turn = order[phase + 1]
            if turn % 2 == 1:
                if turn == split_turn:
                    moved["z", turn] = [swap("prow", prow_count, turn, mine, lambda n: not close(n))]
                else:
                    moved["z", turn] = [swap("prow", prow_count, turn, mine)]
            elif turn in items:
                moved["z", turn] = [items[turn]]
        if phase == 0 and split_turn:
            moved["middle", split_turn] = [middle]
        mine, *results = lax.optimization_barrier([mine] + [value for values in moved.values() for value in values])
        results = iter(results)
        for (turn, j), values in moved.items():
            arrived = [next(results) for _ in values]
            if turn == "middle":
                middle = arrived[0]
            elif turn == "z" and j == split_turn:
                items[j] = jnp.where(close(prow_id), middle, arrived[0])
            elif turn == "z":
                items[j] = arrived[0]
            else:
                held[turn][j] = arrived[0] if len(arrived) == 1 else jnp.concatenate(arrived)
        if 0 <= phase - levels + 1 < len(order) - 1:
            take(order[phase - levels + 1], list(held[order[phase - levels + 1]]))
        if phase == len(order) + levels - 3:
            early = [j for j in held[order[-1]] if j == 0 or level_of[j] < levels]
            if len(early) == span or levels < 2:
                early = []
            else:
                take(order[-1], early)
    take(order[-1], [j for j in range(span) if j not in early])
    near = [whole for _, _, whole, _ in parts]
    far = [swapped for _, _, _, swapped in parts]
    places = [(turn, 2 * j) for turn, which, _, _ in parts for j in which]
    return near + far, places + [(turn, col + 1) for turn, col in places]


def places_of(placement, order, prow_id, pcol_id, pcol_count):
    total = placement.shape[0]
    own = total // len(order)
    unit_of = [0] * len(order)
    for unit, (row_turn, col_turn) in enumerate(order):
        unit_of[row_turn * pcol_count + col_turn] = unit
    holder = jnp.arange(len(order))
    turn = ((holder // pcol_count) ^ prow_id) * pcol_count + ((holder % pcol_count) ^ pcol_id)
    units = jnp.sum(jnp.where(turn[:, None] == jnp.arange(len(order))[None, :], jnp.array(unit_of)[None, :], 0), axis=1)
    place = (units[:, None] * own + jnp.arange(own)[None, :]).reshape(1, total)
    blocks = total // NB
    in_block = jnp.arange(blocks)[:, None] == placement[None, :] // NB
    digits = jnp.concatenate([jnp.where(in_block, place // NB, 0), jnp.where(in_block, place % NB, 0)]).astype(jnp.bfloat16)
    at_row = (jnp.arange(NB)[:, None] == placement[None, :] % NB).astype(jnp.bfloat16)
    found = dot_bf16(digits, at_row, NT).astype(jnp.int32)
    return found[:blocks] * NB + found[blocks:]


def per_device(factors, x_factor, zinv_factor, placement):
    prow_count = lax.axis_size("prow")
    pcol_count = lax.axis_size("pcol")
    total_rows = placement.shape[0]
    local_rows = total_rows // prow_count
    local_cols = total_rows // pcol_count
    prow_id = lax.axis_index("prow")
    pcol_id = lax.axis_index("pcol")
    _, own, width = factors.shape
    count = prow_count * pcol_count
    lanes = BLK
    mine = factors.transpose(1, 0, 2).reshape(own, RANK * width // lanes, lanes)
    sources, order = gather_factors(mine, prow_count, pcol_count, prow_id)
    found = places_of(placement, order, prow_id, pcol_id, pcol_count)
    by_row = lax.dynamic_index_in_dim(found.reshape(local_rows // NB, prow_count, NB), prow_id, 1, keepdims=False)
    by_col = lax.dynamic_index_in_dim(found.reshape(local_cols // NB, pcol_count, NB), pcol_id, 1, keepdims=False)
    lead_rows, lead_cols = K // prow_count, K // pcol_count
    places = jnp.concatenate([found[:K // NB], by_row[lead_rows // NB:], by_col[lead_cols // NB:]])
    places = jnp.pad(places, ((0, -places.shape[0] % (256 // NB)), (0, 0))).reshape(-1)
    place = jnp.stack([prow_id, pcol_id]).astype(jnp.int32)
    lead_x, lead_z, schur_local, front, top = assemble(
        place, places.astype(jnp.int32), sources, x_factor, zinv_factor, local_rows, local_cols, lead_rows, lead_cols)
    pieces = lax.all_gather(front, "pcol", axis=0, tiled=False)
    tops = [top] + [lax.ppermute(top, "prow", [(n, n ^ turn) for n in range(prow_count)]) for turn in range(1, prow_count)]
    high, low, inverses = factor(lead_x, lead_z)
    return solve(place, high, low, inverses, pieces, schur_local, tops)


def solution(mesh):
    in_specs = (P(None, ("prow", "pcol"), None), P(), P(), P())
    out_specs = (P("prow", "pcol"), P("prow", "pcol"))
    return jax.shard_map(
        per_device, mesh=mesh, in_specs=in_specs, out_specs=out_specs, check_vma=False
    )
```
